32 devices in a mesh: blk: 4 (over y, x), box: 8 (over z, core).
Axes of the slice: x: 2, y: 2, z: 4, core: 2. Of those that a mesh axis runs over, the one named last changes fastest.
Arguments:
- excitation: bfloat16 [4, 16, 1024, 512], P('blk', 'box'), may hold values from -6 to 6
- leaf_basis: bfloat16 [4, 16, 384, 1024], P('blk', 'box'), may hold values from -0.1875 to 0.1875
- transfer: bfloat16 [4, 5, 16, 384, 768], P('blk', None, 'box'), may hold values from -0.21875 to 0.21875
- transfer_index: int32 [4, 5, 16], P('blk', None, 'box'), may hold values from 0 to 1
- out_basis: bfloat16 [4, 16, 1024, 384], P('blk', 'box'), may hold values from -0.21875 to 0.21875
Outputs:
- field: bfloat16 [16, 1024, 512], P('box', 'blk')
The draws below stay inside these ranges and needn't reach their ends.
All inputs are finite; a program needn't handle non-finite values.
Results may differ from the reference program's by a relative error of at most 0.018.
Values may be sent and summed in bfloat16 or wider, within the bound.
No kernel may reach another device: no remote copies, remote signals or barrier semaphores. Data moves between devices by JAX's collectives and lax.ppermute only.
A program may use at most 64 MiB of HBM per device.

```python
import jax
import jax.numpy as jnp
from jax import lax

RANK = 384
COLS = 512
LEAF = 1024
OUTROWS = 1024
BOX_DEV = 2
SLOT_DEV = 2
LEVELS = 5
BLOCKS = 4
BOXES = 16
SLOTS = 16
N_BOX = 8


def touch_ends(array, own_key, least, top_value):
    longest = array.shape.index(max(array.shape))
    spots = []
    for shift in (0, 1):
        where = [jax.random.randint(jax.random.fold_in(own_key, axis), (), 0, length) for axis, length in enumerate(array.shape)]
        where[longest] = (where[longest] + shift) % array.shape[longest]
        spots.append(tuple(where))
    return array.at[spots[0]].set(least).at[spots[1]].set(top_value)


def with_spikes(values, rng, source, target, shards_of, factor):
    owner, partner = [(jnp.arange(values.shape[axis_at]) // (values.shape[axis_at] // shards_of)).reshape([-1 if axis == axis_at else 1 for axis in range(values.ndim)]) for axis_at in (source, target)]
    chosen = jax.random.permutation(rng, shards_of)[partner]
    strong = (owner == chosen) | (owner == (partner + shards_of // 2) % shards_of)
    return jnp.where(strong, factor * values, values)


def steps_of(key, shape, shards, least, largest):
    level = 1.0
    for axis_at, blocks in shards:
        draws = jax.random.uniform(jax.random.fold_in(jax.random.fold_in(key, 6), axis_at), (blocks,), jnp.float32, least / len(shards), largest / len(shards))
        level = level * jnp.repeat(jnp.exp(draws), shape[axis_at] // blocks).reshape((-1,) + (1,) * (len(shape) - 1 - axis_at))
    return level


def centred(own_key, extent, scale, reach, cuts=(), kind=jnp.bfloat16):
    array = scale * jax.random.normal(own_key, extent, jnp.float32)
    if cuts:
        array = array * steps_of(own_key, extent, cuts, -0.22, 0.18)
    return jnp.clip(array, -reach, reach).astype(kind)


def noise_with(rng, extent, width, most, cuts, heavy, kind=jnp.bfloat16):
    entries = width * jax.random.normal(rng, extent, jnp.float32)
    if cuts:
        entries = entries * steps_of(rng, extent, cuts, -0.22, 0.18)
    return jnp.clip(with_spikes(entries, jax.random.fold_in(rng, 3), *heavy), -most, most).astype(kind)


def setup_inputs(seed: int = 0) -> dict:
    keys = jax.random.split(jax.random.key(seed), 6)
    excitation = centred(keys[0], (BLOCKS, BOXES, LEAF, COLS), 1.0, 6.0, ((0, 4), (1, 8)))
    leaf_basis = centred(keys[1], (BLOCKS, BOXES, RANK, LEAF), LEAF ** -0.5, 0.1875, ((0, 4), (1, 8)))
    transfer = centred(keys[2], (BLOCKS, LEVELS, SLOTS, RANK, 2 * RANK), (2 * RANK) ** -0.5, 0.21875, ((0, 4), (2, 8)))
    transfer_index = touch_ends(jax.random.randint(keys[3], (BLOCKS, LEVELS, BOXES), 0, SLOT_DEV), jax.random.fold_in(keys[3], 1), 0, SLOT_DEV - 1).astype(jnp.int32)
    out_basis = noise_with(keys[4], (BLOCKS, BOXES, OUTROWS, RANK), (RANK * BLOCKS) ** -0.5, 0.21875, ((0, 4), (1, 8)), (0, 2, 4, 2.0))
    return {"excitation": excitation, "leaf_basis": leaf_basis, "transfer": transfer, "transfer_index": transfer_index, "out_basis": out_basis}


def one_block(total, pieces):
    excite, leaves, blocks, index, basis = pieces
    coeff = jnp.einsum('brp,bpc->brc', leaves.astype(jnp.float32), excite.astype(jnp.float32)).astype(jnp.bfloat16)
    boxes = jnp.arange(BOXES, dtype=jnp.int32)
    nbits = N_BOX.bit_length() - 1
    for level in range(LEVELS):
        if level == 0:
            mask = 1
        else:
            mask = BOX_DEV * 2 ** ((level - 1) % nbits)
        partner = jnp.bitwise_xor(boxes, mask)
        lower = (jnp.bitwise_and(boxes, mask) == 0)[:, None, None]
        other = coeff[partner]
        first = jnp.where(lower, coeff, other)
        second = jnp.where(lower, other, coeff)
        slot = (boxes // BOX_DEV) * SLOT_DEV + index[level]
        chosen = blocks[level][slot].astype(jnp.float32)
        mixed = jnp.einsum('brs,bsc->brc', chosen[:, :, :RANK], first.astype(jnp.float32))
        mixed = mixed + jnp.einsum('brs,bsc->brc', chosen[:, :, RANK:], second.astype(jnp.float32))
        coeff = mixed.astype(jnp.bfloat16)
    term = jnp.einsum('bqr,brc->bqc', basis.astype(jnp.float32), coeff.astype(jnp.float32))
    return total + term, None


def reference(excitation, leaf_basis, transfer, transfer_index, out_basis):
    start = jnp.zeros((BOXES, OUTROWS, COLS), jnp.float32)
    total, unused = lax.scan(one_block, start, (excitation, leaf_basis, transfer, transfer_index, out_basis))
    return total.astype(jnp.bfloat16)
```

```python
import jax
import jax.numpy as jnp
from jax import lax
from jax.sharding import PartitionSpec as P

COLUMN_CHUNKS = 2


def partner(value, axis, mask):
    pairs = [(source, source ^ mask) for source in range(lax.axis_size(axis))]
    return lax.ppermute(value, axis, pairs)


def dot(a, b):
    return jnp.dot(a, b, preferred_element_type=jnp.float32)


def on_device(excitation, leaf_basis, transfer, transfer_index, out_basis):
    boxes = leaf_basis.shape[1]
    rank = leaf_basis.shape[2]
    levels = transfer.shape[1]
    columns = excitation.shape[3]
    width = columns // COLUMN_CHUNKS
    n_blk = lax.axis_size("blk")
    rows = out_basis.shape[2] // n_blk
    nbits = lax.axis_size("box").bit_length() - 1
    position = lax.axis_index("box")
    block = lax.axis_index("blk")

    def half(level, slot, upper):
        index = transfer_index[0, level, slot]
        lo = jnp.where(index == 1, transfer[0, level, 1, :, :rank], transfer[0, level, 0, :, :rank])
        hi = jnp.where(index == 1, transfer[0, level, 1, :, rank:], transfer[0, level, 0, :, rank:])
        return jnp.where(upper, hi, lo), jnp.where(upper, lo, hi)

    chunks = [(c, s) for c in range(COLUMN_CHUNKS) for s in range(boxes)]
    leaf = {
        (c, s): dot(leaf_basis[0, s], excitation[0, s, :, c * width : (c + 1) * width]).astype(jnp.bfloat16)
        for c, s in chunks
    }
    coeff = {}
    for c, s in chunks:
        lo, hi = half(0, s, False)
        coeff[c, s] = (dot(lo, leaf[c, 0]) + dot(hi, leaf[c, 1])).astype(jnp.bfloat16)
    for level in range(1, levels):
        bit = (level - 1) % nbits
        upper = (position >> bit) & 1 == 1
        pairs = [half(level, s, upper) for s in range(boxes)]
        after = {}
        for c, s in chunks:
            own, other = pairs[s]
            mine = coeff[c, s]
            theirs = partner(mine, "box", 2**bit)
            after[c, s] = (dot(own, mine) + dot(other, theirs)).astype(jnp.bfloat16)
        coeff = after
    parts = [
        [lax.dynamic_slice_in_dim(out_basis[0, s], (block ^ d) * rows, rows, 0) for d in range(n_blk)]
        for s in range(boxes)
    ]
    total = {}
    for c, s in chunks:
        total[c, s] = dot(parts[s][0], coeff[c, s])
        for d in range(n_blk - 1, 0, -1):
            piece = dot(parts[s][d], coeff[c, s]).astype(jnp.bfloat16)
            total[c, s] = total[c, s] + partner(piece, "blk", d).astype(jnp.float32)
        total[c, s] = total[c, s].astype(jnp.bfloat16)
    return jnp.stack(
        [jnp.concatenate([total[c, s] for c in range(COLUMN_CHUNKS)], axis=1) for s in range(boxes)]
    )


def solution(mesh):
    in_specs = (
        P("blk", "box", None, None),
        P("blk", "box", None, None),
        P("blk", None, "box", None, None),
        P("blk", None, "box"),
        P("blk", "box", None, None),
    )
    out_specs = P("box", "blk", None)
    return jax.shard_map(
        on_device, mesh=mesh, in_specs=in_specs, out_specs=out_specs, check_vma=False
    )
```

```python
import functools

import jax
import jax.numpy as jnp
from jax import lax
from jax.experimental import pallas as pl
from jax.experimental.pallas import tpu as pltpu
from jax.sharding import PartitionSpec as P

HALVES = 2
BF16 = jnp.bfloat16
ANY = pl.BlockSpec(memory_space=pl.ANY)
VMEM = pl.BlockSpec(memory_space=pltpu.VMEM)


def dot(a, b):
    return jnp.dot(a, b, preferred_element_type=jnp.float32)


def in_vmem(*shape, dtype=BF16):
    return pltpu.VMEM(shape, dtype)


def here(value):
    return pltpu.with_memory_space_constraint(value, pltpu.VMEM)


def in_hbm(value):
    return pltpu.with_memory_space_constraint(value, pltpu.HBM)


def call(kernel, name, in_specs, out_shape, scratch, args, flops=0, bytes_accessed=0, limit=None, after=()):
    many = isinstance(out_shape, (list, tuple))
    count = len(in_specs)

    def body(*refs):
        kernel(*refs[:count], *refs[count + len(after) :])

    args = [*args, *after]
    return pl.pallas_call(
        body,
        name=name,
        in_specs=[*in_specs, *[ANY] * len(after)],
        out_specs=[VMEM] * len(out_shape) if many else VMEM,
        out_shape=out_shape,
        scratch_shapes=scratch,
        compiler_params=pltpu.CompilerParams(vmem_limit_bytes=limit or 8 * 2**20),
        cost_estimate=pl.CostEstimate(flops=flops, bytes_accessed=bytes_accessed, transcendentals=0),
    )(*args)


def partner(value, axis, mask):
    pairs = [(source, source ^ mask) for source in range(lax.axis_size(axis))]
    return lax.ppermute(value, axis, pairs)


def leaf_kernel(excite, leaves, blocks, index, first_ref, second_ref, next_ref, excite_v, leaves_v, blocks_v, index_s, coeff, sems):
    slots, rank = leaves.shape[0], leaves.shape[1]
    width = first_ref.shape[2]
    listing = pltpu.make_async_copy(index, index_s, sems.at[0])
    listing.start()
    loads = []
    for s in range(slots):
        a = pltpu.make_async_copy(leaves.at[s], leaves_v.at[s], sems.at[1 + s])
        b = pltpu.make_async_copy(excite.at[s], excite_v.at[s], sems.at[3 + s])
        a.start()
        b.start()
        loads.append((a, b))
    listing.wait()
    weights = []
    for s in range(slots):
        c = pltpu.make_async_copy(blocks.at[0, index_s[s, 0]], blocks_v.at[s], sems.at[5 + s])
        c.start()
        weights.append(c)
    later = []
    for s in range(slots):
        c = pltpu.make_async_copy(blocks.at[1, index_s[s, 1]], next_ref.at[s], sems.at[7 + s])
        c.start()
        later.append(c)
    for s in range(slots):
        for load in loads[s]:
            load.wait()
        coeff[s * rank : (s + 1) * rank, :] = dot(leaves_v[s], excite_v[s]).astype(BF16)
    for s in range(slots):
        weights[s].wait()
        out = dot(blocks_v[s], coeff[...]).astype(BF16)
        first_ref[s] = out[:, :width]
        second_ref[s] = out[:, width:]
    for c in later:
        c.wait()


def prefetch_kernel(blocks, basis, index, *refs):
    count = blocks.shape[0] - 2
    outs, basis_v, index_s, sems = refs[:count], refs[count], refs[count + 1], refs[count + 2]
    listing = pltpu.make_async_copy(index, index_s, sems.at[0])
    listing.start()
    listing.wait()
    copies = []
    for level in range(count):
        for s in range(2):
            c = pltpu.make_async_copy(
                blocks.at[level + 2, index_s[s, level + 2]], outs[level].at[s], sems.at[1 + 2 * level + s]
            )
            c.start()
            copies.append(c)
    c = pltpu.make_async_copy(basis, basis_v, sems.at[1 + 2 * count])
    c.start()
    copies.append(c)
    for c in copies:
        c.wait()


def mix(weights, own, other, bit, buf):
    rank = own.shape[0]
    upper = (lax.axis_index("box") >> bit) & 1
    buf[pl.ds(pl.multiple_of(upper * rank, rank), rank), :] = own
    buf[pl.ds(pl.multiple_of((1 - upper) * rank, rank), rank), :] = other
    return dot(weights, buf[...]).astype(BF16)


def first_kernel(bit, s, own, other, weights, out, buf):
    out[...] = mix(weights[s], own[s], other[s], bit, buf)


def level_kernel(bit, s, own, other, weights, out, buf):
    out[...] = mix(weights[s], own[...], other[...], bit, buf)


def pair_kernel(bit, s, bit_next, s_next, own, other, weights, own_n, other_n, weights_n, out, out_n, buf, buf_n):
    out[...] = mix(weights[s], own[...], other[...], bit, buf)
    out_n[...] = mix(weights_n[s_next], own_n[s_next], other_n[s_next], bit_next, buf_n)


def last_kernel(bit, s, own, other, weights, basis, *refs):
    pieces, mine, buf = refs[:-2], refs[-2], refs[-1]
    coeff = mix(weights[s], own[...], other[...], bit, buf)
    rows = mine.shape[0]
    me = lax.axis_index("blk")
    for d, piece in enumerate(pieces, 1):
        start = pl.multiple_of((me ^ d) * rows, rows)
        piece[...] = dot(basis[s, pl.ds(start, rows), :], coeff).astype(BF16)
    start = pl.multiple_of(me * rows, rows)
    mine[...] = dot(basis[s, pl.ds(start, rows), :], coeff)


def sum_kernel(places, per, *refs):
    out = refs[-1]
    for at, (s, start, width) in enumerate(places):
        group = refs[at * per : (at + 1) * per]
        total = group[0][...]
        for piece in group[1:]:
            total = total + piece[...].astype(jnp.float32)
        out[s, :, start : start + width] = total.astype(BF16)


def on_device(excitation, leaf_basis, transfer, transfer_index, out_basis):
    excite, leaves, blocks, basis = excitation[0], leaf_basis[0], transfer[0], out_basis[0]
    index = transfer_index[0].T
    slots, rank, points = leaves.shape
    levels = blocks.shape[0]
    columns = excite.shape[2]
    width = columns // HALVES
    n_blk = lax.axis_size("blk")
    rows = basis.shape[1] // n_blk
    nbits = lax.axis_size("box").bit_length() - 1
    bits = [None] + [(level - 1) % nbits for level in range(1, levels)]
    pair = (slots, rank, 2 * rank)

    *coeff1, weights1 = call(
        leaf_kernel,
        "leaf",
        [ANY] * 4,
        [in_vmem(slots, rank, width)] * 2 + [in_vmem(*pair)],
        [
            in_vmem(*excite.shape),
            in_vmem(*leaves.shape),
            in_vmem(*pair),
            pltpu.SMEM(index.shape, jnp.int32),
            in_vmem(2 * rank, columns),
            pltpu.SemaphoreType.DMA((9,)),
        ],
        [in_hbm(excite), in_hbm(leaves), in_hbm(blocks), in_hbm(index)],
        flops=2 * slots * rank * columns * (points + 2 * rank),
        bytes_accessed=6 * 2**20,
        limit=24 * 2**20,
    )
    near1 = [partner(c, "box", 2 ** bits[1]) for c in coeff1]

    chunks = [(h, s) for h in range(HALVES) for s in range(slots)]
    shape = in_vmem(rank, width)
    buf = in_vmem(2 * rank, width)
    work = 4 * rank * rank * width
    touched = 2 * (2 * rank * rank + 3 * rank * width)

    def step(level, j, own, other, after=()):
        return call(
            functools.partial(level_kernel, bits[level], chunks[j][1]),
            f"level{level}_{j}",
            [VMEM] * 3,
            shape,
            [buf],
            [here(own), here(other), here(weights[level])],
            flops=work,
            bytes_accessed=touched,
            after=after,
        )

    h, s = chunks[0]
    coeff2 = call(
        functools.partial(first_kernel, bits[1], s),
        "level1_0",
        [VMEM] * 3,
        shape,
        [buf],
        [here(coeff1[h]), here(near1[h]), here(weights1)],
        flops=work,
        bytes_accessed=touched,
    )
    near2 = partner(coeff2, "box", 2 ** bits[2])
    *weights, basis_v = call(
        prefetch_kernel,
        "prefetch",
        [ANY] * 3,
        [in_vmem(*pair)] * (levels - 2) + [in_vmem(*basis.shape)],
        [pltpu.SMEM(index.shape, jnp.int32), pltpu.SemaphoreType.DMA((2 * levels,))],
        [in_hbm(blocks), in_hbm(basis), in_hbm(index)],
        bytes_accessed=5 * 2**20,
        after=[coeff2],
    )
    weights = [None, weights1] + weights
    coeff3, near3, groups = {}, {}, []

    def finish(j):
        h, s = chunks[j]
        own, other = coeff3[j], near3[j]
        follow = [coeff3[j + 1]] if j + 1 < len(chunks) else []
        for level in range(3, levels - 1):
            own = step(level, j, own, other, follow)
            other = partner(own, "box", 2 ** bits[level + 1])
        *pieces, mine = call(
            functools.partial(last_kernel, bits[levels - 1], s),
            f"last_{j}",
            [VMEM] * 4,
            [in_vmem(rows, width)] * (n_blk - 1) + [in_vmem(rows, width, dtype=jnp.float32)],
            [buf],
            [here(own), here(other), here(weights[levels - 1]), here(basis_v)],
            flops=work + 2 * n_blk * rows * rank * width,
            bytes_accessed=touched + 2 * n_blk * rows * (rank + width),
        )
        got = {d: partner(pieces[d - 1], "blk", d) for d in range(n_blk - 1, 0, -1)}
        groups.extend([mine] + [got[d] for d in range(1, n_blk)])
        return mine

    done = []
    for j in range(len(chunks)):
        if j + 1 < len(chunks):
            h, s = chunks[j + 1]
            coeff3[j], coeff2_next = call(
                functools.partial(pair_kernel, bits[2], chunks[j][1], bits[1], s),
                f"level2_{j}_level1_{j + 1}",
                [VMEM] * 6,
                [shape] * 2,
                [buf] * 2,
                [here(coeff2), here(near2), here(weights[2]), here(coeff1[h]), here(near1[h]), here(weights1)],
                flops=2 * work,
                bytes_accessed=2 * touched,
                after=done[-1:],
            )
        else:
            coeff3[j] = step(2, j, coeff2, near2, done[-1:])
        near3[j] = partner(coeff3[j], "box", 2 ** bits[3])
        if j + 1 < len(chunks):
            coeff2 = coeff2_next
            near2 = partner(coeff2, "box", 2 ** bits[2])
        if j > 0:
            done.append(finish(j - 1))
    finish(len(chunks) - 1)
    return pl.pallas_call(
        functools.partial(sum_kernel, [(s, h * width, width) for h, s in chunks], n_blk),
        name="sum",
        in_specs=[VMEM] * len(groups),
        out_specs=VMEM,
        out_shape=jax.ShapeDtypeStruct((slots, rows, columns), BF16),
        compiler_params=pltpu.CompilerParams(vmem_limit_bytes=16 * 2**20),
    )(*[here(g) for g in groups])


def solution(mesh):
    in_specs = (
        P("blk", "box", None, None),
        P("blk", "box", None, None),
        P("blk", None, "box", None, None),
        P("blk", None, "box"),
        P("blk", "box", None, None),
    )
    out_specs = P("box", "blk", None)
    return jax.shard_map(
        on_device, mesh=mesh, in_specs=in_specs, out_specs=out_specs, check_vma=False
    )
```

```python
import functools

import jax
import jax.numpy as jnp
from jax import lax
from jax.experimental import pallas as pl
from jax.experimental.pallas import tpu as pltpu
from jax.sharding import PartitionSpec as P

HALVES = 2
BF16 = jnp.bfloat16
F32 = jnp.float32
ANY = pl.BlockSpec(memory_space=pl.ANY)
VMEM = pl.BlockSpec(memory_space=pltpu.VMEM)


def dot(a, b):
    return jnp.dot(a, b, preferred_element_type=F32)


def in_vmem(*shape, dtype=BF16):
    return pltpu.VMEM(shape, dtype)


def here(value):
    return pltpu.with_memory_space_constraint(value, pltpu.VMEM)


def in_hbm(value):
    return pltpu.with_memory_space_constraint(value, pltpu.HBM)


def call(kernel, name, in_specs, out_shape, scratch, args, after=(), flops=6 * 10**9, limit=8 * 2**20):
    count = len(in_specs)

    def body(*refs):
        kernel(*refs[:count], *refs[count + len(after) :])

    return pl.pallas_call(
        body,
        name=name,
        in_specs=[*in_specs, *[ANY] * len(after)],
        out_specs=[VMEM] * len(out_shape),
        out_shape=out_shape,
        scratch_shapes=scratch,
        compiler_params=pltpu.CompilerParams(vmem_limit_bytes=limit),
        cost_estimate=pl.CostEstimate(flops=flops, bytes_accessed=0, transcendentals=0),
    )(*args, *after)


def partner(value, axis, mask):
    pairs = [(source, source ^ mask) for source in range(lax.axis_size(axis))]
    return lax.ppermute(value, axis, pairs)


def leaf_kernel(excite, leaves, blocks, index, *refs):
    firsts, next_ref = refs[:HALVES], refs[HALVES]
    excite_v, leaves_v, blocks_v, index_s, coeff, sems = refs[HALVES + 1 :]
    slots, rank = leaves.shape[0], leaves.shape[1]
    width = firsts[0].shape[2]
    listing = pltpu.make_async_copy(index, index_s, sems.at[0])
    listing.start()
    loads = []
    for s in range(slots):
        a = pltpu.make_async_copy(leaves.at[s], leaves_v.at[s], sems.at[1 + s])
        b = pltpu.make_async_copy(excite.at[s], excite_v.at[s], sems.at[3 + s])
        a.start()
        b.start()
        loads.append((a, b))
    listing.wait()
    weights, later = [], []
    for s in range(slots):
        c = pltpu.make_async_copy(blocks.at[0, index_s[s, 0]], blocks_v.at[s], sems.at[5 + s])
        c.start()
        weights.append(c)
    for s in range(slots):
        c = pltpu.make_async_copy(blocks.at[1, index_s[s, 1]], next_ref.at[s], sems.at[7 + s])
        c.start()
        later.append(c)
    for s in range(slots):
        for load in loads[s]:
            load.wait()
        coeff[s * rank : (s + 1) * rank, :] = dot(leaves_v[s], excite_v[s]).astype(BF16)
    for s in range(slots):
        weights[s].wait()
        out = dot(blocks_v[s], coeff[...]).astype(BF16)
        for h in range(HALVES):
            firsts[h][s] = out[:, h * width : (h + 1) * width]
    for c in later:
        c.wait()


def prefetch_kernel(blocks, basis, index, *refs):
    count = blocks.shape[0] - 2
    outs, basis_v, index_s, sems = refs[:count], refs[count], refs[count + 1], refs[count + 2]
    listing = pltpu.make_async_copy(index, index_s, sems.at[0])
    listing.start()
    listing.wait()
    copies = []
    for level in range(count):
        for s in range(2):
            c = pltpu.make_async_copy(
                blocks.at[level + 2, index_s[s, level + 2]], outs[level].at[s], sems.at[1 + 2 * level + s]
            )
            c.start()
            copies.append(c)
    c = pltpu.make_async_copy(basis, basis_v, sems.at[1 + 2 * count])
    c.start()
    copies.append(c)
    for c in copies:
        c.wait()


def upper_half(bit):
    return (lax.axis_index("box") >> bit) & 1


def mix(weights, own, other, bit, buf):
    rank = own.shape[0]
    upper = upper_half(bit)
    buf[pl.ds(pl.multiple_of(upper * rank, rank), rank), :] = own
    buf[pl.ds(pl.multiple_of((1 - upper) * rank, rank), rank), :] = other
    return dot(weights, buf[...]).astype(BF16)


def levels_kernel(jobs, *refs):
    count = len(jobs)
    ins, outs, bufs = refs[: 3 * count], refs[3 * count : 4 * count], refs[4 * count :]
    for at, (bit, s, both) in enumerate(jobs):
        own, other, weights = ins[3 * at : 3 * at + 3]
        own, other = (own[s], other[s]) if both else (own[...], other[...])
        outs[at][...] = mix(weights[s], own, other, bit, bufs[at])


def half_dot(weights, s, half, value):
    rank = value.shape[0]
    return dot(weights[s, :, pl.ds(pl.multiple_of(half * rank, 128), rank)], value)


def between_kernel(bit, s, fold, total, own, weights, *refs):
    refs = list(refs)
    ins = [refs.pop(0) for _ in range(2 * (fold + total))]
    partial = refs.pop(0)
    partial[...] = half_dot(weights, s, upper_half(bit), own[...])
    if fold:
        keep, got = ins.pop(0), ins.pop(0)
        send, rest = refs.pop(0), refs.pop(0)
        rows = rest.shape[0]
        rest[...] = keep[:rows] + got[:rows].astype(F32)
        send[...] = (keep[rows:] + got[rows:].astype(F32)).astype(BF16)
    if total:
        keep, got = ins.pop(0), ins.pop(0)
        refs.pop(0)[...] = (keep[...] + got[...].astype(F32)).astype(BF16)


def last_kernel(bit, s, order, partial, other, weights, basis, *refs):
    coeff = (partial[...] + half_dot(weights, s, 1 - upper_half(bit), other[...])).astype(BF16)
    rows = basis.shape[1] // lax.axis_size("blk")
    me = lax.axis_index("blk")
    for ref, distances in zip(refs, order):
        for at, d in enumerate(distances):
            start = pl.multiple_of((me ^ d) * rows, rows)
            piece = dot(basis[s, pl.ds(start, rows), :], coeff)
            ref[at * rows : (at + 1) * rows, :] = piece.astype(ref.dtype)


def fold_kernel(keep, got, send, rest):
    rows = rest.shape[0]
    rest[...] = keep[:rows] + got[:rows].astype(F32)
    send[...] = (keep[rows:] + got[rows:].astype(F32)).astype(BF16)


def end_kernel(places, counts, *refs):
    refs = list(refs)
    out = refs[-1]
    for (s, start, width), count in zip(places, counts):
        group = [refs.pop(0) for _ in range(count)]
        total = group[0][...].astype(F32)
        for piece in group[1:]:
            total = total + piece[...].astype(F32)
        out[s, :, start : start + width] = total.astype(BF16)


def on_device(excitation, leaf_basis, transfer, transfer_index, out_basis):
    excite, leaves, blocks, basis = excitation[0], leaf_basis[0], transfer[0], out_basis[0]
    index = transfer_index[0].T
    slots, rank, points = leaves.shape
    levels = blocks.shape[0]
    columns = excite.shape[2]
    width = columns // HALVES
    n_blk = lax.axis_size("blk")
    rows = basis.shape[1] // n_blk
    nbits = lax.axis_size("box").bit_length() - 1
    bits = [None] + [(level - 1) % nbits for level in range(1, levels)]
    pair = in_vmem(slots, rank, 2 * rank)
    shape = in_vmem(rank, width)
    buf = in_vmem(2 * rank, width)
    chunks = [(h, s) for h in range(HALVES) for s in range(slots)]

    *coeff1, weights1 = call(
        leaf_kernel,
        "leaf",
        [ANY] * 4,
        [in_vmem(slots, rank, width)] * HALVES + [pair],
        [
            in_vmem(*excite.shape),
            in_vmem(*leaves.shape),
            pair,
            pltpu.SMEM(index.shape, jnp.int32),
            in_vmem(2 * rank, columns),
            pltpu.SemaphoreType.DMA((9,)),
        ],
        [in_hbm(excite), in_hbm(leaves), in_hbm(blocks), in_hbm(index)],
        limit=24 * 2**20,
    )
    weights = [None, weights1]
    near1 = [partner(c, "box", 2 ** bits[1]) for c in coeff1]

    def cross(level, value):
        return partner(value, "box", 2 ** bits[level])

    def step(name, jobs, after=()):
        args = [here(v) for level, j, own, other in jobs for v in (own, other, weights[level])]
        return call(
            functools.partial(
                levels_kernel, [(bits[level], chunks[j][1], level == 1) for level, j, _, _ in jobs]
            ),
            name,
            [VMEM] * len(args),
            [shape] * len(jobs),
            [buf] * len(jobs),
            args,
            after,
        )

    def job1(j):
        h = chunks[j][0]
        return (1, j, coeff1[h], near1[h])

    coeff2, near2, coeff3, near3 = {}, {}, {}, {}
    coeff2[0], coeff2[1] = step("level1_a", [job1(0), job1(1)])
    for j in (0, 1):
        near2[j] = cross(2, coeff2[j])
    *more, basis_v = call(
        prefetch_kernel,
        "prefetch",
        [ANY] * 3,
        [pair] * (levels - 2) + [in_vmem(*basis.shape)],
        [pltpu.SMEM(index.shape, jnp.int32), pltpu.SemaphoreType.DMA((2 * levels,))],
        [in_hbm(blocks), in_hbm(basis), in_hbm(index)],
        [coeff2[0]],
    )
    weights += more
    (coeff3[0],) = step("level2_0", [(2, 0, coeff2[0], near2[0])])
    near3[0] = cross(3, coeff3[0])
    coeff3[1], coeff2[2], coeff2[3] = step(
        "level2_1", [(2, 1, coeff2[1], near2[1]), job1(2), job1(3)], [coeff3[0]]
    )
    near3[1] = cross(3, coeff3[1])
    for j in (2, 3):
        near2[j] = cross(2, coeff2[j])

    masks = [1 << b for b in range(n_blk.bit_length() - 1)]

    def halving(j):
        order = masks if j % 2 else masks[::-1]
        pieces = [0]
        for mask in order[::-1]:
            pieces = pieces + [d | mask for d in pieces]
        return order, pieces

    def result(count, dtype):
        return in_vmem(count * rows, width, dtype=dtype)

    def tail(j, after, folding, totalling):
        s = chunks[j][1]
        (coeff4,) = step(f"level3_{j}", [(3, j, coeff3[j], near3[j])], after)
        near4 = cross(4, coeff4)
        outs, extra = [in_vmem(rank, width, dtype=F32)], []
        if folding is not None:
            keep, got, count = folding
            extra += [keep, got]
            outs += [result(count // 2, BF16), result(count // 2, F32)]
        if totalling is not None:
            extra += totalling
            outs += [result(1, BF16)]
        partial, *rest = call(
            functools.partial(
                between_kernel, bits[4], s, folding is not None, totalling is not None
            ),
            f"between_{j}",
            [VMEM] * (2 + len(extra)),
            outs,
            [],
            [here(v) for v in (coeff4, weights[4], *extra)],
            flops=6 * 10**9,
        )
        if j == len(chunks) - 1:
            order = [[0]] + [[d] for d in range(1, n_blk)]
        else:
            pieces = halving(j)[1]
            order = [pieces[: n_blk // 2], pieces[n_blk // 2 :]]
        kinds = [F32] + [BF16] * (len(order) - 1)
        out = call(
            functools.partial(last_kernel, bits[4], s, order),
            f"last_{j}",
            [VMEM] * 4,
            [result(len(o), kind) for o, kind in zip(order, kinds)],
            [],
            [here(v) for v in (partial, near4, weights[4], basis_v)],
        )
        return out, rest

    def fold_all(j, keep, got, count):
        for mask in halving(j)[0][1:-1]:
            send, keep = call(
                fold_kernel,
                f"fold_{j}_{mask}",
                [VMEM] * 2,
                [result(count // 2, BF16), result(count // 2, F32)],
                [],
                [here(keep), here(got)],
            )
            got = partner(send, "blk", mask)
            count //= 2
        return keep, got, count

    def begin(j, out):
        keep, send = out
        return fold_all(j, keep, partner(send, "blk", halving(j)[0][0]), n_blk // 2)

    out0, _ = tail(0, [coeff3[1]], None, None)
    fold0 = begin(0, out0)
    (coeff3[2],) = step("level2_2", [(2, 2, coeff2[2], near2[2])], [out0[0]])
    near3[2] = cross(3, coeff3[2])
    (coeff3[3],) = step("level2_3", [(2, 3, coeff2[3], near2[3])], [coeff3[2]])
    near3[3] = cross(3, coeff3[3])
    out1, (send0, keep0) = tail(1, [coeff3[3]], fold0, None)
    got0 = partner(send0, "blk", halving(0)[0][-1])
    fold1 = begin(1, out1)
    out2, (send1, keep1, total0) = tail(2, [out1[0]], fold1, [keep0, got0])
    got1 = partner(send1, "blk", halving(1)[0][-1])
    fold2 = begin(2, out2)
    out3, (send2, keep2, total1) = tail(3, [out2[0]], fold2, [keep1, got1])
    got2 = partner(send2, "blk", halving(2)[0][-1])
    group3 = [out3[0]] + [partner(out3[d], "blk", d) for d in range(1, n_blk)]
    groups = [[total0], [total1], [keep2, got2], group3]
    flat = [here(v) for group in groups for v in group]
    return pl.pallas_call(
        functools.partial(
            end_kernel, [(s, h * width, width) for h, s in chunks], [len(group) for group in groups]
        ),
        name="end",
        in_specs=[VMEM] * len(flat),
        out_specs=VMEM,
        out_shape=jax.ShapeDtypeStruct((slots, rows, columns), BF16),
        compiler_params=pltpu.CompilerParams(vmem_limit_bytes=8 * 2**20),
    )(*flat)


def solution(mesh):
    in_specs = (
        P("blk", "box", None, None),
        P("blk", "box", None, None),
        P("blk", None, "box", None, None),
        P("blk", None, "box"),
        P("blk", "box", None, None),
    )
    out_specs = P("box", "blk", None)
    return jax.shard_map(
        on_device, mesh=mesh, in_specs=in_specs, out_specs=out_specs, check_vma=False
    )
```

```python
import functools

import jax
import jax.numpy as jnp
from jax import lax
from jax.experimental import pallas as pl
from jax.experimental.pallas import tpu as pltpu
from jax.sharding import PartitionSpec as P

SHARES = (1, 2, 3, 2)
PRELOADED = 2
COST = 6 * 10**9
BF16 = jnp.bfloat16
F32 = jnp.float32
ANY = pl.BlockSpec(memory_space=pl.ANY)
VMEM = pl.BlockSpec(memory_space=pltpu.VMEM)


def dot(a, b):
    return jnp.dot(a, b, preferred_element_type=F32)


def in_vmem(*shape, dtype=BF16):
    return pltpu.VMEM(shape, dtype)


def here(value):
    return pltpu.with_memory_space_constraint(value, pltpu.VMEM)


def in_hbm(value):
    return pltpu.with_memory_space_constraint(value, pltpu.HBM)


def call(kernel, name, in_specs, out_shape, scratch, args, after=(), flops=COST, limit=8 * 2**20):
    count = len(in_specs)

    def body(*refs):
        kernel(*refs[:count], *refs[count + len(after) :])

    return pl.pallas_call(
        body,
        name=name,
        in_specs=[*in_specs, *[ANY] * len(after)],
        out_specs=[VMEM] * len(out_shape),
        out_shape=out_shape,
        scratch_shapes=scratch,
        compiler_params=pltpu.CompilerParams(vmem_limit_bytes=limit),
        cost_estimate=pl.CostEstimate(flops=flops, bytes_accessed=0, transcendentals=0),
    )(*args, *after)


def partner(value, axis, mask):
    pairs = [(source, source ^ mask) for source in range(lax.axis_size(axis))]
    return lax.ppermute(value, axis, pairs)


def leaf_kernel(excite, leaves, blocks, index, first, rest, *refs):
    count = PRELOADED
    nexts = refs[:count]
    excite_v, leaves_v, blocks_v, index_s, coeff, sems = refs[count:]
    slots, rank = leaves.shape[0], leaves.shape[1]
    columns, width = excite.shape[2], first.shape[1]
    listing = pltpu.make_async_copy(index, index_s, sems.at[0])
    listing.start()
    loads = []
    for s in range(slots):
        a = pltpu.make_async_copy(leaves.at[s], leaves_v.at[s], sems.at[1 + s])
        b = pltpu.make_async_copy(excite.at[s], excite_v.at[s], sems.at[3 + s])
        a.start()
        b.start()
        loads.append((a, b))
    listing.wait()
    weights, later = [], []
    for s in range(slots):
        c = pltpu.make_async_copy(blocks.at[0, index_s[s, 0]], blocks_v.at[s], sems.at[5 + s])
        c.start()
        weights.append(c)
    for level in range(1, 1 + count):
        for s in range(slots):
            c = pltpu.make_async_copy(
                blocks.at[level, index_s[s, level]], nexts[level - 1].at[s], sems.at[5 + 2 * level + s]
            )
            c.start()
            later.append(c)
    for s in range(slots):
        for load in loads[s]:
            load.wait()
        coeff[s * rank : (s + 1) * rank, :] = dot(leaves_v[s], excite_v[s]).astype(BF16)
    for s in range(slots):
        weights[s].wait()
        out = dot(blocks_v[s], coeff[...]).astype(BF16)
        if s == 0:
            first[...] = out[:, :width]
            rest[:, : columns - width] = out[:, width:]
        else:
            rest[:, s * columns - width : (s + 1) * columns - width] = out
    for c in later:
        c.wait()


def prefetch_kernel(blocks, basis, index, *refs):
    count = blocks.shape[0] - 1 - PRELOADED
    outs, basis_v, index_s, sems = refs[:count], refs[count], refs[count + 1], refs[count + 2]
    listing = pltpu.make_async_copy(index, index_s, sems.at[0])
    listing.start()
    c = pltpu.make_async_copy(basis, basis_v, sems.at[1 + 2 * count])
    c.start()
    copies = [c]
    listing.wait()
    for at in range(count):
        level = at + 1 + PRELOADED
        for s in range(2):
            c = pltpu.make_async_copy(blocks.at[level, index_s[s, level]], outs[at].at[s], sems.at[1 + 2 * at + s])
            c.start()
            copies.append(c)
    for c in copies:
        c.wait()


def upper_half(bit):
    return (lax.axis_index("box") >> bit) & 1


def mix(weights, own, other, bit, buf, parts, out):
    rank = own.shape[0]
    upper = upper_half(bit)
    buf[pl.ds(pl.multiple_of(upper * rank, rank), rank), :] = own
    buf[pl.ds(pl.multiple_of((1 - upper) * rank, rank), rank), :] = other
    for s, start, stop in parts:
        out[:, start:stop] = dot(weights[s], buf[:, start:stop]).astype(BF16)


def levels_kernel(jobs, *refs):
    count = len(jobs)
    ins, outs, bufs = refs[: 3 * count], refs[3 * count : 4 * count], refs[4 * count :]
    for at, (bit, parts, lanes) in enumerate(jobs):
        own, other, weights = ins[3 * at : 3 * at + 3]
        mix(weights, own[:, lanes], other[:, lanes], bit, bufs[at], parts, outs[at])


def half_dot(weights, s, half, value):
    rank = value.shape[0]
    return dot(weights[s, :, pl.ds(pl.multiple_of(half * rank, 128), rank)], value)


def between_kernel(bit, parts, fold, total, own, weights, *refs):
    refs = list(refs)
    ins = [refs.pop(0) for _ in range(2 * (fold + total))]
    partial = refs.pop(0)
    for s, start, stop in parts:
        partial[:, start:stop] = half_dot(weights, s, upper_half(bit), own[:, start:stop])
    if fold:
        fold_kernel(ins.pop(0), ins.pop(0), refs.pop(0), refs.pop(0))
    if total:
        keep, got = ins.pop(0), ins.pop(0)
        refs.pop(0)[...] = (keep[...] + got[...].astype(F32)).astype(BF16)


def last_kernel(bit, parts, order, partial, other, weights, basis, *refs):
    rows = basis.shape[1] // lax.axis_size("blk")
    me = lax.axis_index("blk")
    for s, start, stop in parts:
        mixed = partial[:, start:stop] + half_dot(weights, s, 1 - upper_half(bit), other[:, start:stop])
        coeff = mixed.astype(BF16)
        for ref, distances in zip(refs, order):
            for at, d in enumerate(distances):
                row = pl.multiple_of((me ^ d) * rows, rows)
                piece = dot(basis[s, pl.ds(row, rows), :], coeff)
                ref[at * rows : (at + 1) * rows, start:stop] = piece.astype(ref.dtype)


def fold_kernel(keep, got, send, rest):
    rows = rest.shape[0]
    rest[...] = keep[:rows] + got[:rows].astype(F32)
    send[...] = (keep[rows:] + got[rows:].astype(F32)).astype(BF16)


def end_kernel(places, counts, *refs):
    refs = list(refs)
    out = refs[-1]
    for place, count in zip(places, counts):
        group = [refs.pop(0) for _ in range(count)]
        for s, column, start, stop in place:
            total = group[0][:, start:stop].astype(F32)
            for piece in group[1:]:
                total = total + piece[:, start:stop].astype(F32)
            out[s, :, column : column + stop - start] = total.astype(BF16)


def on_device(excitation, leaf_basis, transfer, transfer_index, out_basis):
    excite, leaves, blocks, basis = excitation[0], leaf_basis[0], transfer[0], out_basis[0]
    index = transfer_index[0].T
    slots, rank, points = leaves.shape
    levels = blocks.shape[0]
    columns = excite.shape[2]
    n_blk = lax.axis_size("blk")
    rows = basis.shape[1] // n_blk
    nbits = lax.axis_size("box").bit_length() - 1
    bits = [None] + [(level - 1) % nbits for level in range(1, levels)]
    pair = in_vmem(slots, rank, 2 * rank)

    unit = slots * columns // sum(SHARES)
    widths = [unit * share for share in SHARES]
    begins = [sum(widths[:j]) for j in range(len(widths))]
    parts, places = [], []
    for begin, width in zip(begins, widths):
        part, place, lane = [], [], 0
        while lane < width:
            s, column = divmod(begin + lane, columns)
            size = min(width - lane, columns - column)
            part.append((s, lane, lane + size))
            place.append((s, column, lane, lane + size))
            lane += size
        parts.append(part)
        places.append(place)

    first, rest, *weights = call(
        leaf_kernel,
        "leaf",
        [ANY] * 4,
        [in_vmem(rank, widths[0]), in_vmem(rank, slots * columns - widths[0])] + [pair] * PRELOADED,
        [
            in_vmem(*excite.shape),
            in_vmem(*leaves.shape),
            pair,
            pltpu.SMEM(index.shape, jnp.int32),
            in_vmem(2 * rank, columns),
            pltpu.SemaphoreType.DMA((7 + 2 * PRELOADED,)),
        ],
        [in_hbm(excite), in_hbm(leaves), in_hbm(blocks), in_hbm(index)],
        limit=24 * 2**20,
    )
    weights = [None, *weights]

    def cross(level, value):
        return partner(value, "box", 2 ** bits[level])

    near_first, near_rest = cross(1, first), cross(1, rest)

    def step(name, jobs, after=(), flops=COST):
        args = [here(v) for level, j, own, other in jobs for v in (own, other, weights[level])]
        described, sizes = [], []
        for level, j, _, _ in jobs:
            begin = begins[j] - widths[0] if level == 1 and j else 0
            described.append((bits[level], parts[j], slice(begin, begin + widths[j])))
            sizes.append(widths[j])
        return call(
            functools.partial(levels_kernel, described),
            name,
            [VMEM] * len(args),
            [in_vmem(rank, size) for size in sizes],
            [in_vmem(2 * rank, size) for size in sizes],
            args,
            after,
            flops,
        )

    def job1(j):
        return (1, j, rest, near_rest) if j else (1, j, first, near_first)

    coeff2, near2, coeff3, near3 = {}, {}, {}, {}

    def second(j, value):
        coeff2[j] = value
        near2[j] = cross(2, value)

    def third(j, value):
        coeff3[j] = value
        near3[j] = cross(3, value)

    (value,) = step("level1_0", [job1(0)])
    second(0, value)
    (value,) = step("level1_1", [job1(1)], [coeff2[0]])
    second(1, value)
    value, ahead = step("level2_0", [(2, 0, coeff2[0], near2[0]), job1(2)], [coeff2[1]])
    third(0, value)
    second(2, ahead)
    *more, basis_v = call(
        prefetch_kernel,
        "prefetch",
        [ANY] * 3,
        [pair] * (levels - 1 - PRELOADED) + [in_vmem(*basis.shape)],
        [pltpu.SMEM(index.shape, jnp.int32), pltpu.SemaphoreType.DMA((2 * levels,))],
        [in_hbm(blocks), in_hbm(basis), in_hbm(index)],
        [coeff3[0]],
    )
    weights += more
    value, ahead = step("level2_1", [(2, 1, coeff2[1], near2[1]), job1(3)], [basis_v])
    third(1, value)
    second(3, ahead)

    masks = [1 << b for b in range(n_blk.bit_length() - 1)]

    def halving(j):
        order = masks if j % 2 else masks[::-1]
        pieces = [0]
        for mask in order[::-1]:
            pieces = pieces + [d | mask for d in pieces]
        return order, pieces

    def result(j, count, dtype):
        return in_vmem(count * rows, widths[j], dtype=dtype)

    def tail(j, after, direct, folding=None, totalling=None):
        (coeff4,) = step(f"level3_{j}", [(3, j, coeff3[j], near3[j])], after, flops=0 if j == 1 else COST)
        near4 = cross(4, coeff4)
        outs, extra = [in_vmem(rank, widths[j], dtype=F32)], []
        if folding is not None:
            at, keep, got, count = folding
            extra += [keep, got]
            outs += [result(at, count // 2, BF16), result(at, count // 2, F32)]
        if totalling is not None:
            at, keep, got = totalling
            extra += [keep, got]
            outs += [result(at, 1, BF16)]
        partial, *more = call(
            functools.partial(
                between_kernel, bits[4], parts[j], folding is not None, totalling is not None
            ),
            f"between_{j}",
            [VMEM] * (2 + len(extra)),
            outs,
            [],
            [here(v) for v in (coeff4, weights[4], *extra)],
        )
        if direct:
            order = [[d] for d in range(n_blk)]
        else:
            pieces = halving(j)[1]
            order = [pieces[: n_blk // 2], pieces[n_blk // 2 :]]
        kinds = [F32] + [BF16] * (len(order) - 1)
        out = call(
            functools.partial(last_kernel, bits[4], parts[j], order),
            f"last_{j}",
            [VMEM] * 4,
            [result(j, len(o), kind) for o, kind in zip(order, kinds)],
            [],
            [here(v) for v in (partial, near4, weights[4], basis_v)],
        )
        return out, more

    def begin_sum(j, out):
        keep, send = out
        order = halving(j)[0]
        got, count = partner(send, "blk", order[0]), n_blk // 2
        for mask in order[1:-1]:
            send, keep = call(
                fold_kernel,
                f"fold_{j}_{mask}",
                [VMEM] * 2,
                [result(j, count // 2, BF16), result(j, count // 2, F32)],
                [],
                [here(keep), here(got)],
            )
            got, count = partner(send, "blk", mask), count // 2
        return j, keep, got, count

    def direct_sum(out):
        return [out[0]] + [partner(out[d], "blk", d) for d in range(n_blk - 1, 0, -1)]

    out0, _ = tail(0, [coeff3[1]], False)
    fold0 = begin_sum(0, out0)
    (value,) = step("level2_2", [(2, 2, coeff2[2], near2[2])], [out0[0]])
    third(2, value)
    (value,) = step("level2_3", [(2, 3, coeff2[3], near2[3])], [coeff3[2]])
    third(3, value)
    out1, (send0, keep0) = tail(1, [coeff3[3]], False, fold0)
    got0 = partner(send0, "blk", halving(0)[0][-1])
    fold1 = begin_sum(1, out1)
    out2, (send1, keep1, total0) = tail(2, [out1[0]], True, fold1, (0, keep0, got0))
    got1 = partner(send1, "blk", halving(1)[0][-1])
    group2 = direct_sum(out2)
    out3, (total1,) = tail(3, [out2[0]], True, None, (1, keep1, got1))
    group3 = direct_sum(out3)
    groups = [[total0], [total1], group2, group3]
    flat = [here(v) for group in groups for v in group]
    return pl.pallas_call(
        functools.partial(end_kernel, places, [len(group) for group in groups]),
        name="end",
        in_specs=[VMEM] * len(flat),
        out_specs=VMEM,
        out_shape=jax.ShapeDtypeStruct((slots, rows, columns), BF16),
        compiler_params=pltpu.CompilerParams(vmem_limit_bytes=8 * 2**20),
    )(*flat)


def solution(mesh):
    in_specs = (
        P("blk", "box", None, None),
        P("blk", "box", None, None),
        P("blk", None, "box", None, None),
        P("blk", None, "box"),
        P("blk", "box", None, None),
    )
    out_specs = P("box", "blk", None)
    return jax.shard_map(
        on_device, mesh=mesh, in_specs=in_specs, out_specs=out_specs, check_vma=False
    )
```

```python
import functools

import jax
import jax.numpy as jnp
from jax import lax
from jax.experimental import pallas as pl
from jax.experimental.pallas import tpu as pltpu
from jax.sharding import PartitionSpec as P

SHARES = (1, 2, 3, 2)
PRELOADED = 2
COST = 6 * 10**9
BF16 = jnp.bfloat16
F32 = jnp.float32
ANY = pl.BlockSpec(memory_space=pl.ANY)
VMEM = pl.BlockSpec(memory_space=pltpu.VMEM)


def dot(a, b):
    return jnp.dot(a, b, preferred_element_type=F32)


def in_vmem(*shape, dtype=BF16):
    return pltpu.VMEM(shape, dtype)


def here(value):
    return pltpu.with_memory_space_constraint(value, pltpu.VMEM)


def in_hbm(value):
    return pltpu.with_memory_space_constraint(value, pltpu.HBM)


def call(kernel, name, in_specs, out_shape, scratch, args, after=(), flops=COST, limit=8 * 2**20):
    count = len(in_specs)

    def body(*refs):
        kernel(*refs[:count], *refs[count + len(after) :])

    return pl.pallas_call(
        body,
        name=name,
        in_specs=[*in_specs, *[ANY] * len(after)],
        out_specs=[VMEM] * len(out_shape),
        out_shape=out_shape,
        scratch_shapes=scratch,
        compiler_params=pltpu.CompilerParams(vmem_limit_bytes=limit),
        cost_estimate=pl.CostEstimate(flops=flops, bytes_accessed=0, transcendentals=0),
    )(*args, *after)


def partner(value, axis, mask):
    pairs = [(source, source ^ mask) for source in range(lax.axis_size(axis))]
    return lax.ppermute(value, axis, pairs)


def leaf_kernel(excite, leaves, blocks, index, first, rest, *refs):
    count = PRELOADED
    nexts = refs[:count]
    excite_v, leaves_v, blocks_v, index_s, coeff, sems = refs[count:]
    slots, rank = leaves.shape[0], leaves.shape[1]
    columns, width = excite.shape[2], first.shape[1]
    listing = pltpu.make_async_copy(index, index_s, sems.at[0])
    listing.start()
    loads = []
    for s in range(slots):
        a = pltpu.make_async_copy(leaves.at[s], leaves_v.at[s], sems.at[1 + s])
        b = pltpu.make_async_copy(excite.at[s], excite_v.at[s], sems.at[3 + s])
        a.start()
        b.start()
        loads.append((a, b))
    listing.wait()
    weights, later = [], []
    for s in range(slots):
        c = pltpu.make_async_copy(blocks.at[0, index_s[s, 0]], blocks_v.at[s], sems.at[5 + s])
        c.start()
        weights.append(c)
    for level in range(1, 1 + count):
        for s in range(slots):
            c = pltpu.make_async_copy(
                blocks.at[level, index_s[s, level]], nexts[level - 1].at[s], sems.at[5 + 2 * level + s]
            )
            c.start()
            later.append(c)
    for s in range(slots):
        for load in loads[s]:
            load.wait()
        coeff[s * rank : (s + 1) * rank, :] = dot(leaves_v[s], excite_v[s]).astype(BF16)
    for s in range(slots):
        weights[s].wait()
        out = dot(blocks_v[s], coeff[...]).astype(BF16)
        if s == 0:
            first[...] = out[:, :width]
            rest[:, : columns - width] = out[:, width:]
        else:
            rest[:, s * columns - width : (s + 1) * columns - width] = out
    for c in later:
        c.wait()


def prefetch_kernel(blocks, basis, index, *refs):
    count = blocks.shape[0] - 1 - PRELOADED
    outs, basis_v, index_s, sems = refs[:count], refs[count], refs[count + 1], refs[count + 2]
    listing = pltpu.make_async_copy(index, index_s, sems.at[0])
    listing.start()
    c = pltpu.make_async_copy(basis, basis_v, sems.at[1 + 2 * count])
    c.start()
    copies = [c]
    listing.wait()
    for at in range(count):
        level = at + 1 + PRELOADED
        for s in range(2):
            c = pltpu.make_async_copy(blocks.at[level, index_s[s, level]], outs[at].at[s], sems.at[1 + 2 * at + s])
            c.start()
            copies.append(c)
    for c in copies:
        c.wait()


def upper_half(bit):
    return (lax.axis_index("box") >> bit) & 1


def mix(weights, own, other, bit, buf, parts, out):
    rank = own.shape[0]
    upper = upper_half(bit)
    buf[pl.ds(pl.multiple_of(upper * rank, rank), rank), :] = own
    buf[pl.ds(pl.multiple_of((1 - upper) * rank, rank), rank), :] = other
    for s, start, stop in parts:
        out[:, start:stop] = dot(weights[s], buf[:, start:stop]).astype(BF16)


def levels_kernel(jobs, *refs):
    count = len(jobs)
    ins, outs, bufs = refs[: 3 * count], refs[3 * count : 4 * count], refs[4 * count :]
    for at, (bit, parts, lanes) in enumerate(jobs):
        own, other, weights = ins[3 * at : 3 * at + 3]
        mix(weights, own[:, lanes], other[:, lanes], bit, bufs[at], parts, outs[at])


def half_dot(weights, s, half, value):
    rank = value.shape[0]
    return dot(weights[s, :, pl.ds(pl.multiple_of(half * rank, 128), rank)], value)


def half_kernel(bit, parts, own, weights, partial):
    for s, start, stop in parts:
        partial[:, start:stop] = half_dot(weights, s, upper_half(bit), own[:, start:stop])


def last_kernel(bit, parts, partial, other, weights, basis, mine, pieces):
    rows = mine.shape[0]
    row = pl.multiple_of(lax.axis_index("blk") * rows, rows)
    for s, start, stop in parts:
        mixed = partial[:, start:stop] + half_dot(weights, s, 1 - upper_half(bit), other[:, start:stop])
        coeff = mixed.astype(BF16)
        pieces[:, start:stop] = dot(basis[s], coeff).astype(BF16)
        mine[:, start:stop] = dot(basis[s, pl.ds(row, rows), :], coeff)


def end_kernel(places, *refs):
    refs, out = list(refs[:-1]), refs[-1]
    me = lax.axis_index("blk")
    for place in places:
        mine, got = refs.pop(0), refs.pop(0)
        rows = mine.shape[0]
        count = got.shape[0] // rows
        for s, column, start, stop in place:
            total = mine[:, start:stop]
            for d in range(1, count):
                row = pl.multiple_of((me ^ d) * rows, rows)
                total = total + got[pl.ds(row, rows), start:stop].astype(F32)
            out[s, :, column : column + stop - start] = total.astype(BF16)


def on_device(excitation, leaf_basis, transfer, transfer_index, out_basis):
    excite, leaves, blocks, basis = excitation[0], leaf_basis[0], transfer[0], out_basis[0]
    index = transfer_index[0].T
    slots, rank, points = leaves.shape
    levels = blocks.shape[0]
    columns = excite.shape[2]
    n_blk = lax.axis_size("blk")
    rows = basis.shape[1] // n_blk
    nbits = lax.axis_size("box").bit_length() - 1
    bits = [None] + [(level - 1) % nbits for level in range(1, levels)]
    pair = in_vmem(slots, rank, 2 * rank)

    unit = slots * columns // sum(SHARES)
    widths = [unit * share for share in SHARES]
    begins = [sum(widths[:j]) for j in range(len(widths))]
    parts, places = [], []
    for begin, width in zip(begins, widths):
        part, place, lane = [], [], 0
        while lane < width:
            s, column = divmod(begin + lane, columns)
            size = min(width - lane, columns - column)
            part.append((s, lane, lane + size))
            place.append((s, column, lane, lane + size))
            lane += size
        parts.append(part)
        places.append(place)

    first, rest, *weights = call(
        leaf_kernel,
        "leaf",
        [ANY] * 4,
        [in_vmem(rank, widths[0]), in_vmem(rank, slots * columns - widths[0])] + [pair] * PRELOADED,
        [
            in_vmem(*excite.shape),
            in_vmem(*leaves.shape),
            pair,
            pltpu.SMEM(index.shape, jnp.int32),
            in_vmem(2 * rank, columns),
            pltpu.SemaphoreType.DMA((7 + 2 * PRELOADED,)),
        ],
        [in_hbm(excite), in_hbm(leaves), in_hbm(blocks), in_hbm(index)],
        limit=24 * 2**20,
    )
    weights = [None, *weights]

    def cross(level, value):
        return partner(value, "box", 2 ** bits[level])

    near_first, near_rest = cross(1, first), cross(1, rest)

    def step(name, jobs, after=(), flops=COST):
        args = [here(v) for level, j, own, other in jobs for v in (own, other, weights[level])]
        described, sizes = [], []
        for level, j, _, _ in jobs:
            begin = begins[j] - widths[0] if level == 1 and j else 0
            described.append((bits[level], parts[j], slice(begin, begin + widths[j])))
            sizes.append(widths[j])
        return call(
            functools.partial(levels_kernel, described),
            name,
            [VMEM] * len(args),
            [in_vmem(rank, size) for size in sizes],
            [in_vmem(2 * rank, size) for size in sizes],
            args,
            after,
            flops,
        )

    def job1(j):
        return (1, j, rest, near_rest) if j else (1, j, first, near_first)

    coeff2, near2, coeff3, near3 = {}, {}, {}, {}

    def second(j, value):
        coeff2[j] = value
        near2[j] = cross(2, value)

    def third(j, value):
        coeff3[j] = value
        near3[j] = cross(3, value)

    (value,) = step("level1_0", [job1(0)])
    second(0, value)
    (value,) = step("level1_1", [job1(1)], [coeff2[0]])
    second(1, value)
    value, ahead = step("level2_0", [(2, 0, coeff2[0], near2[0]), job1(2)], [coeff2[1]])
    third(0, value)
    second(2, ahead)
    *more, basis_v = call(
        prefetch_kernel,
        "prefetch",
        [ANY] * 3,
        [pair] * (levels - 1 - PRELOADED) + [in_vmem(*basis.shape)],
        [pltpu.SMEM(index.shape, jnp.int32), pltpu.SemaphoreType.DMA((2 * levels,))],
        [in_hbm(blocks), in_hbm(basis), in_hbm(index)],
        [coeff3[0]],
    )
    weights += more
    value, ahead = step("level2_1", [(2, 1, coeff2[1], near2[1]), job1(3)], [basis_v])
    third(1, value)
    second(3, ahead)

    def tail(j, after, flops=COST):
        (coeff4,) = step(f"level3_{j}", [(3, j, coeff3[j], near3[j])], after, flops)
        near4 = cross(4, coeff4)
        (partial,) = call(
            functools.partial(half_kernel, bits[4], parts[j]),
            f"half_{j}",
            [VMEM] * 2,
            [in_vmem(rank, widths[j], dtype=F32)],
            [],
            [here(coeff4), here(weights[4])],
        )
        mine, pieces = call(
            functools.partial(last_kernel, bits[4], parts[j]),
            f"last_{j}",
            [VMEM] * 4,
            [in_vmem(rows, widths[j], dtype=F32), in_vmem(n_blk * rows, widths[j])],
            [],
            [here(v) for v in (partial, near4, weights[4], basis_v)],
        )
        return mine, lax.all_to_all(pieces, "blk", 0, 0, tiled=True)

    groups = [tail(0, [coeff3[1]])]
    (value,) = step("level2_2", [(2, 2, coeff2[2], near2[2])], [groups[0][0]])
    third(2, value)
    (value,) = step("level2_3", [(2, 3, coeff2[3], near2[3])], [coeff3[2]])
    third(3, value)
    groups.append(tail(1, [coeff3[3]]))
    groups.append(tail(2, [groups[1][0]]))
    groups.append(tail(3, [groups[2][0]]))
    flat = [here(v) for group in groups for v in group]
    return pl.pallas_call(
        functools.partial(end_kernel, places),
        name="end",
        in_specs=[VMEM] * len(flat),
        out_specs=VMEM,
        out_shape=jax.ShapeDtypeStruct((slots, rows, columns), BF16),
        compiler_params=pltpu.CompilerParams(vmem_limit_bytes=8 * 2**20),
    )(*flat)


def solution(mesh):
    in_specs = (
        P("blk", "box", None, None),
        P("blk", "box", None, None),
        P("blk", None, "box", None, None),
        P("blk", None, "box"),
        P("blk", "box", None, None),
    )
    out_specs = P("box", "blk", None)
    return jax.shard_map(
        on_device, mesh=mesh, in_specs=in_specs, out_specs=out_specs, check_vma=False
    )
```

```python
import functools

import jax
import jax.numpy as jnp
from jax import lax
from jax.experimental import pallas as pl
from jax.experimental.pallas import tpu as pltpu
from jax.sharding import PartitionSpec as P

SHARES = (1, 2, 3, 2)
PRELOADED = 2
COST = 6 * 10**9
BF16 = jnp.bfloat16
F32 = jnp.float32
ANY = pl.BlockSpec(memory_space=pl.ANY)
VMEM = pl.BlockSpec(memory_space=pltpu.VMEM)


def dot(a, b):
    return jnp.dot(a, b, preferred_element_type=F32)


def in_vmem(*shape, dtype=BF16):
    return pltpu.VMEM(shape, dtype)


def here(value):
    return pltpu.with_memory_space_constraint(value, pltpu.VMEM)


def in_hbm(value):
    return pltpu.with_memory_space_constraint(value, pltpu.HBM)


def call(kernel, name, in_specs, out_shape, scratch, args, after=(), flops=COST, limit=8 * 2**20):
    count = len(in_specs)

    def body(*refs):
        kernel(*refs[:count], *refs[count + len(after) :])

    return pl.pallas_call(
        body,
        name=name,
        in_specs=[*in_specs, *[ANY] * len(after)],
        out_specs=[VMEM] * len(out_shape),
        out_shape=out_shape,
        scratch_shapes=scratch,
        compiler_params=pltpu.CompilerParams(vmem_limit_bytes=limit),
        cost_estimate=pl.CostEstimate(flops=flops, bytes_accessed=0, transcendentals=0),
    )(*args, *after)


def partner(value, axis, mask):
    pairs = [(source, source ^ mask) for source in range(lax.axis_size(axis))]
    return lax.ppermute(value, axis, pairs)


def leaf_kernel(excite, leaves, blocks, index, first, rest, *refs):
    count = PRELOADED
    nexts = refs[:count]
    excite_v, leaves_v, blocks_v, index_s, coeff, sems = refs[count:]
    slots, rank = leaves.shape[0], leaves.shape[1]
    columns, width = excite.shape[2], first.shape[1]
    listing = pltpu.make_async_copy(index, index_s, sems.at[0])
    listing.start()
    loads = []
    for s in range(slots):
        a = pltpu.make_async_copy(leaves.at[s], leaves_v.at[s], sems.at[1 + s])
        b = pltpu.make_async_copy(excite.at[s], excite_v.at[s], sems.at[3 + s])
        a.start()
        b.start()
        loads.append((a, b))
    listing.wait()
    weights, later = [], []
    for s in range(slots):
        c = pltpu.make_async_copy(blocks.at[0, index_s[s, 0]], blocks_v.at[s], sems.at[5 + s])
        c.start()
        weights.append(c)
    for level in range(1, 1 + count):
        for s in range(slots):
            c = pltpu.make_async_copy(
                blocks.at[level, index_s[s, level]], nexts[level - 1].at[s], sems.at[5 + 2 * level + s]
            )
            c.start()
            later.append(c)
    for s in range(slots):
        for load in loads[s]:
            load.wait()
        coeff[s * rank : (s + 1) * rank, :] = dot(leaves_v[s], excite_v[s]).astype(BF16)
    for s in range(slots):
        weights[s].wait()
        out = dot(blocks_v[s], coeff[...]).astype(BF16)
        if s == 0:
            first[...] = out[:, :width]
            rest[:, : columns - width] = out[:, width:]
        else:
            rest[:, s * columns - width : (s + 1) * columns - width] = out
    for c in later:
        c.wait()


def prefetch_kernel(blocks, basis, index, *refs):
    count = blocks.shape[0] - 1 - PRELOADED
    outs, basis_v, index_s, sems = refs[:count], refs[count], refs[count + 1], refs[count + 2]
    listing = pltpu.make_async_copy(index, index_s, sems.at[0])
    listing.start()
    c = pltpu.make_async_copy(basis, basis_v, sems.at[1 + 2 * count])
    c.start()
    copies = [c]
    listing.wait()
    for at in range(count):
        level = at + 1 + PRELOADED
        for s in range(2):
            c = pltpu.make_async_copy(blocks.at[level, index_s[s, level]], outs[at].at[s], sems.at[1 + 2 * at + s])
            c.start()
            copies.append(c)
    for c in copies:
        c.wait()


def upper_half(bit):
    return (lax.axis_index("box") >> bit) & 1


def mix(weights, own, other, bit, buf, parts, out):
    rank = own.shape[0]
    upper = upper_half(bit)
    buf[pl.ds(pl.multiple_of(upper * rank, rank), rank), :] = own
    buf[pl.ds(pl.multiple_of((1 - upper) * rank, rank), rank), :] = other
    for s, start, stop in parts:
        out[:, start:stop] = dot(weights[s], buf[:, start:stop]).astype(BF16)


def levels_kernel(jobs, *refs):
    count = len(jobs)
    ins, outs, bufs = refs[: 3 * count], refs[3 * count : 4 * count], refs[4 * count :]
    for at, (bit, parts, lanes) in enumerate(jobs):
        own, other, weights = ins[3 * at : 3 * at + 3]
        mix(weights, own[:, lanes], other[:, lanes], bit, bufs[at], parts, outs[at])


def half_dot(weights, s, half, value):
    rank = value.shape[0]
    return dot(weights[s, :, pl.ds(pl.multiple_of(half * rank, 128), rank)], value)


def between_kernel(bit, parts, fold, total, own, weights, *refs):
    refs = list(refs)
    ins = [refs.pop(0) for _ in range(2 * (fold + total))]
    partial = refs.pop(0)
    for s, start, stop in parts:
        partial[:, start:stop] = half_dot(weights, s, upper_half(bit), own[:, start:stop])
    if fold:
        fold_kernel(ins.pop(0), ins.pop(0), refs.pop(0), refs.pop(0))
    if total:
        keep, got = ins.pop(0), ins.pop(0)
        refs.pop(0)[...] = (keep[...] + got[...].astype(F32)).astype(BF16)


def last_kernel(bit, parts, order, partial, other, weights, basis, *refs):
    rows = basis.shape[1] // lax.axis_size("blk")
    me = lax.axis_index("blk")
    for s, start, stop in parts:
        mixed = partial[:, start:stop] + half_dot(weights, s, 1 - upper_half(bit), other[:, start:stop])
        coeff = mixed.astype(BF16)
        for ref, distances in zip(refs, order):
            for at, d in enumerate(distances):
                row = pl.multiple_of((me ^ d) * rows, rows)
                piece = dot(basis[s, pl.ds(row, rows), :], coeff)
                ref[at * rows : (at + 1) * rows, start:stop] = piece.astype(ref.dtype)


def fold_kernel(keep, got, send, rest):
    rows = rest.shape[0]
    rest[...] = keep[:rows] + got[:rows].astype(F32)
    send[...] = (keep[rows:] + got[rows:].astype(F32)).astype(BF16)


def end_kernel(places, counts, *refs):
    refs = list(refs)
    out = refs[-1]
    for place, count in zip(places, counts):
        group = [refs.pop(0) for _ in range(count)]
        for s, column, start, stop in place:
            total = group[0][:, start:stop].astype(F32)
            for piece in group[1:]:
                total = total + piece[:, start:stop].astype(F32)
            out[s, :, column : column + stop - start] = total.astype(BF16)


def on_device(excitation, leaf_basis, transfer, transfer_index, out_basis):
    excite, leaves, blocks, basis = excitation[0], leaf_basis[0], transfer[0], out_basis[0]
    index = transfer_index[0].T
    slots, rank, points = leaves.shape
    levels = blocks.shape[0]
    columns = excite.shape[2]
    n_blk = lax.axis_size("blk")
    rows = basis.shape[1] // n_blk
    nbits = lax.axis_size("box").bit_length() - 1
    bits = [None] + [(level - 1) % nbits for level in range(1, levels)]
    pair = in_vmem(slots, rank, 2 * rank)

    unit = slots * columns // sum(SHARES)
    widths = [unit * share for share in SHARES]
    begins = [sum(widths[:j]) for j in range(len(widths))]
    parts, places = [], []
    for begin, width in zip(begins, widths):
        part, place, lane = [], [], 0
        while lane < width:
            s, column = divmod(begin + lane, columns)
            size = min(width - lane, columns - column)
            part.append((s, lane, lane + size))
            place.append((s, column, lane, lane + size))
            lane += size
        parts.append(part)
        places.append(place)

    first, rest, *weights = call(
        leaf_kernel,
        "leaf",
        [ANY] * 4,
        [in_vmem(rank, widths[0]), in_vmem(rank, slots * columns - widths[0])] + [pair] * PRELOADED,
        [
            in_vmem(*excite.shape),
            in_vmem(*leaves.shape),
            pair,
            pltpu.SMEM(index.shape, jnp.int32),
            in_vmem(2 * rank, columns),
            pltpu.SemaphoreType.DMA((7 + 2 * PRELOADED,)),
        ],
        [in_hbm(excite), in_hbm(leaves), in_hbm(blocks), in_hbm(index)],
        limit=24 * 2**20,
    )
    weights = [None, *weights]

    def cross(level, value):
        return partner(value, "box", 2 ** bits[level])

    near_first, near_rest = cross(1, first), cross(1, rest)

    def step(name, jobs, after=(), flops=COST):
        args = [here(v) for level, j, own, other in jobs for v in (own, other, weights[level])]
        described, sizes = [], []
        for level, j, _, _ in jobs:
            begin = begins[j] - widths[0] if level == 1 and j else 0
            described.append((bits[level], parts[j], slice(begin, begin + widths[j])))
            sizes.append(widths[j])
        return call(
            functools.partial(levels_kernel, described),
            name,
            [VMEM] * len(args),
            [in_vmem(rank, size) for size in sizes],
            [in_vmem(2 * rank, size) for size in sizes],
            args,
            after,
            flops,
        )

    def job1(j):
        return (1, j, rest, near_rest) if j else (1, j, first, near_first)

    coeff2, near2, coeff3, near3 = {}, {}, {}, {}

    def second(j, value):
        coeff2[j] = value
        near2[j] = cross(2, value)

    def third(j, value):
        coeff3[j] = value
        near3[j] = cross(3, value)

    (value,) = step("level1_0", [job1(0)])
    second(0, value)
    (value,) = step("level1_1", [job1(1)], [coeff2[0]])
    second(1, value)
    value, ahead = step("level2_0", [(2, 0, coeff2[0], near2[0]), job1(2)], [coeff2[1]])
    third(0, value)
    second(2, ahead)
    *more, basis_v = call(
        prefetch_kernel,
        "prefetch",
        [ANY] * 3,
        [pair] * (levels - 1 - PRELOADED) + [in_vmem(*basis.shape)],
        [pltpu.SMEM(index.shape, jnp.int32), pltpu.SemaphoreType.DMA((2 * levels,))],
        [in_hbm(blocks), in_hbm(basis), in_hbm(index)],
        [coeff3[0]],
    )
    weights += more
    (value,) = step("level2_1", [(2, 1, coeff2[1], near2[1])], [basis_v])
    third(1, value)

    masks = [1 << b for b in range(n_blk.bit_length() - 1)]

    def halving(j):
        order = masks if j % 2 else masks[::-1]
        pieces = [0]
        for mask in order[::-1]:
            pieces = pieces + [d | mask for d in pieces]
        return order, pieces

    def result(j, count, dtype):
        return in_vmem(count * rows, widths[j], dtype=dtype)

    def tail(j, after, direct, folding=None, totalling=None):
        (coeff4,) = step(f"level3_{j}", [(3, j, coeff3[j], near3[j])], after, flops=0 if j == 1 else COST)
        near4 = cross(4, coeff4)
        outs, extra = [in_vmem(rank, widths[j], dtype=F32)], []
        if folding is not None:
            at, keep, got, count = folding
            extra += [keep, got]
            outs += [result(at, count // 2, BF16), result(at, count // 2, F32)]
        if totalling is not None:
            at, keep, got = totalling
            extra += [keep, got]
            outs += [result(at, 1, BF16)]
        partial, *more = call(
            functools.partial(
                between_kernel, bits[4], parts[j], folding is not None, totalling is not None
            ),
            f"between_{j}",
            [VMEM] * (2 + len(extra)),
            outs,
            [],
            [here(v) for v in (coeff4, weights[4], *extra)],
        )
        if direct:
            order = [[d] for d in range(n_blk)]
        else:
            pieces = halving(j)[1]
            order = [pieces[: n_blk // 2], pieces[n_blk // 2 :]]
        kinds = [F32] + [BF16] * (len(order) - 1)
        out = call(
            functools.partial(last_kernel, bits[4], parts[j], order),
            f"last_{j}",
            [VMEM] * 4,
            [result(j, len(o), kind) for o, kind in zip(order, kinds)],
            [],
            [here(v) for v in (partial, near4, weights[4], basis_v)],
        )
        return out, more

    def begin_sum(j, out):
        keep, send = out
        order = halving(j)[0]
        got, count = partner(send, "blk", order[0]), n_blk // 2
        for mask in order[1:-1]:
            send, keep = call(
                fold_kernel,
                f"fold_{j}_{mask}",
                [VMEM] * 2,
                [result(j, count // 2, BF16), result(j, count // 2, F32)],
                [],
                [here(keep), here(got)],
            )
            got, count = partner(send, "blk", mask), count // 2
        return j, keep, got, count

    def direct_sum(out):
        return [out[0]] + [partner(out[d], "blk", d) for d in range(n_blk - 1, 0, -1)]

    out0, _ = tail(0, [coeff3[1]], False)
    fold0 = begin_sum(0, out0)
    value, ahead = step("level2_2", [(2, 2, coeff2[2], near2[2]), job1(3)], [out0[0]])
    third(2, value)
    second(3, ahead)
    out1, (send0, keep0) = tail(1, [coeff3[2]], False, fold0)
    got0 = partner(send0, "blk", halving(0)[0][-1])
    fold1 = begin_sum(1, out1)
    (value,) = step("level2_3", [(2, 3, coeff2[3], near2[3])], [out1[0]])
    third(3, value)
    out2, (send1, keep1, total0) = tail(2, [coeff3[3]], True, fold1, (0, keep0, got0))
    got1 = partner(send1, "blk", halving(1)[0][-1])
    group2 = direct_sum(out2)
    out3, (total1,) = tail(3, [out2[0]], True, None, (1, keep1, got1))
    group3 = direct_sum(out3)
    groups = [[total0], [total1], group2, group3]
    flat = [here(v) for group in groups for v in group]
    return pl.pallas_call(
        functools.partial(end_kernel, places, [len(group) for group in groups]),
        name="end",
        in_specs=[VMEM] * len(flat),
        out_specs=VMEM,
        out_shape=jax.ShapeDtypeStruct((slots, rows, columns), BF16),
        compiler_params=pltpu.CompilerParams(vmem_limit_bytes=8 * 2**20),
    )(*flat)


def solution(mesh):
    in_specs = (
        P("blk", "box", None, None),
        P("blk", "box", None, None),
        P("blk", None, "box", None, None),
        P("blk", None, "box"),
        P("blk", "box", None, None),
    )
    out_specs = P("box", "blk", None)
    return jax.shard_map(
        on_device, mesh=mesh, in_specs=in_specs, out_specs=out_specs, check_vma=False
    )
```

```python
import functools

import jax
import jax.numpy as jnp
from jax import lax
from jax.experimental import pallas as pl
from jax.experimental.pallas import tpu as pltpu
from jax.sharding import PartitionSpec as P

SHARES = (1, 2, 2, 3)
PRELOADED = 2
COST = 6 * 10**9
BF16 = jnp.bfloat16
F32 = jnp.float32
ANY = pl.BlockSpec(memory_space=pl.ANY)
VMEM = pl.BlockSpec(memory_space=pltpu.VMEM)


def dot(a, b):
    return jnp.dot(a, b, preferred_element_type=F32)


def in_vmem(*shape, dtype=BF16):
    return pltpu.VMEM(shape, dtype)


def here(value):
    return pltpu.with_memory_space_constraint(value, pltpu.VMEM)


def in_hbm(value):
    return pltpu.with_memory_space_constraint(value, pltpu.HBM)


def call(kernel, name, in_specs, out_shape, scratch, args, after=(), flops=COST, limit=8 * 2**20):
    count = len(in_specs)

    def body(*refs):
        kernel(*refs[:count], *refs[count + len(after) :])

    return pl.pallas_call(
        body,
        name=name,
        in_specs=[*in_specs, *[ANY] * len(after)],
        out_specs=[VMEM] * len(out_shape),
        out_shape=out_shape,
        scratch_shapes=scratch,
        compiler_params=pltpu.CompilerParams(vmem_limit_bytes=limit),
        cost_estimate=pl.CostEstimate(flops=flops, bytes_accessed=0, transcendentals=0),
    )(*args, *after)


def partner(value, axis, mask):
    pairs = [(source, source ^ mask) for source in range(lax.axis_size(axis))]
    return lax.ppermute(value, axis, pairs)


def leaf_kernel(excite, leaves, blocks, index, first, rest, *refs):
    count = PRELOADED
    nexts = refs[:count]
    excite_v, leaves_v, blocks_v, index_s, coeff, sems = refs[count:]
    slots, rank = leaves.shape[0], leaves.shape[1]
    columns, width = excite.shape[2], first.shape[1]
    listing = pltpu.make_async_copy(index, index_s, sems.at[0])
    listing.start()
    loads = []
    for s in range(slots):
        a = pltpu.make_async_copy(leaves.at[s], leaves_v.at[s], sems.at[1 + s])
        b = pltpu.make_async_copy(excite.at[s], excite_v.at[s], sems.at[3 + s])
        a.start()
        b.start()
        loads.append((a, b))
    listing.wait()
    weights, later = [], []
    for s in range(slots):
        c = pltpu.make_async_copy(blocks.at[0, index_s[s, 0]], blocks_v.at[s], sems.at[5 + s])
        c.start()
        weights.append(c)
    for level in range(1, 1 + count):
        for s in range(slots):
            c = pltpu.make_async_copy(
                blocks.at[level, index_s[s, level]], nexts[level - 1].at[s], sems.at[5 + 2 * level + s]
            )
            c.start()
            later.append(c)
    for s in range(slots):
        for load in loads[s]:
            load.wait()
        coeff[s * rank : (s + 1) * rank, :] = dot(leaves_v[s], excite_v[s]).astype(BF16)
    for s in range(slots):
        weights[s].wait()
        out = dot(blocks_v[s], coeff[...]).astype(BF16)
        if s == 0:
            first[...] = out[:, :width]
            rest[:, : columns - width] = out[:, width:]
        else:
            rest[:, s * columns - width : (s + 1) * columns - width] = out
    for c in later:
        c.wait()


def prefetch_kernel(blocks, basis, index, *refs):
    count = blocks.shape[0] - 1 - PRELOADED
    outs, basis_v, index_s, sems = refs[:count], refs[count], refs[count + 1], refs[count + 2]
    listing = pltpu.make_async_copy(index, index_s, sems.at[0])
    listing.start()
    c = pltpu.make_async_copy(basis, basis_v, sems.at[1 + 2 * count])
    c.start()
    copies = [c]
    listing.wait()
    for at in range(count):
        level = at + 1 + PRELOADED
        for s in range(2):
            c = pltpu.make_async_copy(blocks.at[level, index_s[s, level]], outs[at].at[s], sems.at[1 + 2 * at + s])
            c.start()
            copies.append(c)
    for c in copies:
        c.wait()


def upper_half(bit):
    return (lax.axis_index("box") >> bit) & 1


def mix(weights, own, other, bit, buf, parts, out):
    rank = own.shape[0]
    upper = upper_half(bit)
    buf[pl.ds(pl.multiple_of(upper * rank, rank), rank), :] = own
    buf[pl.ds(pl.multiple_of((1 - upper) * rank, rank), rank), :] = other
    for s, start, stop in parts:
        out[:, start:stop] = dot(weights[s], buf[:, start:stop]).astype(BF16)


def levels_kernel(jobs, *refs):
    count = len(jobs)
    ins, outs, bufs = refs[: 3 * count], refs[3 * count : 4 * count], refs[4 * count :]
    for at, (bit, parts, lanes) in enumerate(jobs):
        own, other, weights = ins[3 * at : 3 * at + 3]
        mix(weights, own[:, lanes], other[:, lanes], bit, bufs[at], parts, outs[at])


def half_dot(weights, s, half, value):
    rank = value.shape[0]
    return dot(weights[s, :, pl.ds(pl.multiple_of(half * rank, 128), rank)], value)


def between_kernel(bit, parts, fold, total, own, weights, *refs):
    refs = list(refs)
    ins = [refs.pop(0) for _ in range(2 * (fold + total))]
    partial = refs.pop(0)
    for s, start, stop in parts:
        partial[:, start:stop] = half_dot(weights, s, upper_half(bit), own[:, start:stop])
    if fold:
        fold_kernel(ins.pop(0), ins.pop(0), refs.pop(0), refs.pop(0))
    if total:
        keep, got = ins.pop(0), ins.pop(0)
        refs.pop(0)[...] = (keep[...] + got[...].astype(F32)).astype(BF16)


def last_kernel(bit, parts, order, partial, other, weights, basis, *refs):
    rows = basis.shape[1] // lax.axis_size("blk")
    me = lax.axis_index("blk")
    for s, start, stop in parts:
        mixed = partial[:, start:stop] + half_dot(weights, s, 1 - upper_half(bit), other[:, start:stop])
        coeff = mixed.astype(BF16)
        for ref, distances in zip(refs, order):
            for at, d in enumerate(distances):
                row = pl.multiple_of((me ^ d) * rows, rows)
                piece = dot(basis[s, pl.ds(row, rows), :], coeff)
                ref[at * rows : (at + 1) * rows, start:stop] = piece.astype(ref.dtype)


def fold_kernel(keep, got, send, rest):
    rows = rest.shape[0]
    rest[...] = keep[:rows] + got[:rows].astype(F32)
    send[...] = (keep[rows:] + got[rows:].astype(F32)).astype(BF16)


def end_kernel(places, counts, *refs):
    refs = list(refs)
    out = refs[-1]
    for place, count in zip(places, counts):
        group = [refs.pop(0) for _ in range(count)]
        for s, column, start, stop in place:
            total = group[0][:, start:stop].astype(F32)
            for piece in group[1:]:
                total = total + piece[:, start:stop].astype(F32)
            out[s, :, column : column + stop - start] = total.astype(BF16)


def on_device(excitation, leaf_basis, transfer, transfer_index, out_basis):
    excite, leaves, blocks, basis = excitation[0], leaf_basis[0], transfer[0], out_basis[0]
    index = transfer_index[0].T
    slots, rank, points = leaves.shape
    levels = blocks.shape[0]
    columns = excite.shape[2]
    n_blk = lax.axis_size("blk")
    rows = basis.shape[1] // n_blk
    nbits = lax.axis_size("box").bit_length() - 1
    bits = [None] + [(level - 1) % nbits for level in range(1, levels)]
    pair = in_vmem(slots, rank, 2 * rank)

    unit = slots * columns // sum(SHARES)
    widths = [unit * share for share in SHARES]
    begins = [sum(widths[:j]) for j in range(len(widths))]
    parts, places = [], []
    for begin, width in zip(begins, widths):
        part, place, lane = [], [], 0
        while lane < width:
            s, column = divmod(begin + lane, columns)
            size = min(width - lane, columns - column)
            part.append((s, lane, lane + size))
            place.append((s, column, lane, lane + size))
            lane += size
        parts.append(part)
        places.append(place)

    first, rest, *weights = call(
        leaf_kernel,
        "leaf",
        [ANY] * 4,
        [in_vmem(rank, widths[0]), in_vmem(rank, slots * columns - widths[0])] + [pair] * PRELOADED,
        [
            in_vmem(*excite.shape),
            in_vmem(*leaves.shape),
            pair,
            pltpu.SMEM(index.shape, jnp.int32),
            in_vmem(2 * rank, columns),
            pltpu.SemaphoreType.DMA((7 + 2 * PRELOADED,)),
        ],
        [in_hbm(excite), in_hbm(leaves), in_hbm(blocks), in_hbm(index)],
        limit=24 * 2**20,
    )
    weights = [None, *weights]

    def cross(level, value):
        return partner(value, "box", 2 ** bits[level])

    near_first, near_rest = cross(1, first), cross(1, rest)

    def step(name, jobs, after=(), flops=COST):
        args = [here(v) for level, j, own, other in jobs for v in (own, other, weights[level])]
        described, sizes = [], []
        for level, j, _, _ in jobs:
            begin = begins[j] - widths[0] if level == 1 and j else 0
            described.append((bits[level], parts[j], slice(begin, begin + widths[j])))
            sizes.append(widths[j])
        return call(
            functools.partial(levels_kernel, described),
            name,
            [VMEM] * len(args),
            [in_vmem(rank, size) for size in sizes],
            [in_vmem(2 * rank, size) for size in sizes],
            args,
            after,
            flops,
        )

    def job1(j):
        return (1, j, rest, near_rest) if j else (1, j, first, near_first)

    coeff2, near2, coeff3, near3 = {}, {}, {}, {}

    def second(j, value):
        coeff2[j] = value
        near2[j] = cross(2, value)

    def third(j, value):
        coeff3[j] = value
        near3[j] = cross(3, value)

    (value,) = step("level1_0", [job1(0)])
    second(0, value)
    (value,) = step("level1_1", [job1(1)], [coeff2[0]])
    second(1, value)
    value, ahead = step("level2_0", [(2, 0, coeff2[0], near2[0]), job1(2)], [coeff2[1]])
    third(0, value)
    second(2, ahead)
    *more, basis_v = call(
        prefetch_kernel,
        "prefetch",
        [ANY] * 3,
        [pair] * (levels - 1 - PRELOADED) + [in_vmem(*basis.shape)],
        [pltpu.SMEM(index.shape, jnp.int32), pltpu.SemaphoreType.DMA((2 * levels,))],
        [in_hbm(blocks), in_hbm(basis), in_hbm(index)],
        [coeff3[0]],
    )
    weights += more
    (value,) = step("level2_1", [(2, 1, coeff2[1], near2[1])], [basis_v])
    third(1, value)

    masks = [1 << b for b in range(n_blk.bit_length() - 1)]

    def halving(j):
        order = masks if j % 2 else masks[::-1]
        pieces = [0]
        for mask in order[::-1]:
            pieces = pieces + [d | mask for d in pieces]
        return order, pieces

    def result(j, count, dtype):
        return in_vmem(count * rows, widths[j], dtype=dtype)

    def tail(j, after, direct, folding=None, totalling=None):
        (coeff4,) = step(f"level3_{j}", [(3, j, coeff3[j], near3[j])], after, flops=0 if j == 1 else COST)
        near4 = cross(4, coeff4)
        outs, extra = [in_vmem(rank, widths[j], dtype=F32)], []
        if folding is not None:
            at, keep, got, count = folding
            extra += [keep, got]
            outs += [result(at, count // 2, BF16), result(at, count // 2, F32)]
        if totalling is not None:
            at, keep, got = totalling
            extra += [keep, got]
            outs += [result(at, 1, BF16)]
        partial, *more = call(
            functools.partial(
                between_kernel, bits[4], parts[j], folding is not None, totalling is not None
            ),
            f"between_{j}",
            [VMEM] * (2 + len(extra)),
            outs,
            [],
            [here(v) for v in (coeff4, weights[4], *extra)],
        )
        if direct:
            order = [[d] for d in range(n_blk)]
        else:
            pieces = halving(j)[1]
            order = [pieces[: n_blk // 2], pieces[n_blk // 2 :]]
        kinds = [F32] + [BF16] * (len(order) - 1)
        out = call(
            functools.partial(last_kernel, bits[4], parts[j], order),
            f"last_{j}",
            [VMEM] * 4,
            [result(j, len(o), kind) for o, kind in zip(order, kinds)],
            [],
            [here(v) for v in (partial, near4, weights[4], basis_v)],
        )
        return out, more

    def begin_sum(j, out):
        keep, send = out
        order = halving(j)[0]
        got, count = partner(send, "blk", order[0]), n_blk // 2
        for mask in order[1:-1]:
            send, keep = call(
                fold_kernel,
                f"fold_{j}_{mask}",
                [VMEM] * 2,
                [result(j, count // 2, BF16), result(j, count // 2, F32)],
                [],
                [here(keep), here(got)],
            )
            got, count = partner(send, "blk", mask), count // 2
        return j, keep, got, count

    def direct_sum(out):
        return [out[0]] + [partner(out[d], "blk", d) for d in range(n_blk - 1, 0, -1)]

    out0, _ = tail(0, [coeff3[1]], False)
    fold0 = begin_sum(0, out0)
    value, ahead = step("level2_2", [(2, 2, coeff2[2], near2[2]), job1(3)], [out0[0]])
    third(2, value)
    second(3, ahead)
    out1, (send0, keep0) = tail(1, [coeff3[2]], False, fold0)
    got0 = partner(send0, "blk", halving(0)[0][-1])
    fold1 = begin_sum(1, out1)
    (value,) = step("level2_3", [(2, 3, coeff2[3], near2[3])], [out1[0]])
    third(3, value)
    out2, (send1, keep1, total0) = tail(2, [coeff3[3]], True, fold1, (0, keep0, got0))
    got1 = partner(send1, "blk", halving(1)[0][-1])
    group2 = direct_sum(out2)
    out3, (total1,) = tail(3, [out2[0]], True, None, (1, keep1, got1))
    group3 = direct_sum(out3)
    groups = [[total0], [total1], group2, group3]
    flat = [here(v) for group in groups for v in group]
    return pl.pallas_call(
        functools.partial(end_kernel, places, [len(group) for group in groups]),
        name="end",
        in_specs=[VMEM] * len(flat),
        out_specs=VMEM,
        out_shape=jax.ShapeDtypeStruct((slots, rows, columns), BF16),
        compiler_params=pltpu.CompilerParams(vmem_limit_bytes=8 * 2**20),
    )(*flat)


def solution(mesh):
    in_specs = (
        P("blk", "box", None, None),
        P("blk", "box", None, None),
        P("blk", None, "box", None, None),
        P("blk", None, "box"),
        P("blk", "box", None, None),
    )
    out_specs = P("box", "blk", None)
    return jax.shard_map(
        on_device, mesh=mesh, in_specs=in_specs, out_specs=out_specs, check_vma=False
    )
```

```python
import functools

import jax
import jax.numpy as jnp
from jax import lax
from jax.experimental import pallas as pl
from jax.experimental.pallas import tpu as pltpu
from jax.sharding import PartitionSpec as P

SHARES = (1, 2, 2, 2, 1)
GROUPS = ((0, 1), (1, 1), (2, 1), (3, 2))
DIRECT = 2
PRELOADED = 2
COST = 6 * 10**9
BF16 = jnp.bfloat16
F32 = jnp.float32
ANY = pl.BlockSpec(memory_space=pl.ANY)
VMEM = pl.BlockSpec(memory_space=pltpu.VMEM)


def dot(a, b):
    return jnp.dot(a, b, preferred_element_type=F32)


def in_vmem(*shape, dtype=BF16):
    return pltpu.VMEM(shape, dtype)


def here(value):
    return pltpu.with_memory_space_constraint(value, pltpu.VMEM)


def in_hbm(value):
    return pltpu.with_memory_space_constraint(value, pltpu.HBM)


def call(kernel, name, in_specs, out_shape, scratch, args, after=(), flops=COST, limit=8 * 2**20):
    count = len(in_specs)

    def body(*refs):
        kernel(*refs[:count], *refs[count + len(after) :])

    return pl.pallas_call(
        body,
        name=name,
        in_specs=[*in_specs, *[ANY] * len(after)],
        out_specs=[VMEM] * len(out_shape),
        out_shape=out_shape,
        scratch_shapes=scratch,
        compiler_params=pltpu.CompilerParams(vmem_limit_bytes=limit),
        cost_estimate=pl.CostEstimate(flops=flops, bytes_accessed=0, transcendentals=0),
    )(*args, *after)


def partner(value, axis, mask):
    pairs = [(source, source ^ mask) for source in range(lax.axis_size(axis))]
    return lax.ppermute(value, axis, pairs)


def leaf_kernel(excite, leaves, blocks, index, first, rest, *refs):
    count = PRELOADED
    nexts = refs[:count]
    excite_v, leaves_v, blocks_v, index_s, coeff, sems = refs[count:]
    slots, rank = leaves.shape[0], leaves.shape[1]
    columns, width = excite.shape[2], first.shape[1]
    listing = pltpu.make_async_copy(index, index_s, sems.at[0])
    listing.start()
    loads = []
    for s in range(slots):
        a = pltpu.make_async_copy(leaves.at[s], leaves_v.at[s], sems.at[1 + s])
        b = pltpu.make_async_copy(excite.at[s], excite_v.at[s], sems.at[3 + s])
        a.start()
        b.start()
        loads.append((a, b))
    listing.wait()
    weights, later = [], []
    for s in range(slots):
        c = pltpu.make_async_copy(blocks.at[0, index_s[s, 0]], blocks_v.at[s], sems.at[5 + s])
        c.start()
        weights.append(c)
    for level in range(1, 1 + count):
        for s in range(slots):
            c = pltpu.make_async_copy(
                blocks.at[level, index_s[s, level]], nexts[level - 1].at[s], sems.at[5 + 2 * level + s]
            )
            c.start()
            later.append(c)
    for s in range(slots):
        for load in loads[s]:
            load.wait()
        coeff[s * rank : (s + 1) * rank, :] = dot(leaves_v[s], excite_v[s]).astype(BF16)
    for s in range(slots):
        weights[s].wait()
        out = dot(blocks_v[s], coeff[...]).astype(BF16)
        if s == 0:
            first[...] = out[:, :width]
            rest[:, : columns - width] = out[:, width:]
        else:
            rest[:, s * columns - width : (s + 1) * columns - width] = out
    for c in later:
        c.wait()


def prefetch_kernel(blocks, basis, index, *refs):
    count = blocks.shape[0] - 1 - PRELOADED
    outs, basis_v, index_s, sems = refs[:count], refs[count], refs[count + 1], refs[count + 2]
    listing = pltpu.make_async_copy(index, index_s, sems.at[0])
    listing.start()
    c = pltpu.make_async_copy(basis, basis_v, sems.at[1 + 2 * count])
    c.start()
    copies = [c]
    listing.wait()
    for at in range(count):
        level = at + 1 + PRELOADED
        for s in range(2):
            c = pltpu.make_async_copy(blocks.at[level, index_s[s, level]], outs[at].at[s], sems.at[1 + 2 * at + s])
            c.start()
            copies.append(c)
    for c in copies:
        c.wait()


def upper_half(bit):
    return (lax.axis_index("box") >> bit) & 1


def mix(weights, own, other, bit, buf, parts, out):
    rank = own.shape[0]
    upper = upper_half(bit)
    buf[pl.ds(pl.multiple_of(upper * rank, rank), rank), :] = own
    buf[pl.ds(pl.multiple_of((1 - upper) * rank, rank), rank), :] = other
    for s, start, stop in parts:
        out[:, start:stop] = dot(weights[s], buf[:, start:stop]).astype(BF16)


def levels_kernel(jobs, *refs):
    count = len(jobs)
    ins, outs, bufs = refs[: 3 * count], refs[3 * count : 4 * count], refs[4 * count :]
    for at, (bit, parts, lanes) in enumerate(jobs):
        own, other, weights = ins[3 * at : 3 * at + 3]
        mix(weights, own[:, lanes], other[:, lanes], bit, bufs[at], parts, outs[at])


def half_dot(weights, s, half, value):
    rank = value.shape[0]
    return dot(weights[s, :, pl.ds(pl.multiple_of(half * rank, 128), rank)], value)


def between_kernel(bit, parts, fold, total, own, weights, *refs):
    refs = list(refs)
    ins = [refs.pop(0) for _ in range(2 * (fold + total))]
    partial = refs.pop(0)
    for s, start, stop in parts:
        partial[:, start:stop] = half_dot(weights, s, upper_half(bit), own[:, start:stop])
    if fold:
        fold_kernel(ins.pop(0), ins.pop(0), refs.pop(0), refs.pop(0))
    if total:
        keep, got = ins.pop(0), ins.pop(0)
        refs.pop(0)[...] = (keep[...] + got[...].astype(F32)).astype(BF16)


def last_kernel(bit, parts, order, partial, other, weights, basis, *refs):
    rows = basis.shape[1] // lax.axis_size("blk")
    me = lax.axis_index("blk")
    for s, start, stop in parts:
        mixed = partial[:, start:stop] + half_dot(weights, s, 1 - upper_half(bit), other[:, start:stop])
        coeff = mixed.astype(BF16)
        for ref, distances in zip(refs, order):
            for at, d in enumerate(distances):
                row = pl.multiple_of((me ^ d) * rows, rows)
                piece = dot(basis[s, pl.ds(row, rows), :], coeff)
                ref[at * rows : (at + 1) * rows, start:stop] = piece.astype(ref.dtype)


def fold_kernel(keep, got, send, rest):
    rows = rest.shape[0]
    rest[...] = keep[:rows] + got[:rows].astype(F32)
    send[...] = (keep[rows:] + got[rows:].astype(F32)).astype(BF16)


def end_kernel(places, counts, *refs):
    refs = list(refs)
    out = refs[-1]
    for place, count in zip(places, counts):
        group = [refs.pop(0) for _ in range(count)]
        for s, column, start, stop in place:
            total = group[0][:, start:stop].astype(F32)
            for piece in group[1:]:
                total = total + piece[:, start:stop].astype(F32)
            out[s, :, column : column + stop - start] = total.astype(BF16)


def on_device(excitation, leaf_basis, transfer, transfer_index, out_basis):
    excite, leaves, blocks, basis = excitation[0], leaf_basis[0], transfer[0], out_basis[0]
    index = transfer_index[0].T
    slots, rank, points = leaves.shape
    levels = blocks.shape[0]
    columns = excite.shape[2]
    n_blk = lax.axis_size("blk")
    rows = basis.shape[1] // n_blk
    nbits = lax.axis_size("box").bit_length() - 1
    bits = [None] + [(level - 1) % nbits for level in range(1, levels)]
    pair = in_vmem(slots, rank, 2 * rank)

    unit = slots * columns // sum(SHARES)
    widths = [unit * share for share in SHARES]
    begins = [sum(widths[:j]) for j in range(len(widths))]
    parts, places = [], []
    for begin, width in zip(begins, widths):
        part, place, lane = [], [], 0
        while lane < width:
            s, column = divmod(begin + lane, columns)
            size = min(width - lane, columns - column)
            part.append((s, lane, lane + size))
            place.append((s, column, lane, lane + size))
            lane += size
        parts.append(part)
        places.append(place)

    first, rest, *weights = call(
        leaf_kernel,
        "leaf",
        [ANY] * 4,
        [in_vmem(rank, widths[0]), in_vmem(rank, slots * columns - widths[0])] + [pair] * PRELOADED,
        [
            in_vmem(*excite.shape),
            in_vmem(*leaves.shape),
            pair,
            pltpu.SMEM(index.shape, jnp.int32),
            in_vmem(2 * rank, columns),
            pltpu.SemaphoreType.DMA((7 + 2 * PRELOADED,)),
        ],
        [in_hbm(excite), in_hbm(leaves), in_hbm(blocks), in_hbm(index)],
        limit=24 * 2**20,
    )
    weights = [None, *weights]

    def cross(level, value):
        return partner(value, "box", 2 ** bits[level])

    near_first, near_rest = cross(1, first), cross(1, rest)

    def step(name, jobs, after=(), flops=COST):
        args = [here(v) for level, _, _, own, other, _ in jobs for v in (own, other, weights[level])]
        described, sizes = [], []
        for level, j, many, _, _, begin in jobs:
            part, size = spans(j, many)
            described.append((bits[level], part, slice(begin, begin + size)))
            sizes.append(size)
        return call(
            functools.partial(levels_kernel, described),
            name,
            [VMEM] * len(args),
            [in_vmem(rank, size) for size in sizes],
            [in_vmem(2 * rank, size) for size in sizes],
            args,
            after,
            flops,
        )

    def spans(j, many):
        part, lane = [], 0
        for at in range(j, j + many):
            part += [(s, lane + start, lane + stop) for s, start, stop in parts[at]]
            lane += widths[at]
        return part, lane

    def job1(group):
        j, many = group
        if j == 0:
            return (1, j, many, first, near_first, 0)
        return (1, j, many, rest, near_rest, begins[j] - widths[0])

    def job2(j):
        (start, many), own, other = next(
            (group, own, other) for group, own, other in sent if group[0] <= j < sum(group)
        )
        return (2, j, 1, own, other, begins[j] - begins[start])

    coeff3, near3 = {}, {}

    sent = []

    def second(group, value):
        sent.append((group, value, cross(2, value)))

    def third(j, value):
        coeff3[j] = value
        near3[j] = cross(3, value)

    (value,) = step("level1_0", [job1(GROUPS[0])])
    second(GROUPS[0], value)
    (value,) = step("level1_1", [job1(GROUPS[1])], [value])
    second(GROUPS[1], value)
    value, ahead = step("level2_0", [job2(0), job1(GROUPS[2])], [value])
    third(0, value)
    second(GROUPS[2], ahead)
    *more, basis_v = call(
        prefetch_kernel,
        "prefetch",
        [ANY] * 3,
        [pair] * (levels - 1 - PRELOADED) + [in_vmem(*basis.shape)],
        [pltpu.SMEM(index.shape, jnp.int32), pltpu.SemaphoreType.DMA((2 * levels,))],
        [in_hbm(blocks), in_hbm(basis), in_hbm(index)],
        [coeff3[0]],
    )
    weights += more
    (value,) = step("level2_1", [job2(1)], [basis_v])
    third(1, value)

    masks = [1 << b for b in range(n_blk.bit_length() - 1)]

    def halving(j):
        order = masks if j % 2 else masks[::-1]
        pieces = [0]
        for mask in order[::-1]:
            pieces = pieces + [d | mask for d in pieces]
        return order, pieces

    def result(j, count, dtype):
        return in_vmem(count * rows, widths[j], dtype=dtype)

    def tail(j, after, direct, folding=None, totalling=None):
        (coeff4,) = step(f"level3_{j}", [(3, j, 1, coeff3[j], near3[j], 0)], after)
        near4 = cross(4, coeff4)
        outs, extra = [in_vmem(rank, widths[j], dtype=F32)], []
        if folding is not None:
            at, keep, got, count = folding
            extra += [keep, got]
            outs += [result(at, count // 2, BF16), result(at, count // 2, F32)]
        if totalling is not None:
            at, keep, got = totalling
            extra += [keep, got]
            outs += [result(at, 1, BF16)]
        partial, *more = call(
            functools.partial(
                between_kernel, bits[4], parts[j], folding is not None, totalling is not None
            ),
            f"between_{j}",
            [VMEM] * (2 + len(extra)),
            outs,
            [],
            [here(v) for v in (coeff4, weights[4], *extra)],
        )
        if direct:
            order = [[d] for d in range(n_blk)]
        else:
            pieces = halving(j)[1]
            order = [pieces[: n_blk // 2], pieces[n_blk // 2 :]]
        kinds = [F32] + [BF16] * (len(order) - 1)
        out = call(
            functools.partial(last_kernel, bits[4], parts[j], order),
            f"last_{j}",
            [VMEM] * 4,
            [result(j, len(o), kind) for o, kind in zip(order, kinds)],
            [],
            [here(v) for v in (partial, near4, weights[4], basis_v)],
        )
        return out, more

    def begin_sum(j, out):
        keep, send = out
        order = halving(j)[0]
        got, count = partner(send, "blk", order[0]), n_blk // 2
        for mask in order[1:-1]:
            send, keep = call(
                fold_kernel,
                f"fold_{j}_{mask}",
                [VMEM] * 2,
                [result(j, count // 2, BF16), result(j, count // 2, F32)],
                [],
                [here(keep), here(got)],
            )
            got, count = partner(send, "blk", mask), count // 2
        return j, keep, got, count

    def direct_sum(out):
        return [out[0]] + [partner(out[d], "blk", d) for d in range(n_blk - 1, 0, -1)]

    count = len(widths)
    groups = {}
    folding = totalling = out = None
    for j in range(count):
        after = [coeff3[j + 1]] if j + 1 < count else [out[0]]
        out, more = tail(j, after, j >= count - DIRECT, folding, totalling)
        if totalling is not None:
            groups[totalling[0]] = [more.pop()]
        totalling = None
        if folding is not None:
            at, (send, keep) = folding[0], more
            totalling = (at, keep, partner(send, "blk", halving(at)[0][-1]))
        folding = None
        if j < count - DIRECT:
            folding = begin_sum(j, out)
        else:
            groups[j] = direct_sum(out)
        if j + 2 < count:
            group = GROUPS[j + 3] if j + 3 < len(GROUPS) else None
            jobs = [job2(j + 2)] + ([job1(group)] if group else [])
            value, *ahead = step(f"level2_{j + 2}", jobs, [out[0]])
            third(j + 2, value)
            if group:
                second(group, *ahead)
    groups = [groups[j] for j in range(count)]
    flat = [here(v) for group in groups for v in group]
    return pl.pallas_call(
        functools.partial(end_kernel, places, [len(group) for group in groups]),
        name="end",
        in_specs=[VMEM] * len(flat),
        out_specs=VMEM,
        out_shape=jax.ShapeDtypeStruct((slots, rows, columns), BF16),
        compiler_params=pltpu.CompilerParams(vmem_limit_bytes=8 * 2**20),
    )(*flat)


def solution(mesh):
    in_specs = (
        P("blk", "box", None, None),
        P("blk", "box", None, None),
        P("blk", None, "box", None, None),
        P("blk", None, "box"),
        P("blk", "box", None, None),
    )
    out_specs = P("box", "blk", None)
    return jax.shard_map(
        on_device, mesh=mesh, in_specs=in_specs, out_specs=out_specs, check_vma=False
    )
```

```python
import functools

import jax
import jax.numpy as jnp
from jax import lax
from jax.experimental import pallas as pl
from jax.experimental.pallas import tpu as pltpu
from jax.sharding import PartitionSpec as P

SHARES = (1, 2, 3, 2)
PRELOADED = 2
COST = 6 * 10**9
BF16 = jnp.bfloat16
F32 = jnp.float32
ANY = pl.BlockSpec(memory_space=pl.ANY)
VMEM = pl.BlockSpec(memory_space=pltpu.VMEM)


def dot(a, b):
    return jnp.dot(a, b, preferred_element_type=F32)


def in_vmem(*shape, dtype=BF16):
    return pltpu.VMEM(shape, dtype)


def here(value):
    return pltpu.with_memory_space_constraint(value, pltpu.VMEM)


def in_hbm(value):
    return pltpu.with_memory_space_constraint(value, pltpu.HBM)


def call(kernel, name, in_specs, out_shape, scratch, args, after=(), flops=COST, limit=8 * 2**20):
    count = len(in_specs)

    def body(*refs):
        kernel(*refs[:count], *refs[count + len(after) :])

    return pl.pallas_call(
        body,
        name=name,
        in_specs=[*in_specs, *[ANY] * len(after)],
        out_specs=[VMEM] * len(out_shape),
        out_shape=out_shape,
        scratch_shapes=scratch,
        compiler_params=pltpu.CompilerParams(vmem_limit_bytes=limit),
        cost_estimate=pl.CostEstimate(flops=flops, bytes_accessed=0, transcendentals=0),
    )(*args, *after)


def partner(value, axis, mask):
    pairs = [(source, source ^ mask) for source in range(lax.axis_size(axis))]
    return lax.ppermute(value, axis, pairs)


def leaf_kernel(excite, leaves, blocks, index, first, rest, *refs):
    count = PRELOADED
    nexts = refs[:count]
    excite_v, leaves_v, blocks_v, index_s, coeff, sems = refs[count:]
    slots, rank = leaves.shape[0], leaves.shape[1]
    columns, width = excite.shape[2], first.shape[1]
    listing = pltpu.make_async_copy(index, index_s, sems.at[0])
    listing.start()
    loads = []
    for s in range(slots):
        a = pltpu.make_async_copy(leaves.at[s], leaves_v.at[s], sems.at[1 + s])
        b = pltpu.make_async_copy(excite.at[s], excite_v.at[s], sems.at[3 + s])
        a.start()
        b.start()
        loads.append((a, b))
    listing.wait()
    weights, later = [], []
    for s in range(slots):
        c = pltpu.make_async_copy(blocks.at[0, index_s[s, 0]], blocks_v.at[s], sems.at[5 + s])
        c.start()
        weights.append(c)
    for level in range(1, 1 + count):
        for s in range(slots):
            c = pltpu.make_async_copy(
                blocks.at[level, index_s[s, level]], nexts[level - 1].at[s], sems.at[5 + 2 * level + s]
            )
            c.start()
            later.append(c)
    for s in range(slots):
        for load in loads[s]:
            load.wait()
        coeff[s * rank : (s + 1) * rank, :] = dot(leaves_v[s], excite_v[s]).astype(BF16)
    for s in range(slots):
        weights[s].wait()
        out = dot(blocks_v[s], coeff[...]).astype(BF16)
        if s == 0:
            first[...] = out[:, :width]
            rest[:, : columns - width] = out[:, width:]
        else:
            rest[:, s * columns - width : (s + 1) * columns - width] = out
    for c in later:
        c.wait()


def prefetch_kernel(blocks, basis, index, *refs):
    count = blocks.shape[0] - 1 - PRELOADED
    outs, basis_v, index_s, sems = refs[:count], refs[count], refs[count + 1], refs[count + 2]
    listing = pltpu.make_async_copy(index, index_s, sems.at[0])
    listing.start()
    c = pltpu.make_async_copy(basis, basis_v, sems.at[1 + 2 * count])
    c.start()
    copies = [c]
    listing.wait()
    for at in range(count):
        level = at + 1 + PRELOADED
        for s in range(2):
            c = pltpu.make_async_copy(blocks.at[level, index_s[s, level]], outs[at].at[s], sems.at[1 + 2 * at + s])
            c.start()
            copies.append(c)
    for c in copies:
        c.wait()


def upper_half(bit):
    return (lax.axis_index("box") >> bit) & 1


def mix(weights, own, other, bit, buf, parts, out):
    rank = own.shape[0]
    upper = upper_half(bit)
    buf[pl.ds(pl.multiple_of(upper * rank, rank), rank), :] = own
    buf[pl.ds(pl.multiple_of((1 - upper) * rank, rank), rank), :] = other
    for s, start, stop in parts:
        out[:, start:stop] = dot(weights[s], buf[:, start:stop]).astype(BF16)


def levels_kernel(jobs, *refs):
    count = len(jobs)
    ins, outs, bufs = refs[: 3 * count], refs[3 * count : 4 * count], refs[4 * count :]
    for at, (bit, parts, lanes) in enumerate(jobs):
        own, other, weights = ins[3 * at : 3 * at + 3]
        mix(weights, own[:, lanes], other[:, lanes], bit, bufs[at], parts, outs[at])


def half_dot(weights, s, half, value):
    rank = value.shape[0]
    return dot(weights[s, :, pl.ds(pl.multiple_of(half * rank, 128), rank)], value)


def between_kernel(bit, parts, fold, total, own, weights, *refs):
    refs = list(refs)
    ins = [refs.pop(0) for _ in range(2 * (fold + total))]
    partial = refs.pop(0)
    for s, start, stop in parts:
        partial[:, start:stop] = half_dot(weights, s, upper_half(bit), own[:, start:stop])
    if fold:
        fold_kernel(ins.pop(0), ins.pop(0), refs.pop(0), refs.pop(0))
    if total:
        keep, got = ins.pop(0), ins.pop(0)
        refs.pop(0)[...] = (keep[...] + got[...].astype(F32)).astype(BF16)


def last_kernel(bit, parts, order, partial, other, weights, basis, *refs):
    rows = basis.shape[1] // lax.axis_size("blk")
    me = lax.axis_index("blk")
    for s, start, stop in parts:
        mixed = partial[:, start:stop] + half_dot(weights, s, 1 - upper_half(bit), other[:, start:stop])
        coeff = mixed.astype(BF16)
        for ref, distances in zip(refs, order):
            for at, d in enumerate(distances):
                row = pl.multiple_of((me ^ d) * rows, rows)
                piece = dot(basis[s, pl.ds(row, rows), :], coeff)
                ref[at * rows : (at + 1) * rows, start:stop] = piece.astype(ref.dtype)


def fold_kernel(keep, got, send, rest):
    rows = rest.shape[0]
    rest[...] = keep[:rows] + got[:rows].astype(F32)
    send[...] = (keep[rows:] + got[rows:].astype(F32)).astype(BF16)


def sum_kernel(keep, got, total):
    total[...] = (keep[...] + got[...].astype(F32)).astype(BF16)


def end_kernel(places, counts, *refs):
    refs = list(refs)
    out = refs[-1]
    for place, count in zip(places, counts):
        group = [refs.pop(0) for _ in range(count)]
        for s, column, start, stop in place:
            total = group[0][:, start:stop].astype(F32)
            for piece in group[1:]:
                total = total + piece[:, start:stop].astype(F32)
            out[s, :, column : column + stop - start] = total.astype(BF16)


def on_device(excitation, leaf_basis, transfer, transfer_index, out_basis):
    excite, leaves, blocks, basis = excitation[0], leaf_basis[0], transfer[0], out_basis[0]
    index = transfer_index[0].T
    slots, rank, points = leaves.shape
    levels = blocks.shape[0]
    columns = excite.shape[2]
    n_blk = lax.axis_size("blk")
    rows = basis.shape[1] // n_blk
    nbits = lax.axis_size("box").bit_length() - 1
    bits = [None] + [(level - 1) % nbits for level in range(1, levels)]
    pair = in_vmem(slots, rank, 2 * rank)

    unit = slots * columns // sum(SHARES)
    widths = [unit * share for share in SHARES]
    begins = [sum(widths[:j]) for j in range(len(widths))]
    parts, places = [], []
    for begin, width in zip(begins, widths):
        part, place, lane = [], [], 0
        while lane < width:
            s, column = divmod(begin + lane, columns)
            size = min(width - lane, columns - column)
            part.append((s, lane, lane + size))
            place.append((s, column, lane, lane + size))
            lane += size
        parts.append(part)
        places.append(place)

    first, rest, *weights = call(
        leaf_kernel,
        "leaf",
        [ANY] * 4,
        [in_vmem(rank, widths[0]), in_vmem(rank, slots * columns - widths[0])] + [pair] * PRELOADED,
        [
            in_vmem(*excite.shape),
            in_vmem(*leaves.shape),
            pair,
            pltpu.SMEM(index.shape, jnp.int32),
            in_vmem(2 * rank, columns),
            pltpu.SemaphoreType.DMA((7 + 2 * PRELOADED,)),
        ],
        [in_hbm(excite), in_hbm(leaves), in_hbm(blocks), in_hbm(index)],
        limit=24 * 2**20,
    )
    weights = [None, *weights]

    def cross(level, value):
        return partner(value, "box", 2 ** bits[level])

    near_first, near_rest = cross(1, first), cross(1, rest)

    def step(name, jobs, after=(), flops=COST):
        args = [here(v) for level, j, own, other in jobs for v in (own, other, weights[level])]
        described, sizes = [], []
        for level, j, _, _ in jobs:
            begin = begins[j] - widths[0] if level == 1 and j else 0
            described.append((bits[level], parts[j], slice(begin, begin + widths[j])))
            sizes.append(widths[j])
        return call(
            functools.partial(levels_kernel, described),
            name,
            [VMEM] * len(args),
            [in_vmem(rank, size) for size in sizes],
            [in_vmem(2 * rank, size) for size in sizes],
            args,
            after,
            flops,
        )

    def job1(j):
        return (1, j, rest, near_rest) if j else (1, j, first, near_first)

    coeff2, near2, coeff3, near3 = {}, {}, {}, {}

    def second(j, value):
        coeff2[j] = value
        near2[j] = cross(2, value)

    def third(j, value):
        coeff3[j] = value
        near3[j] = cross(3, value)

    (value,) = step("level1_0", [job1(0)])
    second(0, value)
    (value,) = step("level1_1", [job1(1)], [coeff2[0]])
    second(1, value)
    value, ahead = step("level2_0", [(2, 0, coeff2[0], near2[0]), job1(2)], [coeff2[1]])
    third(0, value)
    second(2, ahead)
    *more, basis_v = call(
        prefetch_kernel,
        "prefetch",
        [ANY] * 3,
        [pair] * (levels - 1 - PRELOADED) + [in_vmem(*basis.shape)],
        [pltpu.SMEM(index.shape, jnp.int32), pltpu.SemaphoreType.DMA((2 * levels,))],
        [in_hbm(blocks), in_hbm(basis), in_hbm(index)],
        [coeff3[0]],
    )
    weights += more
    (value,) = step("level2_1", [(2, 1, coeff2[1], near2[1])], [basis_v])
    third(1, value)

    masks = [1 << b for b in range(n_blk.bit_length() - 1)]

    def halving(j):
        order = masks if j % 2 else masks[::-1]
        pieces = [0]
        for mask in order[::-1]:
            pieces = pieces + [d | mask for d in pieces]
        return order, pieces

    def result(j, count, dtype):
        return in_vmem(count * rows, widths[j], dtype=dtype)

    def tail(j, after, direct, folding=None, totalling=None):
        (coeff4,) = step(f"level3_{j}", [(3, j, coeff3[j], near3[j])], after, flops=0 if j == 1 else COST)
        near4 = cross(4, coeff4)
        outs, extra = [in_vmem(rank, widths[j], dtype=F32)], []
        if folding is not None:
            at, keep, got, count = folding
            extra += [keep, got]
            outs += [result(at, count // 2, BF16), result(at, count // 2, F32)]
        if totalling is not None:
            at, keep, got = totalling
            extra += [keep, got]
            outs += [result(at, 1, BF16)]
        partial, *more = call(
            functools.partial(
                between_kernel, bits[4], parts[j], folding is not None, totalling is not None
            ),
            f"between_{j}",
            [VMEM] * (2 + len(extra)),
            outs,
            [],
            [here(v) for v in (coeff4, weights[4], *extra)],
        )
        if direct:
            order = [[d] for d in range(n_blk)]
        else:
            pieces = halving(j)[1]
            order = [pieces[: n_blk // 2], pieces[n_blk // 2 :]]
        kinds = [F32] + [BF16] * (len(order) - 1)
        out = call(
            functools.partial(last_kernel, bits[4], parts[j], order),
            f"last_{j}",
            [VMEM] * 4,
            [result(j, len(o), kind) for o, kind in zip(order, kinds)],
            [],
            [here(v) for v in (partial, near4, weights[4], basis_v)],
        )
        return out, more

    def begin_sum(j, out):
        keep, send = out
        order = halving(j)[0]
        got, count = partner(send, "blk", order[0]), n_blk // 2
        for mask in order[1:-1]:
            send, keep = call(
                fold_kernel,
                f"fold_{j}_{mask}",
                [VMEM] * 2,
                [result(j, count // 2, BF16), result(j, count // 2, F32)],
                [],
                [here(keep), here(got)],
            )
            got, count = partner(send, "blk", mask), count // 2
        return j, keep, got, count

    def direct_sum(out):
        return [out[0]] + [partner(out[d], "blk", d) for d in range(n_blk - 1, 0, -1)]

    out0, _ = tail(0, [coeff3[1]], False)
    fold0 = begin_sum(0, out0)
    value, ahead = step("level2_2", [(2, 2, coeff2[2], near2[2]), job1(3)], [out0[0]])
    third(2, value)
    second(3, ahead)
    out1, (send0, keep0) = tail(1, [coeff3[2]], False, fold0)
    got0 = partner(send0, "blk", halving(0)[0][-1])
    fold1 = begin_sum(1, out1)
    (total0,) = call(
        sum_kernel, "sum_0", [VMEM] * 2, [result(0, 1, BF16)], [], [here(keep0), here(got0)], [out1[0]]
    )
    at, keep, got, count = fold1
    send1, keep1 = call(
        fold_kernel,
        "fold_1",
        [VMEM] * 2,
        [result(1, count // 2, BF16), result(1, count // 2, F32)],
        [],
        [here(keep), here(got)],
        [total0],
    )
    (value,) = step("level2_3", [(2, 3, coeff2[3], near2[3])], [keep1])
    third(3, value)
    out2, _ = tail(2, [coeff3[3]], True, None, None)
    got1 = partner(send1, "blk", halving(1)[0][-1])
    group2 = direct_sum(out2)
    out3, (total1,) = tail(3, [out2[0]], True, None, (1, keep1, got1))
    group3 = direct_sum(out3)
    groups = [[total0], [total1], group2, group3]
    flat = [here(v) for group in groups for v in group]
    return pl.pallas_call(
        functools.partial(end_kernel, places, [len(group) for group in groups]),
        name="end",
        in_specs=[VMEM] * len(flat),
        out_specs=VMEM,
        out_shape=jax.ShapeDtypeStruct((slots, rows, columns), BF16),
        compiler_params=pltpu.CompilerParams(vmem_limit_bytes=8 * 2**20),
    )(*flat)


def solution(mesh):
    in_specs = (
        P("blk", "box", None, None),
        P("blk", "box", None, None),
        P("blk", None, "box", None, None),
        P("blk", None, "box"),
        P("blk", "box", None, None),
    )
    out_specs = P("box", "blk", None)
    return jax.shard_map(
        on_device, mesh=mesh, in_specs=in_specs, out_specs=out_specs, check_vma=False
    )
```

```python
import functools

import jax
import jax.numpy as jnp
from jax import lax
from jax.experimental import pallas as pl
from jax.experimental.pallas import tpu as pltpu
from jax.sharding import PartitionSpec as P

SHARES = (1, 2, 3, 2)
PRELOADED = 2
COST = 6 * 10**9
BF16 = jnp.bfloat16
F32 = jnp.float32
ANY = pl.BlockSpec(memory_space=pl.ANY)
VMEM = pl.BlockSpec(memory_space=pltpu.VMEM)


def dot(a, b):
    return jnp.dot(a, b, preferred_element_type=F32)


def in_vmem(*shape, dtype=BF16):
    return pltpu.VMEM(shape, dtype)


def here(value):
    return pltpu.with_memory_space_constraint(value, pltpu.VMEM)


def in_hbm(value):
    return pltpu.with_memory_space_constraint(value, pltpu.HBM)


def call(kernel, name, in_specs, out_shape, scratch, args, after=(), flops=COST, limit=8 * 2**20):
    count = len(in_specs)

    def body(*refs):
        kernel(*refs[:count], *refs[count + len(after) :])

    return pl.pallas_call(
        body,
        name=name,
        in_specs=[*in_specs, *[ANY] * len(after)],
        out_specs=[VMEM] * len(out_shape),
        out_shape=out_shape,
        scratch_shapes=scratch,
        compiler_params=pltpu.CompilerParams(vmem_limit_bytes=limit),
        cost_estimate=pl.CostEstimate(flops=flops, bytes_accessed=0, transcendentals=0),
    )(*args, *after)


def partner(value, axis, mask):
    pairs = [(source, source ^ mask) for source in range(lax.axis_size(axis))]
    return lax.ppermute(value, axis, pairs)


def leaf_kernel(excite, leaves, blocks, index, first, rest, *refs):
    count = PRELOADED
    nexts = refs[:count]
    excite_v, leaves_v, blocks_v, index_s, coeff, sems = refs[count:]
    slots, rank = leaves.shape[0], leaves.shape[1]
    columns, width = excite.shape[2], first.shape[1]
    listing = pltpu.make_async_copy(index, index_s, sems.at[0])
    listing.start()
    loads = []
    for s in range(slots):
        a = pltpu.make_async_copy(leaves.at[s], leaves_v.at[s], sems.at[1 + s])
        b = pltpu.make_async_copy(excite.at[s], excite_v.at[s], sems.at[3 + s])
        a.start()
        b.start()
        loads.append((a, b))
    listing.wait()
    weights, later = [], []
    for s in range(slots):
        c = pltpu.make_async_copy(blocks.at[0, index_s[s, 0]], blocks_v.at[s], sems.at[5 + s])
        c.start()
        weights.append(c)
    for level in range(1, 1 + count):
        for s in range(slots):
            c = pltpu.make_async_copy(
                blocks.at[level, index_s[s, level]], nexts[level - 1].at[s], sems.at[5 + 2 * level + s]
            )
            c.start()
            later.append(c)
    for s in range(slots):
        for load in loads[s]:
            load.wait()
        coeff[s * rank : (s + 1) * rank, :] = dot(leaves_v[s], excite_v[s]).astype(BF16)
    for s in range(slots):
        weights[s].wait()
        out = dot(blocks_v[s], coeff[...]).astype(BF16)
        if s == 0:
            first[...] = out[:, :width]
            rest[:, : columns - width] = out[:, width:]
        else:
            rest[:, s * columns - width : (s + 1) * columns - width] = out
    for c in later:
        c.wait()


def prefetch_kernel(blocks, basis, index, *refs):
    count = blocks.shape[0] - 1 - PRELOADED
    outs, basis_v, index_s, sems = refs[:count], refs[count], refs[count + 1], refs[count + 2]
    listing = pltpu.make_async_copy(index, index_s, sems.at[0])
    listing.start()
    c = pltpu.make_async_copy(basis, basis_v, sems.at[1 + 2 * count])
    c.start()
    copies = [c]
    listing.wait()
    for at in range(count):
        level = at + 1 + PRELOADED
        for s in range(2):
            c = pltpu.make_async_copy(blocks.at[level, index_s[s, level]], outs[at].at[s], sems.at[1 + 2 * at + s])
            c.start()
            copies.append(c)
    for c in copies:
        c.wait()


def upper_half(bit):
    return (lax.axis_index("box") >> bit) & 1


def mix(weights, own, other, bit, buf, parts, out):
    rank = own.shape[0]
    upper = upper_half(bit)
    buf[pl.ds(pl.multiple_of(upper * rank, rank), rank), :] = own
    buf[pl.ds(pl.multiple_of((1 - upper) * rank, rank), rank), :] = other
    for s, start, stop in parts:
        out[:, start:stop] = dot(weights[s], buf[:, start:stop]).astype(BF16)


def levels_kernel(jobs, *refs):
    count = len(jobs)
    ins, outs, bufs = refs[: 3 * count], refs[3 * count : 4 * count], refs[4 * count :]
    for at, (bit, parts, lanes) in enumerate(jobs):
        own, other, weights = ins[3 * at : 3 * at + 3]
        mix(weights, own[:, lanes], other[:, lanes], bit, bufs[at], parts, outs[at])


def half_dot(weights, s, half, value):
    rank = value.shape[0]
    return dot(weights[s, :, pl.ds(pl.multiple_of(half * rank, 128), rank)], value)


def between_kernel(bit, parts, fold, total, own, weights, *refs):
    refs = list(refs)
    ins = [refs.pop(0) for _ in range(2 * (fold + total))]
    partial = refs.pop(0)
    for s, start, stop in parts:
        partial[:, start:stop] = half_dot(weights, s, upper_half(bit), own[:, start:stop])
    if fold:
        fold_kernel(ins.pop(0), ins.pop(0), refs.pop(0), refs.pop(0))
    if total:
        keep, got = ins.pop(0), ins.pop(0)
        refs.pop(0)[...] = (keep[...] + got[...].astype(F32)).astype(BF16)


def last_kernel(bit, parts, order, partial, other, weights, basis, *refs):
    rows = basis.shape[1] // lax.axis_size("blk")
    me = lax.axis_index("blk")
    for s, start, stop in parts:
        mixed = partial[:, start:stop] + half_dot(weights, s, 1 - upper_half(bit), other[:, start:stop])
        coeff = mixed.astype(BF16)
        for ref, distances in zip(refs, order):
            for at, d in enumerate(distances):
                row = pl.multiple_of((me ^ d) * rows, rows)
                piece = dot(basis[s, pl.ds(row, rows), :], coeff)
                ref[at * rows : (at + 1) * rows, start:stop] = piece.astype(ref.dtype)


def fold_kernel(keep, got, send, rest):
    rows = rest.shape[0]
    rest[...] = keep[:rows] + got[:rows].astype(F32)
    send[...] = (keep[rows:] + got[rows:].astype(F32)).astype(BF16)


def sum_kernel(keep, got, total):
    total[...] = (keep[...] + got[...].astype(F32)).astype(BF16)


def end_kernel(places, counts, *refs):
    refs = list(refs)
    out = refs[-1]
    for place, count in zip(places, counts):
        group = [refs.pop(0) for _ in range(count)]
        for s, column, start, stop in place:
            total = group[0][:, start:stop].astype(F32)
            for piece in group[1:]:
                total = total + piece[:, start:stop].astype(F32)
            out[s, :, column : column + stop - start] = total.astype(BF16)


def on_device(excitation, leaf_basis, transfer, transfer_index, out_basis):
    excite, leaves, blocks, basis = excitation[0], leaf_basis[0], transfer[0], out_basis[0]
    index = transfer_index[0].T
    slots, rank, points = leaves.shape
    levels = blocks.shape[0]
    columns = excite.shape[2]
    n_blk = lax.axis_size("blk")
    rows = basis.shape[1] // n_blk
    nbits = lax.axis_size("box").bit_length() - 1
    bits = [None] + [(level - 1) % nbits for level in range(1, levels)]
    pair = in_vmem(slots, rank, 2 * rank)

    unit = slots * columns // sum(SHARES)
    widths = [unit * share for share in SHARES]
    begins = [sum(widths[:j]) for j in range(len(widths))]
    parts, places = [], []
    for begin, width in zip(begins, widths):
        part, place, lane = [], [], 0
        while lane < width:
            s, column = divmod(begin + lane, columns)
            size = min(width - lane, columns - column)
            part.append((s, lane, lane + size))
            place.append((s, column, lane, lane + size))
            lane += size
        parts.append(part)
        places.append(place)

    first, rest, *weights = call(
        leaf_kernel,
        "leaf",
        [ANY] * 4,
        [in_vmem(rank, widths[0]), in_vmem(rank, slots * columns - widths[0])] + [pair] * PRELOADED,
        [
            in_vmem(*excite.shape),
            in_vmem(*leaves.shape),
            pair,
            pltpu.SMEM(index.shape, jnp.int32),
            in_vmem(2 * rank, columns),
            pltpu.SemaphoreType.DMA((7 + 2 * PRELOADED,)),
        ],
        [in_hbm(excite), in_hbm(leaves), in_hbm(blocks), in_hbm(index)],
        limit=24 * 2**20,
    )
    weights = [None, *weights]

    def cross(level, value):
        return partner(value, "box", 2 ** bits[level])

    near_first, near_rest = cross(1, first), cross(1, rest)

    def step(name, jobs, after=(), flops=COST):
        args = [here(v) for level, j, own, other in jobs for v in (own, other, weights[level])]
        described, sizes = [], []
        for level, j, _, _ in jobs:
            begin = begins[j] - widths[0] if level == 1 and j else 0
            described.append((bits[level], parts[j], slice(begin, begin + widths[j])))
            sizes.append(widths[j])
        return call(
            functools.partial(levels_kernel, described),
            name,
            [VMEM] * len(args),
            [in_vmem(rank, size) for size in sizes],
            [in_vmem(2 * rank, size) for size in sizes],
            args,
            after,
            flops,
        )

    def job1(j):
        return (1, j, rest, near_rest) if j else (1, j, first, near_first)

    coeff2, near2, coeff3, near3 = {}, {}, {}, {}

    def second(j, value):
        coeff2[j] = value
        near2[j] = cross(2, value)

    def third(j, value):
        coeff3[j] = value
        near3[j] = cross(3, value)

    (value,) = step("level1_0", [job1(0)])
    second(0, value)
    (value,) = step("level1_1", [job1(1)], [coeff2[0]])
    second(1, value)
    value, ahead = step("level2_0", [(2, 0, coeff2[0], near2[0]), job1(2)], [coeff2[1]])
    third(0, value)
    second(2, ahead)
    *more, basis_v = call(
        prefetch_kernel,
        "prefetch",
        [ANY] * 3,
        [pair] * (levels - 1 - PRELOADED) + [in_vmem(*basis.shape)],
        [pltpu.SMEM(index.shape, jnp.int32), pltpu.SemaphoreType.DMA((2 * levels,))],
        [in_hbm(blocks), in_hbm(basis), in_hbm(index)],
        [coeff3[0]],
    )
    weights += more
    (value,) = step("level2_1", [(2, 1, coeff2[1], near2[1])], [basis_v])
    third(1, value)

    masks = [1 << b for b in range(n_blk.bit_length() - 1)]

    def halving(j):
        order = masks if j % 2 else masks[::-1]
        pieces = [0]
        for mask in order[::-1]:
            pieces = pieces + [d | mask for d in pieces]
        return order, pieces

    def result(j, count, dtype):
        return in_vmem(count * rows, widths[j], dtype=dtype)

    def tail(j, after, direct, folding=None, totalling=None):
        (coeff4,) = step(f"level3_{j}", [(3, j, coeff3[j], near3[j])], after, flops=0 if j == 1 else COST)
        near4 = cross(4, coeff4)
        outs, extra = [in_vmem(rank, widths[j], dtype=F32)], []
        if folding is not None:
            at, keep, got, count = folding
            extra += [keep, got]
            outs += [result(at, count // 2, BF16), result(at, count // 2, F32)]
        if totalling is not None:
            at, keep, got = totalling
            extra += [keep, got]
            outs += [result(at, 1, BF16)]
        partial, *more = call(
            functools.partial(
                between_kernel, bits[4], parts[j], folding is not None, totalling is not None
            ),
            f"between_{j}",
            [VMEM] * (2 + len(extra)),
            outs,
            [],
            [here(v) for v in (coeff4, weights[4], *extra)],
        )
        if direct:
            order = [[d] for d in range(n_blk)]
        else:
            pieces = halving(j)[1]
            order = [pieces[: n_blk // 2], pieces[n_blk // 2 :]]
        kinds = [F32] + [BF16] * (len(order) - 1)
        out = call(
            functools.partial(last_kernel, bits[4], parts[j], order),
            f"last_{j}",
            [VMEM] * 4,
            [result(j, len(o), kind) for o, kind in zip(order, kinds)],
            [],
            [here(v) for v in (partial, near4, weights[4], basis_v)],
        )
        return out, more

    def begin_sum(j, out):
        keep, send = out
        order = halving(j)[0]
        got, count = partner(send, "blk", order[0]), n_blk // 2
        for mask in order[1:-1]:
            send, keep = call(
                fold_kernel,
                f"fold_{j}_{mask}",
                [VMEM] * 2,
                [result(j, count // 2, BF16), result(j, count // 2, F32)],
                [],
                [here(keep), here(got)],
            )
            got, count = partner(send, "blk", mask), count // 2
        return j, keep, got, count

    def direct_sum(out):
        return [out[0]] + [partner(out[d], "blk", d) for d in range(n_blk - 1, 0, -1)]

    out0, _ = tail(0, [coeff3[1]], False)
    fold0 = begin_sum(0, out0)
    (value,) = step("level2_2", [(2, 2, coeff2[2], near2[2])], [out0[0]])
    third(2, value)
    out1, (send0, keep0) = tail(1, [coeff3[2]], False, fold0)
    got0 = partner(send0, "blk", halving(0)[0][-1])
    fold1 = begin_sum(1, out1)
    (value,) = step("level1_3", [job1(3)], [out1[0]])
    second(3, value)
    (total0,) = call(
        sum_kernel, "sum_0", [VMEM] * 2, [result(0, 1, BF16)], [], [here(keep0), here(got0)], [coeff2[3]]
    )
    at, keep, got, count = fold1
    send1, keep1 = call(
        fold_kernel,
        "fold_1",
        [VMEM] * 2,
        [result(1, count // 2, BF16), result(1, count // 2, F32)],
        [],
        [here(keep), here(got)],
        [total0],
    )
    (value,) = step("level2_3", [(2, 3, coeff2[3], near2[3])], [total0])
    third(3, value)
    out2, _ = tail(2, [coeff3[3]], True, None, None)
    got1 = partner(send1, "blk", halving(1)[0][-1])
    group2 = direct_sum(out2)
    out3, (total1,) = tail(3, [out2[0]], True, None, (1, keep1, got1))
    group3 = direct_sum(out3)
    groups = [[total0], [total1], group2, group3]
    flat = [here(v) for group in groups for v in group]
    return pl.pallas_call(
        functools.partial(end_kernel, places, [len(group) for group in groups]),
        name="end",
        in_specs=[VMEM] * len(flat),
        out_specs=VMEM,
        out_shape=jax.ShapeDtypeStruct((slots, rows, columns), BF16),
        compiler_params=pltpu.CompilerParams(vmem_limit_bytes=8 * 2**20),
    )(*flat)


def solution(mesh):
    in_specs = (
        P("blk", "box", None, None),
        P("blk", "box", None, None),
        P("blk", None, "box", None, None),
        P("blk", None, "box"),
        P("blk", "box", None, None),
    )
    out_specs = P("box", "blk", None)
    return jax.shard_map(
        on_device, mesh=mesh, in_specs=in_specs, out_specs=out_specs, check_vma=False
    )
```

```python
import functools

import jax
import jax.numpy as jnp
from jax import lax
from jax.experimental import pallas as pl
from jax.experimental.pallas import tpu as pltpu
from jax.sharding import PartitionSpec as P

SHARES = (1, 2, 3, 2)
PRELOADED = 2
COST = 6 * 10**9
BF16 = jnp.bfloat16
F32 = jnp.float32
ANY = pl.BlockSpec(memory_space=pl.ANY)
VMEM = pl.BlockSpec(memory_space=pltpu.VMEM)


def dot(a, b):
    return jnp.dot(a, b, preferred_element_type=F32)


def in_vmem(*shape, dtype=BF16):
    return pltpu.VMEM(shape, dtype)


def here(value):
    return pltpu.with_memory_space_constraint(value, pltpu.VMEM)


def in_hbm(value):
    return pltpu.with_memory_space_constraint(value, pltpu.HBM)


def call(kernel, name, in_specs, out_shape, scratch, args, after=(), flops=COST, limit=8 * 2**20):
    count = len(in_specs)

    def body(*refs):
        kernel(*refs[:count], *refs[count + len(after) :])

    return pl.pallas_call(
        body,
        name=name,
        in_specs=[*in_specs, *[ANY] * len(after)],
        out_specs=[VMEM] * len(out_shape),
        out_shape=out_shape,
        scratch_shapes=scratch,
        compiler_params=pltpu.CompilerParams(vmem_limit_bytes=limit),
        cost_estimate=pl.CostEstimate(flops=flops, bytes_accessed=0, transcendentals=0),
    )(*args, *after)


def partner(value, axis, mask):
    pairs = [(source, source ^ mask) for source in range(lax.axis_size(axis))]
    return lax.ppermute(value, axis, pairs)


def leaf_kernel(excite, leaves, blocks, index, first, rest, *refs):
    count = PRELOADED
    nexts = refs[:count]
    excite_v, leaves_v, blocks_v, index_s, coeff, sems = refs[count:]
    slots, rank = leaves.shape[0], leaves.shape[1]
    columns, width = excite.shape[2], first.shape[1]
    listing = pltpu.make_async_copy(index, index_s, sems.at[0])
    listing.start()
    loads = []
    for s in range(slots):
        a = pltpu.make_async_copy(leaves.at[s], leaves_v.at[s], sems.at[1 + s])
        b = pltpu.make_async_copy(excite.at[s], excite_v.at[s], sems.at[3 + s])
        a.start()
        b.start()
        loads.append((a, b))
    listing.wait()
    weights, later = [], []
    for s in range(slots):
        c = pltpu.make_async_copy(blocks.at[0, index_s[s, 0]], blocks_v.at[s], sems.at[5 + s])
        c.start()
        weights.append(c)
    for level in range(1, 1 + count):
        for s in range(slots):
            c = pltpu.make_async_copy(
                blocks.at[level, index_s[s, level]], nexts[level - 1].at[s], sems.at[5 + 2 * level + s]
            )
            c.start()
            later.append(c)
    for s in range(slots):
        for load in loads[s]:
            load.wait()
        coeff[s * rank : (s + 1) * rank, :] = dot(leaves_v[s], excite_v[s]).astype(BF16)
    for s in range(slots):
        weights[s].wait()
        out = dot(blocks_v[s], coeff[...]).astype(BF16)
        if s == 0:
            first[...] = out[:, :width]
            rest[:, : columns - width] = out[:, width:]
        else:
            rest[:, s * columns - width : (s + 1) * columns - width] = out
    for c in later:
        c.wait()


def prefetch_kernel(blocks, basis, index, *refs):
    count = blocks.shape[0] - 1 - PRELOADED
    outs, basis_v, index_s, sems = refs[:count], refs[count], refs[count + 1], refs[count + 2]
    listing = pltpu.make_async_copy(index, index_s, sems.at[0])
    listing.start()
    c = pltpu.make_async_copy(basis, basis_v, sems.at[1 + 2 * count])
    c.start()
    copies = [c]
    listing.wait()
    for at in range(count):
        level = at + 1 + PRELOADED
        for s in range(2):
            c = pltpu.make_async_copy(blocks.at[level, index_s[s, level]], outs[at].at[s], sems.at[1 + 2 * at + s])
            c.start()
            copies.append(c)
    for c in copies:
        c.wait()


def upper_half(bit):
    return (lax.axis_index("box") >> bit) & 1


def mix(weights, own, other, bit, buf, parts, out):
    rank = own.shape[0]
    upper = upper_half(bit)
    buf[pl.ds(pl.multiple_of(upper * rank, rank), rank), :] = own
    buf[pl.ds(pl.multiple_of((1 - upper) * rank, rank), rank), :] = other
    for s, start, stop in parts:
        out[:, start:stop] = dot(weights[s], buf[:, start:stop]).astype(BF16)


def levels_kernel(jobs, *refs):
    count = len(jobs)
    ins, outs, bufs = refs[: 3 * count], refs[3 * count : 4 * count], refs[4 * count :]
    for at, (bit, parts, lanes) in enumerate(jobs):
        own, other, weights = ins[3 * at : 3 * at + 3]
        mix(weights, own[:, lanes], other[:, lanes], bit, bufs[at], parts, outs[at])


def half_dot(weights, s, half, value):
    rank = value.shape[0]
    return dot(weights[s, :, pl.ds(pl.multiple_of(half * rank, 128), rank)], value)


def between_kernel(bit, parts, fold, total, own, weights, *refs):
    refs = list(refs)
    ins = [refs.pop(0) for _ in range(2 * (fold + total))]
    partial = refs.pop(0)
    for s, start, stop in parts:
        partial[:, start:stop] = half_dot(weights, s, upper_half(bit), own[:, start:stop])
    if fold:
        fold_kernel(ins.pop(0), ins.pop(0), refs.pop(0), refs.pop(0))
    if total:
        keep, got = ins.pop(0), ins.pop(0)
        refs.pop(0)[...] = (keep[...] + got[...].astype(F32)).astype(BF16)


def last_kernel(bit, parts, order, partial, other, weights, basis, *refs):
    rows = basis.shape[1] // lax.axis_size("blk")
    me = lax.axis_index("blk")
    for s, start, stop in parts:
        mixed = partial[:, start:stop] + half_dot(weights, s, 1 - upper_half(bit), other[:, start:stop])
        coeff = mixed.astype(BF16)
        for ref, distances in zip(refs, order):
            for at, d in enumerate(distances):
                row = pl.multiple_of((me ^ d) * rows, rows)
                piece = dot(basis[s, pl.ds(row, rows), :], coeff)
                ref[at * rows : (at + 1) * rows, start:stop] = piece.astype(ref.dtype)


def fold_kernel(keep, got, send, rest):
    rows = rest.shape[0]
    rest[...] = keep[:rows] + got[:rows].astype(F32)
    send[...] = (keep[rows:] + got[rows:].astype(F32)).astype(BF16)


def sum_kernel(keep, got, total):
    total[...] = (keep[...] + got[...].astype(F32)).astype(BF16)


def end_kernel(places, counts, *refs):
    refs = list(refs)
    out = refs[-1]
    for place, count in zip(places, counts):
        group = [refs.pop(0) for _ in range(count)]
        for s, column, start, stop in place:
            total = group[0][:, start:stop].astype(F32)
            for piece in group[1:]:
                total = total + piece[:, start:stop].astype(F32)
            out[s, :, column : column + stop - start] = total.astype(BF16)


def on_device(excitation, leaf_basis, transfer, transfer_index, out_basis):
    excite, leaves, blocks, basis = excitation[0], leaf_basis[0], transfer[0], out_basis[0]
    index = transfer_index[0].T
    slots, rank, points = leaves.shape
    levels = blocks.shape[0]
    columns = excite.shape[2]
    n_blk = lax.axis_size("blk")
    rows = basis.shape[1] // n_blk
    nbits = lax.axis_size("box").bit_length() - 1
    bits = [None] + [(level - 1) % nbits for level in range(1, levels)]
    pair = in_vmem(slots, rank, 2 * rank)

    unit = slots * columns // sum(SHARES)
    widths = [unit * share for share in SHARES]
    begins = [sum(widths[:j]) for j in range(len(widths))]
    parts, places = [], []
    for begin, width in zip(begins, widths):
        part, place, lane = [], [], 0
        while lane < width:
            s, column = divmod(begin + lane, columns)
            size = min(width - lane, columns - column)
            part.append((s, lane, lane + size))
            place.append((s, column, lane, lane + size))
            lane += size
        parts.append(part)
        places.append(place)

    first, rest, *weights = call(
        leaf_kernel,
        "leaf",
        [ANY] * 4,
        [in_vmem(rank, widths[0]), in_vmem(rank, slots * columns - widths[0])] + [pair] * PRELOADED,
        [
            in_vmem(*excite.shape),
            in_vmem(*leaves.shape),
            pair,
            pltpu.SMEM(index.shape, jnp.int32),
            in_vmem(2 * rank, columns),
            pltpu.SemaphoreType.DMA((7 + 2 * PRELOADED,)),
        ],
        [in_hbm(excite), in_hbm(leaves), in_hbm(blocks), in_hbm(index)],
        limit=24 * 2**20,
    )
    weights = [None, *weights]

    def cross(level, value):
        return partner(value, "box", 2 ** bits[level])

    near_first, near_rest = cross(1, first), cross(1, rest)

    def step(name, jobs, after=(), flops=COST):
        args = [here(v) for level, j, own, other in jobs for v in (own, other, weights[level])]
        described, sizes = [], []
        for level, j, _, _ in jobs:
            begin = begins[j] - widths[0] if level == 1 and j else 0
            described.append((bits[level], parts[j], slice(begin, begin + widths[j])))
            sizes.append(widths[j])
        return call(
            functools.partial(levels_kernel, described),
            name,
            [VMEM] * len(args),
            [in_vmem(rank, size) for size in sizes],
            [in_vmem(2 * rank, size) for size in sizes],
            args,
            after,
            flops,
        )

    def job1(j):
        return (1, j, rest, near_rest) if j else (1, j, first, near_first)

    coeff2, near2, coeff3, near3 = {}, {}, {}, {}

    def second(j, value):
        coeff2[j] = value
        near2[j] = cross(2, value)

    def third(j, value):
        coeff3[j] = value
        near3[j] = cross(3, value)

    (value,) = step("level1_0", [job1(0)])
    second(0, value)
    (value,) = step("level1_1", [job1(1)], [coeff2[0]])
    second(1, value)
    value, ahead = step("level2_0", [(2, 0, coeff2[0], near2[0]), job1(2)], [coeff2[1]])
    third(0, value)
    second(2, ahead)
    *more, basis_v = call(
        prefetch_kernel,
        "prefetch",
        [ANY] * 3,
        [pair] * (levels - 1 - PRELOADED) + [in_vmem(*basis.shape)],
        [pltpu.SMEM(index.shape, jnp.int32), pltpu.SemaphoreType.DMA((2 * levels,))],
        [in_hbm(blocks), in_hbm(basis), in_hbm(index)],
        [coeff3[0]],
    )
    weights += more
    (value,) = step("level2_1", [(2, 1, coeff2[1], near2[1])], [basis_v])
    third(1, value)

    masks = [1 << b for b in range(n_blk.bit_length() - 1)]

    def halving(j):
        order = masks if j % 2 else masks[::-1]
        pieces = [0]
        for mask in order[::-1]:
            pieces = pieces + [d | mask for d in pieces]
        return order, pieces

    def result(j, count, dtype):
        return in_vmem(count * rows, widths[j], dtype=dtype)

    def tail(j, after, direct, folding=None, totalling=None):
        (coeff4,) = step(f"level3_{j}", [(3, j, coeff3[j], near3[j])], after, flops=0 if j == 1 else COST)
        near4 = cross(4, coeff4)
        outs, extra = [in_vmem(rank, widths[j], dtype=F32)], []
        if folding is not None:
            at, keep, got, count = folding
            extra += [keep, got]
            outs += [result(at, count // 2, BF16), result(at, count // 2, F32)]
        if totalling is not None:
            at, keep, got = totalling
            extra += [keep, got]
            outs += [result(at, 1, BF16)]
        partial, *more = call(
            functools.partial(
                between_kernel, bits[4], parts[j], folding is not None, totalling is not None
            ),
            f"between_{j}",
            [VMEM] * (2 + len(extra)),
            outs,
            [],
            [here(v) for v in (coeff4, weights[4], *extra)],
        )
        if direct:
            order = [[d] for d in range(n_blk)]
        else:
            pieces = halving(j)[1]
            order = [pieces[: n_blk // 2], pieces[n_blk // 2 :]]
        kinds = [F32] + [BF16] * (len(order) - 1)
        out = call(
            functools.partial(last_kernel, bits[4], parts[j], order),
            f"last_{j}",
            [VMEM] * 4,
            [result(j, len(o), kind) for o, kind in zip(order, kinds)],
            [],
            [here(v) for v in (partial, near4, weights[4], basis_v)],
        )
        return out, more

    def begin_sum(j, out):
        keep, send = out
        order = halving(j)[0]
        got, count = partner(send, "blk", order[0]), n_blk // 2
        for mask in order[1:-1]:
            send, keep = call(
                fold_kernel,
                f"fold_{j}_{mask}",
                [VMEM] * 2,
                [result(j, count // 2, BF16), result(j, count // 2, F32)],
                [],
                [here(keep), here(got)],
            )
            got, count = partner(send, "blk", mask), count // 2
        return j, keep, got, count

    def direct_sum(out):
        return [out[0]] + [partner(out[d], "blk", d) for d in range(n_blk - 1, 0, -1)]

    out0, _ = tail(0, [coeff3[1]], False)
    fold0 = begin_sum(0, out0)
    (value,) = step("level2_2", [(2, 2, coeff2[2], near2[2])], [out0[0]])
    third(2, value)
    (value,) = step("level1_3", [job1(3)], [coeff3[2]])
    second(3, value)
    def fold(held, after=()):
        at, keep, got, count = held
        send, keep = call(
            fold_kernel,
            f"fold_{at}",
            [VMEM] * 2,
            [result(at, count // 2, BF16), result(at, count // 2, F32)],
            [],
            [here(keep), here(got)],
            after,
        )
        return keep, partner(send, "blk", halving(at)[0][-1])

    out1, _ = tail(1, [coeff2[3]], False)
    fold1 = begin_sum(1, out1)
    keep0, got0 = fold(fold0, [out1[0]])
    keep1, got1 = fold(fold1, [keep0])
    (value,) = step("level2_3", [(2, 3, coeff2[3], near2[3])], [keep1])
    third(3, value)
    out2, (total0,) = tail(2, [coeff3[3]], True, None, (0, keep0, got0))
    group2 = direct_sum(out2)
    out3, (total1,) = tail(3, [out2[0]], True, None, (1, keep1, got1))
    group3 = direct_sum(out3)
    groups = [[total0], [total1], group2, group3]
    flat = [here(v) for group in groups for v in group]
    return pl.pallas_call(
        functools.partial(end_kernel, places, [len(group) for group in groups]),
        name="end",
        in_specs=[VMEM] * len(flat),
        out_specs=VMEM,
        out_shape=jax.ShapeDtypeStruct((slots, rows, columns), BF16),
        compiler_params=pltpu.CompilerParams(vmem_limit_bytes=8 * 2**20),
    )(*flat)


def solution(mesh):
    in_specs = (
        P("blk", "box", None, None),
        P("blk", "box", None, None),
        P("blk", None, "box", None, None),
        P("blk", None, "box"),
        P("blk", "box", None, None),
    )
    out_specs = P("box", "blk", None)
    return jax.shard_map(
        on_device, mesh=mesh, in_specs=in_specs, out_specs=out_specs, check_vma=False
    )
```

```python
import functools

import jax
import jax.numpy as jnp
from jax import lax
from jax.experimental import pallas as pl
from jax.experimental.pallas import tpu as pltpu
from jax.sharding import PartitionSpec as P

SHARES = (1, 2, 3, 2)
PRELOADED = 2
COST = 6 * 10**9
BF16 = jnp.bfloat16
F32 = jnp.float32
ANY = pl.BlockSpec(memory_space=pl.ANY)
VMEM = pl.BlockSpec(memory_space=pltpu.VMEM)


def dot(a, b):
    return jnp.dot(a, b, preferred_element_type=F32)


def in_vmem(*shape, dtype=BF16):
    return pltpu.VMEM(shape, dtype)


def here(value):
    return pltpu.with_memory_space_constraint(value, pltpu.VMEM)


def in_hbm(value):
    return pltpu.with_memory_space_constraint(value, pltpu.HBM)


def call(kernel, name, in_specs, out_shape, scratch, args, after=(), flops=COST, limit=8 * 2**20):
    count = len(in_specs)

    def body(*refs):
        kernel(*refs[:count], *refs[count + len(after) :])

    return pl.pallas_call(
        body,
        name=name,
        in_specs=[*in_specs, *[ANY] * len(after)],
        out_specs=[VMEM] * len(out_shape),
        out_shape=out_shape,
        scratch_shapes=scratch,
        compiler_params=pltpu.CompilerParams(vmem_limit_bytes=limit),
        cost_estimate=pl.CostEstimate(flops=flops, bytes_accessed=0, transcendentals=0),
    )(*args, *after)


def partner(value, axis, mask):
    pairs = [(source, source ^ mask) for source in range(lax.axis_size(axis))]
    return lax.ppermute(value, axis, pairs)


def leaf_kernel(excite, leaves, blocks, index, first, rest, *refs):
    count = PRELOADED
    nexts = refs[:count]
    excite_v, leaves_v, blocks_v, index_s, coeff, sems = refs[count:]
    slots, rank = leaves.shape[0], leaves.shape[1]
    columns, width = excite.shape[2], first.shape[1]
    listing = pltpu.make_async_copy(index, index_s, sems.at[0])
    listing.start()
    loads = []
    for s in range(slots):
        a = pltpu.make_async_copy(leaves.at[s], leaves_v.at[s], sems.at[1 + s])
        b = pltpu.make_async_copy(excite.at[s], excite_v.at[s], sems.at[3 + s])
        a.start()
        b.start()
        loads.append((a, b))
    listing.wait()
    weights, later = [], []
    for s in range(slots):
        c = pltpu.make_async_copy(blocks.at[0, index_s[s, 0]], blocks_v.at[s], sems.at[5 + s])
        c.start()
        weights.append(c)
    for level in range(1, 1 + count):
        for s in range(slots):
            c = pltpu.make_async_copy(
                blocks.at[level, index_s[s, level]], nexts[level - 1].at[s], sems.at[5 + 2 * level + s]
            )
            c.start()
            later.append(c)
    for s in range(slots):
        for load in loads[s]:
            load.wait()
        coeff[s * rank : (s + 1) * rank, :] = dot(leaves_v[s], excite_v[s]).astype(BF16)
    for s in range(slots):
        weights[s].wait()
        out = dot(blocks_v[s], coeff[...]).astype(BF16)
        if s == 0:
            first[...] = out[:, :width]
            rest[:, : columns - width] = out[:, width:]
        else:
            rest[:, s * columns - width : (s + 1) * columns - width] = out
    for c in later:
        c.wait()


def prefetch_kernel(blocks, basis, index, *refs):
    count = blocks.shape[0] - 1 - PRELOADED
    outs, basis_v, index_s, sems = refs[:count], refs[count], refs[count + 1], refs[count + 2]
    listing = pltpu.make_async_copy(index, index_s, sems.at[0])
    listing.start()
    c = pltpu.make_async_copy(basis, basis_v, sems.at[1 + 2 * count])
    c.start()
    copies = [c]
    listing.wait()
    for at in range(count):
        level = at + 1 + PRELOADED
        for s in range(2):
            c = pltpu.make_async_copy(blocks.at[level, index_s[s, level]], outs[at].at[s], sems.at[1 + 2 * at + s])
            c.start()
            copies.append(c)
    for c in copies:
        c.wait()


def upper_half(bit):
    return (lax.axis_index("box") >> bit) & 1


def mix(weights, own, other, bit, buf, parts, out):
    rank = own.shape[0]
    upper = upper_half(bit)
    buf[pl.ds(pl.multiple_of(upper * rank, rank), rank), :] = own
    buf[pl.ds(pl.multiple_of((1 - upper) * rank, rank), rank), :] = other
    for s, start, stop in parts:
        out[:, start:stop] = dot(weights[s], buf[:, start:stop]).astype(BF16)


def levels_kernel(jobs, *refs):
    count = len(jobs)
    ins, outs, bufs = refs[: 3 * count], refs[3 * count : 4 * count], refs[4 * count :]
    for at, (bit, parts, lanes) in enumerate(jobs):
        own, other, weights = ins[3 * at : 3 * at + 3]
        mix(weights, own[:, lanes], other[:, lanes], bit, bufs[at], parts, outs[at])


def half_dot(weights, s, half, value):
    rank = value.shape[0]
    return dot(weights[s, :, pl.ds(pl.multiple_of(half * rank, 128), rank)], value)


def between_kernel(bit, parts, fold, total, own, weights, *refs):
    refs = list(refs)
    ins = [refs.pop(0) for _ in range(2 * (fold + total))]
    partial = refs.pop(0)
    for s, start, stop in parts:
        partial[:, start:stop] = half_dot(weights, s, upper_half(bit), own[:, start:stop])
    if fold:
        fold_kernel(ins.pop(0), ins.pop(0), refs.pop(0), refs.pop(0))
    if total:
        keep, got = ins.pop(0), ins.pop(0)
        refs.pop(0)[...] = (keep[...] + got[...].astype(F32)).astype(BF16)


def last_kernel(bit, parts, order, partial, other, weights, basis, *refs):
    rows = basis.shape[1] // lax.axis_size("blk")
    me = lax.axis_index("blk")
    for s, start, stop in parts:
        mixed = partial[:, start:stop] + half_dot(weights, s, 1 - upper_half(bit), other[:, start:stop])
        coeff = mixed.astype(BF16)
        for ref, distances in zip(refs, order):
            for at, d in enumerate(distances):
                row = pl.multiple_of((me ^ d) * rows, rows)
                piece = dot(basis[s, pl.ds(row, rows), :], coeff)
                ref[at * rows : (at + 1) * rows, start:stop] = piece.astype(ref.dtype)


def fold_kernel(keep, got, send, rest):
    rows = rest.shape[0]
    rest[...] = keep[:rows] + got[:rows].astype(F32)
    send[...] = (keep[rows:] + got[rows:].astype(F32)).astype(BF16)


def sum_kernel(keep, got, total):
    total[...] = (keep[...] + got[...].astype(F32)).astype(BF16)


def end_kernel(places, counts, *refs):
    refs = list(refs)
    out = refs[-1]
    for place, count in zip(places, counts):
        group = [refs.pop(0) for _ in range(count)]
        for s, column, start, stop in place:
            total = group[0][:, start:stop].astype(F32)
            for piece in group[1:]:
                total = total + piece[:, start:stop].astype(F32)
            out[s, :, column : column + stop - start] = total.astype(BF16)


def on_device(excitation, leaf_basis, transfer, transfer_index, out_basis):
    excite, leaves, blocks, basis = excitation[0], leaf_basis[0], transfer[0], out_basis[0]
    index = transfer_index[0].T
    slots, rank, points = leaves.shape
    levels = blocks.shape[0]
    columns = excite.shape[2]
    n_blk = lax.axis_size("blk")
    rows = basis.shape[1] // n_blk
    nbits = lax.axis_size("box").bit_length() - 1
    bits = [None] + [(level - 1) % nbits for level in range(1, levels)]
    pair = in_vmem(slots, rank, 2 * rank)

    unit = slots * columns // sum(SHARES)
    widths = [unit * share for share in SHARES]
    begins = [sum(widths[:j]) for j in range(len(widths))]
    parts, places = [], []
    for begin, width in zip(begins, widths):
        part, place, lane = [], [], 0
        while lane < width:
            s, column = divmod(begin + lane, columns)
            size = min(width - lane, columns - column)
            part.append((s, lane, lane + size))
            place.append((s, column, lane, lane + size))
            lane += size
        parts.append(part)
        places.append(place)

    first, rest, *weights = call(
        leaf_kernel,
        "leaf",
        [ANY] * 4,
        [in_vmem(rank, widths[0]), in_vmem(rank, slots * columns - widths[0])] + [pair] * PRELOADED,
        [
            in_vmem(*excite.shape),
            in_vmem(*leaves.shape),
            pair,
            pltpu.SMEM(index.shape, jnp.int32),
            in_vmem(2 * rank, columns),
            pltpu.SemaphoreType.DMA((7 + 2 * PRELOADED,)),
        ],
        [in_hbm(excite), in_hbm(leaves), in_hbm(blocks), in_hbm(index)],
        limit=24 * 2**20,
    )
    weights = [None, *weights]

    def cross(level, value):
        return partner(value, "box", 2 ** bits[level])

    near_first, near_rest = cross(1, first), cross(1, rest)

    def step(name, jobs, after=(), flops=COST):
        args = [here(v) for level, j, own, other in jobs for v in (own, other, weights[level])]
        described, sizes = [], []
        for level, j, _, _ in jobs:
            begin = begins[j] - widths[0] if level == 1 and j else 0
            described.append((bits[level], parts[j], slice(begin, begin + widths[j])))
            sizes.append(widths[j])
        return call(
            functools.partial(levels_kernel, described),
            name,
            [VMEM] * len(args),
            [in_vmem(rank, size) for size in sizes],
            [in_vmem(2 * rank, size) for size in sizes],
            args,
            after,
            flops,
        )

    def job1(j):
        return (1, j, rest, near_rest) if j else (1, j, first, near_first)

    coeff2, near2, coeff3, near3 = {}, {}, {}, {}

    def second(j, value):
        coeff2[j] = value
        near2[j] = cross(2, value)

    def third(j, value):
        coeff3[j] = value
        near3[j] = cross(3, value)

    (value,) = step("level1_0", [job1(0)])
    second(0, value)
    (value,) = step("level1_1", [job1(1)], [coeff2[0]])
    second(1, value)
    value, ahead = step("level2_0", [(2, 0, coeff2[0], near2[0]), job1(2)], [coeff2[1]])
    third(0, value)
    second(2, ahead)
    *more, basis_v = call(
        prefetch_kernel,
        "prefetch",
        [ANY] * 3,
        [pair] * (levels - 1 - PRELOADED) + [in_vmem(*basis.shape)],
        [pltpu.SMEM(index.shape, jnp.int32), pltpu.SemaphoreType.DMA((2 * levels,))],
        [in_hbm(blocks), in_hbm(basis), in_hbm(index)],
        [coeff3[0]],
    )
    weights += more
    (value,) = step("level2_1", [(2, 1, coeff2[1], near2[1])], [basis_v])
    third(1, value)

    masks = [1 << b for b in range(n_blk.bit_length() - 1)]

    def halving(j):
        order = masks if j % 2 else masks[::-1]
        pieces = [0]
        for mask in order[::-1]:
            pieces = pieces + [d | mask for d in pieces]
        return order, pieces

    def result(j, count, dtype):
        return in_vmem(count * rows, widths[j], dtype=dtype)

    def tail(j, after, direct, folding=None, totalling=None):
        (coeff4,) = step(f"level3_{j}", [(3, j, coeff3[j], near3[j])], after, flops=0 if j == 1 else COST)
        near4 = cross(4, coeff4)
        outs, extra = [in_vmem(rank, widths[j], dtype=F32)], []
        if folding is not None:
            at, keep, got, count = folding
            extra += [keep, got]
            outs += [result(at, count // 2, BF16), result(at, count // 2, F32)]
        if totalling is not None:
            at, keep, got = totalling
            extra += [keep, got]
            outs += [result(at, 1, BF16)]
        partial, *more = call(
            functools.partial(
                between_kernel, bits[4], parts[j], folding is not None, totalling is not None
            ),
            f"between_{j}",
            [VMEM] * (2 + len(extra)),
            outs,
            [],
            [here(v) for v in (coeff4, weights[4], *extra)],
        )
        if direct:
            order = [[d] for d in range(n_blk)]
        else:
            pieces = halving(j)[1]
            order = [pieces[: n_blk // 2], pieces[n_blk // 2 :]]
        kinds = [F32] + [BF16] * (len(order) - 1)
        out = call(
            functools.partial(last_kernel, bits[4], parts[j], order),
            f"last_{j}",
            [VMEM] * 4,
            [result(j, len(o), kind) for o, kind in zip(order, kinds)],
            [],
            [here(v) for v in (partial, near4, weights[4], basis_v)],
        )
        return out, more

    def begin_sum(j, out):
        keep, send = out
        order = halving(j)[0]
        got, count = partner(send, "blk", order[0]), n_blk // 2
        for mask in order[1:-1]:
            send, keep = call(
                fold_kernel,
                f"fold_{j}_{mask}",
                [VMEM] * 2,
                [result(j, count // 2, BF16), result(j, count // 2, F32)],
                [],
                [here(keep), here(got)],
            )
            got, count = partner(send, "blk", mask), count // 2
        return j, keep, got, count

    def direct_sum(out):
        return [out[0]] + [partner(out[d], "blk", d) for d in range(n_blk - 1, 0, -1)]

    out0, _ = tail(0, [coeff3[1]], False)
    fold0 = begin_sum(0, out0)
    (value,) = step("level2_2", [(2, 2, coeff2[2], near2[2])], [out0[0]])
    third(2, value)
    (value,) = step("level1_3", [job1(3)], [coeff3[2]])
    second(3, value)
    def fold(held, after=()):
        at, keep, got, count = held
        send, keep = call(
            fold_kernel,
            f"fold_{at}",
            [VMEM] * 2,
            [result(at, count // 2, BF16), result(at, count // 2, F32)],
            [],
            [here(keep), here(got)],
            after,
        )
        return keep, partner(send, "blk", halving(at)[0][-1])

    out1, _ = tail(1, [coeff2[3]], False)
    fold1 = begin_sum(1, out1)
    keep0, got0 = fold(fold0, [out1[0]])
    (value,) = step("level2_3", [(2, 3, coeff2[3], near2[3])], [keep0])
    third(3, value)
    keep1, got1 = fold(fold1, [coeff3[3]])
    out2, (total0,) = tail(2, [keep1], True, None, (0, keep0, got0))
    group2 = direct_sum(out2)
    out3, (total1,) = tail(3, [out2[0]], True, None, (1, keep1, got1))
    group3 = direct_sum(out3)
    groups = [[total0], [total1], group2, group3]
    flat = [here(v) for group in groups for v in group]
    return pl.pallas_call(
        functools.partial(end_kernel, places, [len(group) for group in groups]),
        name="end",
        in_specs=[VMEM] * len(flat),
        out_specs=VMEM,
        out_shape=jax.ShapeDtypeStruct((slots, rows, columns), BF16),
        compiler_params=pltpu.CompilerParams(vmem_limit_bytes=8 * 2**20),
    )(*flat)


def solution(mesh):
    in_specs = (
        P("blk", "box", None, None),
        P("blk", "box", None, None),
        P("blk", None, "box", None, None),
        P("blk", None, "box"),
        P("blk", "box", None, None),
    )
    out_specs = P("box", "blk", None)
    return jax.shard_map(
        on_device, mesh=mesh, in_specs=in_specs, out_specs=out_specs, check_vma=False
    )
```

```python
import functools

import jax
import jax.numpy as jnp
from jax import lax
from jax.experimental import pallas as pl
from jax.experimental.pallas import tpu as pltpu
from jax.sharding import PartitionSpec as P

SHARES = (1, 2, 3, 2)
PRELOADED = 2
COST = 6 * 10**9
BF16 = jnp.bfloat16
F32 = jnp.float32
ANY = pl.BlockSpec(memory_space=pl.ANY)
VMEM = pl.BlockSpec(memory_space=pltpu.VMEM)


def dot(a, b):
    return jnp.dot(a, b, preferred_element_type=F32)


def in_vmem(*shape, dtype=BF16):
    return pltpu.VMEM(shape, dtype)


def here(value):
    return pltpu.with_memory_space_constraint(value, pltpu.VMEM)


def in_hbm(value):
    return pltpu.with_memory_space_constraint(value, pltpu.HBM)


def call(kernel, name, in_specs, out_shape, scratch, args, after=(), flops=COST, limit=8 * 2**20):
    count = len(in_specs)

    def body(*refs):
        kernel(*refs[:count], *refs[count + len(after) :])

    return pl.pallas_call(
        body,
        name=name,
        in_specs=[*in_specs, *[ANY] * len(after)],
        out_specs=[VMEM] * len(out_shape),
        out_shape=out_shape,
        scratch_shapes=scratch,
        compiler_params=pltpu.CompilerParams(vmem_limit_bytes=limit),
        cost_estimate=pl.CostEstimate(flops=flops, bytes_accessed=0, transcendentals=0),
    )(*args, *after)


def partner(value, axis, mask):
    pairs = [(source, source ^ mask) for source in range(lax.axis_size(axis))]
    return lax.ppermute(value, axis, pairs)


def leaf_kernel(excite, leaves, blocks, index, first, rest, *refs):
    count = PRELOADED
    nexts = refs[:count]
    excite_v, leaves_v, blocks_v, index_s, coeff, sems = refs[count:]
    slots, rank = leaves.shape[0], leaves.shape[1]
    columns, width = excite.shape[2], first.shape[1]
    listing = pltpu.make_async_copy(index, index_s, sems.at[0])
    listing.start()
    loads = []
    for s in range(slots):
        a = pltpu.make_async_copy(leaves.at[s], leaves_v.at[s], sems.at[1 + s])
        b = pltpu.make_async_copy(excite.at[s], excite_v.at[s], sems.at[3 + s])
        a.start()
        b.start()
        loads.append((a, b))
    listing.wait()
    weights, later = [], []
    for s in range(slots):
        c = pltpu.make_async_copy(blocks.at[0, index_s[s, 0]], blocks_v.at[s], sems.at[5 + s])
        c.start()
        weights.append(c)
    for level in range(1, 1 + count):
        for s in range(slots):
            c = pltpu.make_async_copy(
                blocks.at[level, index_s[s, level]], nexts[level - 1].at[s], sems.at[5 + 2 * level + s]
            )
            c.start()
            later.append(c)
    for s in range(slots):
        for load in loads[s]:
            load.wait()
        coeff[s * rank : (s + 1) * rank, :] = dot(leaves_v[s], excite_v[s]).astype(BF16)
    for s in range(slots):
        weights[s].wait()
        out = dot(blocks_v[s], coeff[...]).astype(BF16)
        if s == 0:
            first[...] = out[:, :width]
            rest[:, : columns - width] = out[:, width:]
        else:
            rest[:, s * columns - width : (s + 1) * columns - width] = out
    for c in later:
        c.wait()


def prefetch_kernel(blocks, basis, index, *refs):
    count = blocks.shape[0] - 1 - PRELOADED
    outs, basis_v, index_s, sems = refs[:count], refs[count], refs[count + 1], refs[count + 2]
    listing = pltpu.make_async_copy(index, index_s, sems.at[0])
    listing.start()
    c = pltpu.make_async_copy(basis, basis_v, sems.at[1 + 2 * count])
    c.start()
    copies = [c]
    listing.wait()
    for at in range(count):
        level = at + 1 + PRELOADED
        for s in range(2):
            c = pltpu.make_async_copy(blocks.at[level, index_s[s, level]], outs[at].at[s], sems.at[1 + 2 * at + s])
            c.start()
            copies.append(c)
    for c in copies:
        c.wait()


def upper_half(bit):
    return (lax.axis_index("box") >> bit) & 1


def mix(weights, own, other, bit, buf, parts, out):
    rank = own.shape[0]
    upper = upper_half(bit)
    buf[pl.ds(pl.multiple_of(upper * rank, rank), rank), :] = own
    buf[pl.ds(pl.multiple_of((1 - upper) * rank, rank), rank), :] = other
    for s, start, stop in parts:
        out[:, start:stop] = dot(weights[s], buf[:, start:stop]).astype(BF16)


def levels_kernel(jobs, *refs):
    count = len(jobs)
    ins, outs, bufs = refs[: 3 * count], refs[3 * count : 4 * count], refs[4 * count :]
    for at, (bit, parts, lanes) in enumerate(jobs):
        own, other, weights = ins[3 * at : 3 * at + 3]
        mix(weights, own[:, lanes], other[:, lanes], bit, bufs[at], parts, outs[at])


def half_dot(weights, s, half, value):
    rank = value.shape[0]
    return dot(weights[s, :, pl.ds(pl.multiple_of(half * rank, 128), rank)], value)


def sum_kernel(mine, *refs):
    total = mine[...]
    for piece in refs[:-1]:
        total = total + piece[...].astype(F32)
    refs[-1][...] = total.astype(BF16)


def between_kernel(bit, parts, counts, own, weights, *refs):
    refs = list(refs)
    groups = [[refs.pop(0) for _ in range(count)] for count in counts]
    partial = refs.pop(0)
    for s, start, stop in parts:
        partial[:, start:stop] = half_dot(weights, s, upper_half(bit), own[:, start:stop])
    for group, out in zip(groups, refs):
        sum_kernel(*group, out)


def last_kernel(bit, parts, partial, other, weights, basis, *refs):
    rows = refs[0].shape[0]
    me = lax.axis_index("blk")
    for s, start, stop in parts:
        mixed = partial[:, start:stop] + half_dot(weights, s, 1 - upper_half(bit), other[:, start:stop])
        coeff = mixed.astype(BF16)
        for d, ref in enumerate(refs):
            row = pl.multiple_of((me ^ d) * rows, rows)
            ref[:, start:stop] = dot(basis[s, pl.ds(row, rows), :], coeff).astype(ref.dtype)


def end_kernel(places, counts, *refs):
    refs = list(refs)
    out = refs[-1]
    for place, count in zip(places, counts):
        group = [refs.pop(0) for _ in range(count)]
        for s, column, start, stop in place:
            total = group[0][:, start:stop].astype(F32)
            for piece in group[1:]:
                total = total + piece[:, start:stop].astype(F32)
            out[s, :, column : column + stop - start] = total.astype(BF16)


def on_device(excitation, leaf_basis, transfer, transfer_index, out_basis):
    excite, leaves, blocks, basis = excitation[0], leaf_basis[0], transfer[0], out_basis[0]
    index = transfer_index[0].T
    slots, rank, points = leaves.shape
    levels = blocks.shape[0]
    columns = excite.shape[2]
    n_blk = lax.axis_size("blk")
    rows = basis.shape[1] // n_blk
    nbits = lax.axis_size("box").bit_length() - 1
    bits = [None] + [(level - 1) % nbits for level in range(1, levels)]
    pair = in_vmem(slots, rank, 2 * rank)

    unit = slots * columns // sum(SHARES)
    widths = [unit * share for share in SHARES]
    begins = [sum(widths[:j]) for j in range(len(widths))]
    parts, places = [], []
    for begin, width in zip(begins, widths):
        part, place, lane = [], [], 0
        while lane < width:
            s, column = divmod(begin + lane, columns)
            size = min(width - lane, columns - column)
            part.append((s, lane, lane + size))
            place.append((s, column, lane, lane + size))
            lane += size
        parts.append(part)
        places.append(place)

    first, rest, *weights = call(
        leaf_kernel,
        "leaf",
        [ANY] * 4,
        [in_vmem(rank, widths[0]), in_vmem(rank, slots * columns - widths[0])] + [pair] * PRELOADED,
        [
            in_vmem(*excite.shape),
            in_vmem(*leaves.shape),
            pair,
            pltpu.SMEM(index.shape, jnp.int32),
            in_vmem(2 * rank, columns),
            pltpu.SemaphoreType.DMA((7 + 2 * PRELOADED,)),
        ],
        [in_hbm(excite), in_hbm(leaves), in_hbm(blocks), in_hbm(index)],
        limit=24 * 2**20,
    )
    weights = [None, *weights]

    def cross(level, value):
        return partner(value, "box", 2 ** bits[level])

    near_first, near_rest = cross(1, first), cross(1, rest)

    def step(name, jobs, after=(), flops=COST):
        args = [here(v) for level, j, own, other in jobs for v in (own, other, weights[level])]
        described, sizes = [], []
        for level, j, _, _ in jobs:
            begin = begins[j] - widths[0] if level == 1 and j else 0
            described.append((bits[level], parts[j], slice(begin, begin + widths[j])))
            sizes.append(widths[j])
        return call(
            functools.partial(levels_kernel, described),
            name,
            [VMEM] * len(args),
            [in_vmem(rank, size) for size in sizes],
            [in_vmem(2 * rank, size) for size in sizes],
            args,
            after,
            flops,
        )

    def job1(j):
        return (1, j, rest, near_rest) if j else (1, j, first, near_first)

    coeff2, near2, coeff3, near3 = {}, {}, {}, {}

    def second(j, value):
        coeff2[j] = value
        near2[j] = cross(2, value)

    def third(j, value):
        coeff3[j] = value
        near3[j] = cross(3, value)

    (value,) = step("level1_0", [job1(0)])
    second(0, value)
    (value,) = step("level1_1", [job1(1)], [coeff2[0]])
    second(1, value)
    (value,) = step("level2_0", [(2, 0, coeff2[0], near2[0])], [coeff2[1]])
    third(0, value)
    (value,) = step("level1_2", [job1(2)], [coeff3[0]])
    second(2, value)
    *more, basis_v = call(
        prefetch_kernel,
        "prefetch",
        [ANY] * 3,
        [pair] * (levels - 1 - PRELOADED) + [in_vmem(*basis.shape)],
        [pltpu.SMEM(index.shape, jnp.int32), pltpu.SemaphoreType.DMA((2 * levels,))],
        [in_hbm(blocks), in_hbm(basis), in_hbm(index)],
        [coeff2[2]],
    )
    weights += more
    (value,) = step("level2_1", [(2, 1, coeff2[1], near2[1])], [basis_v])
    third(1, value)

    def tail(j, after, arrived=()):
        (coeff4,) = step(f"level3_{j}", [(3, j, coeff3[j], near3[j])], after)
        near4 = cross(4, coeff4)
        partial, *totals = call(
            functools.partial(between_kernel, bits[4], parts[j], [len(group) for _, group in arrived]),
            f"between_{j}",
            [VMEM] * (2 + sum(len(group) for _, group in arrived)),
            [in_vmem(rank, widths[j], dtype=F32)] + [in_vmem(rows, widths[at]) for at, _ in arrived],
            [],
            [here(v) for v in (coeff4, weights[4], *(v for _, group in arrived for v in group))],
        )
        out = call(
            functools.partial(last_kernel, bits[4], parts[j]),
            f"last_{j}",
            [VMEM] * 4,
            [in_vmem(rows, widths[j], dtype=F32)] + [in_vmem(rows, widths[j])] * (n_blk - 1),
            [],
            [here(v) for v in (partial, near4, weights[4], basis_v)],
            flops=COST if j < len(widths) - 1 else 0,
        )
        group = [out[0]] + [partner(out[d], "blk", d) for d in range(n_blk - 1, 0, -1)]
        return group, totals

    group0, _ = tail(0, [coeff3[1]])
    (value,) = step("level2_2", [(2, 2, coeff2[2], near2[2])], [group0[0]])
    third(2, value)
    (total0,) = call(
        sum_kernel,
        "sum_0",
        [VMEM] * n_blk,
        [in_vmem(rows, widths[0])],
        [],
        [here(v) for v in group0],
        [coeff3[2]],
    )
    (value,) = step("level1_3", [job1(3)], [total0])
    second(3, value)
    group1, _ = tail(1, [coeff2[3]])
    (value,) = step("level2_3", [(2, 3, coeff2[3], near2[3])], [group1[0]])
    third(3, value)
    group2, (total1,) = tail(2, [coeff3[3]], [(1, group1)])
    group3, _ = tail(3, [group2[0]])
    groups = [[total0], [total1], group2, group3]
    flat = [here(v) for group in groups for v in group]
    return pl.pallas_call(
        functools.partial(end_kernel, places, [len(group) for group in groups]),
        name="end",
        in_specs=[VMEM] * len(flat),
        out_specs=VMEM,
        out_shape=jax.ShapeDtypeStruct((slots, rows, columns), BF16),
        compiler_params=pltpu.CompilerParams(vmem_limit_bytes=8 * 2**20),
    )(*flat)


def solution(mesh):
    in_specs = (
        P("blk", "box", None, None),
        P("blk", "box", None, None),
        P("blk", None, "box", None, None),
        P("blk", None, "box"),
        P("blk", "box", None, None),
    )
    out_specs = P("box", "blk", None)
    return jax.shard_map(
        on_device, mesh=mesh, in_specs=in_specs, out_specs=out_specs, check_vma=False
    )
```

```python
import functools

import jax
import jax.numpy as jnp
from jax import lax
from jax.experimental import pallas as pl
from jax.experimental.pallas import tpu as pltpu
from jax.sharding import PartitionSpec as P

SHARES = (1, 3, 2, 2)
PRELOADED = 2
COST = 6 * 10**9
BF16 = jnp.bfloat16
F32 = jnp.float32
ANY = pl.BlockSpec(memory_space=pl.ANY)
VMEM = pl.BlockSpec(memory_space=pltpu.VMEM)


def dot(a, b):
    return jnp.dot(a, b, preferred_element_type=F32)


def in_vmem(*shape, dtype=BF16):
    return pltpu.VMEM(shape, dtype)


def here(value):
    return pltpu.with_memory_space_constraint(value, pltpu.VMEM)


def in_hbm(value):
    return pltpu.with_memory_space_constraint(value, pltpu.HBM)


def call(kernel, name, in_specs, out_shape, scratch, args, after=(), flops=COST, limit=8 * 2**20):
    count = len(in_specs)

    def body(*refs):
        kernel(*refs[:count], *refs[count + len(after) :])

    return pl.pallas_call(
        body,
        name=name,
        in_specs=[*in_specs, *[ANY] * len(after)],
        out_specs=[VMEM] * len(out_shape),
        out_shape=out_shape,
        scratch_shapes=scratch,
        compiler_params=pltpu.CompilerParams(vmem_limit_bytes=limit),
        cost_estimate=pl.CostEstimate(flops=flops, bytes_accessed=0, transcendentals=0),
    )(*args, *after)


def partner(value, axis, mask):
    pairs = [(source, source ^ mask) for source in range(lax.axis_size(axis))]
    return lax.ppermute(value, axis, pairs)


def leaf_kernel(excite, leaves, blocks, index, first, rest, *refs):
    count = PRELOADED
    nexts = refs[:count]
    excite_v, leaves_v, blocks_v, index_s, coeff, sems = refs[count:]
    slots, rank = leaves.shape[0], leaves.shape[1]
    columns, width = excite.shape[2], first.shape[1]
    listing = pltpu.make_async_copy(index, index_s, sems.at[0])
    listing.start()
    loads = []
    for s in range(slots):
        a = pltpu.make_async_copy(leaves.at[s], leaves_v.at[s], sems.at[1 + s])
        b = pltpu.make_async_copy(excite.at[s], excite_v.at[s], sems.at[3 + s])
        a.start()
        b.start()
        loads.append((a, b))
    listing.wait()
    weights, later = [], []
    for s in range(slots):
        c = pltpu.make_async_copy(blocks.at[0, index_s[s, 0]], blocks_v.at[s], sems.at[5 + s])
        c.start()
        weights.append(c)
    for level in range(1, 1 + count):
        for s in range(slots):
            c = pltpu.make_async_copy(
                blocks.at[level, index_s[s, level]], nexts[level - 1].at[s], sems.at[5 + 2 * level + s]
            )
            c.start()
            later.append(c)
    for s in range(slots):
        for load in loads[s]:
            load.wait()
        coeff[s * rank : (s + 1) * rank, :] = dot(leaves_v[s], excite_v[s]).astype(BF16)
    for s in range(slots):
        weights[s].wait()
        out = dot(blocks_v[s], coeff[...]).astype(BF16)
        if s == 0:
            first[...] = out[:, :width]
            rest[:, : columns - width] = out[:, width:]
        else:
            rest[:, s * columns - width : (s + 1) * columns - width] = out
    for c in later:
        c.wait()


def prefetch_kernel(blocks, basis, index, *refs):
    count = blocks.shape[0] - 1 - PRELOADED
    outs, basis_v, index_s, sems = refs[:count], refs[count], refs[count + 1], refs[count + 2]
    listing = pltpu.make_async_copy(index, index_s, sems.at[0])
    listing.start()
    c = pltpu.make_async_copy(basis, basis_v, sems.at[1 + 2 * count])
    c.start()
    copies = [c]
    listing.wait()
    for at in range(count):
        level = at + 1 + PRELOADED
        for s in range(2):
            c = pltpu.make_async_copy(blocks.at[level, index_s[s, level]], outs[at].at[s], sems.at[1 + 2 * at + s])
            c.start()
            copies.append(c)
    for c in copies:
        c.wait()


def upper_half(bit):
    return (lax.axis_index("box") >> bit) & 1


def mix(weights, own, other, bit, buf, parts, out):
    rank = own.shape[0]
    upper = upper_half(bit)
    buf[pl.ds(pl.multiple_of(upper * rank, rank), rank), :] = own
    buf[pl.ds(pl.multiple_of((1 - upper) * rank, rank), rank), :] = other
    for s, start, stop in parts:
        out[:, start:stop] = dot(weights[s], buf[:, start:stop]).astype(BF16)


def levels_kernel(jobs, *refs):
    count = len(jobs)
    ins, outs, bufs = refs[: 3 * count], refs[3 * count : 4 * count], refs[4 * count :]
    for at, (bit, parts, lanes) in enumerate(jobs):
        own, other, weights = ins[3 * at : 3 * at + 3]
        mix(weights, own[:, lanes], other[:, lanes], bit, bufs[at], parts, outs[at])


def half_dot(weights, s, half, value):
    rank = value.shape[0]
    return dot(weights[s, :, pl.ds(pl.multiple_of(half * rank, 128), rank)], value)


def sum_kernel(mine, *refs):
    total = mine[...]
    for piece in refs[:-1]:
        total = total + piece[...].astype(F32)
    refs[-1][...] = total.astype(BF16)


def between_kernel(bit, parts, counts, fold, own, weights, *refs):
    refs = list(refs)
    groups = [[refs.pop(0) for _ in range(count)] for count in counts]
    halves = [refs.pop(0) for _ in range(2 * fold)]
    partial = refs.pop(0)
    for s, start, stop in parts:
        partial[:, start:stop] = half_dot(weights, s, upper_half(bit), own[:, start:stop])
    for group in groups:
        sum_kernel(*group, refs.pop(0))
    if fold:
        fold_kernel(*halves, *refs)


def fold_kernel(keep, got, send, rest):
    rows = rest.shape[0]
    rest[...] = keep[:rows] + got[:rows].astype(F32)
    send[...] = (keep[rows:] + got[rows:].astype(F32)).astype(BF16)


def last_kernel(bit, parts, order, partial, other, weights, basis, *refs):
    rows = basis.shape[1] // lax.axis_size("blk")
    me = lax.axis_index("blk")
    for s, start, stop in parts:
        mixed = partial[:, start:stop] + half_dot(weights, s, 1 - upper_half(bit), other[:, start:stop])
        coeff = mixed.astype(BF16)
        for ref, distances in zip(refs, order):
            for at, d in enumerate(distances):
                row = pl.multiple_of((me ^ d) * rows, rows)
                piece = dot(basis[s, pl.ds(row, rows), :], coeff)
                ref[at * rows : (at + 1) * rows, start:stop] = piece.astype(ref.dtype)


def end_kernel(places, counts, *refs):
    refs = list(refs)
    out = refs[-1]
    for place, count in zip(places, counts):
        group = [refs.pop(0) for _ in range(count)]
        for s, column, start, stop in place:
            total = group[0][:, start:stop].astype(F32)
            for piece in group[1:]:
                total = total + piece[:, start:stop].astype(F32)
            out[s, :, column : column + stop - start] = total.astype(BF16)


def on_device(excitation, leaf_basis, transfer, transfer_index, out_basis):
    excite, leaves, blocks, basis = excitation[0], leaf_basis[0], transfer[0], out_basis[0]
    index = transfer_index[0].T
    slots, rank, points = leaves.shape
    levels = blocks.shape[0]
    columns = excite.shape[2]
    n_blk = lax.axis_size("blk")
    rows = basis.shape[1] // n_blk
    nbits = lax.axis_size("box").bit_length() - 1
    bits = [None] + [(level - 1) % nbits for level in range(1, levels)]
    pair = in_vmem(slots, rank, 2 * rank)

    unit = slots * columns // sum(SHARES)
    widths = [unit * share for share in SHARES]
    begins = [sum(widths[:j]) for j in range(len(widths))]
    parts, places = [], []
    for begin, width in zip(begins, widths):
        part, place, lane = [], [], 0
        while lane < width:
            s, column = divmod(begin + lane, columns)
            size = min(width - lane, columns - column)
            part.append((s, lane, lane + size))
            place.append((s, column, lane, lane + size))
            lane += size
        parts.append(part)
        places.append(place)

    first, rest, *weights = call(
        leaf_kernel,
        "leaf",
        [ANY] * 4,
        [in_vmem(rank, widths[0]), in_vmem(rank, slots * columns - widths[0])] + [pair] * PRELOADED,
        [
            in_vmem(*excite.shape),
            in_vmem(*leaves.shape),
            pair,
            pltpu.SMEM(index.shape, jnp.int32),
            in_vmem(2 * rank, columns),
            pltpu.SemaphoreType.DMA((7 + 2 * PRELOADED,)),
        ],
        [in_hbm(excite), in_hbm(leaves), in_hbm(blocks), in_hbm(index)],
        limit=24 * 2**20,
    )
    weights = [None, *weights]

    def cross(level, value):
        return partner(value, "box", 2 ** bits[level])

    near_first, near_rest = cross(1, first), cross(1, rest)

    def step(name, jobs, after=(), flops=COST):
        args = [here(v) for level, j, own, other in jobs for v in (own, other, weights[level])]
        described, sizes = [], []
        for level, j, _, _ in jobs:
            begin = begins[j] - widths[0] if level == 1 and j else 0
            described.append((bits[level], parts[j], slice(begin, begin + widths[j])))
            sizes.append(widths[j])
        return call(
            functools.partial(levels_kernel, described),
            name,
            [VMEM] * len(args),
            [in_vmem(rank, size) for size in sizes],
            [in_vmem(2 * rank, size) for size in sizes],
            args,
            after,
            flops,
        )

    def job1(j):
        return (1, j, rest, near_rest) if j else (1, j, first, near_first)

    coeff2, near2, coeff3, near3 = {}, {}, {}, {}

    def second(j, value):
        coeff2[j] = value
        near2[j] = cross(2, value)

    def third(j, value):
        coeff3[j] = value
        near3[j] = cross(3, value)

    (value,) = step("level1_0", [job1(0)])
    second(0, value)
    (value,) = step("level1_1", [job1(1)], [coeff2[0]])
    second(1, value)
    (value,) = step("level2_0", [(2, 0, coeff2[0], near2[0])], [coeff2[1]])
    third(0, value)
    (value,) = step("level1_2", [job1(2)], [coeff3[0]])
    second(2, value)
    *more, basis_v = call(
        prefetch_kernel,
        "prefetch",
        [ANY] * 3,
        [pair] * (levels - 1 - PRELOADED) + [in_vmem(*basis.shape)],
        [pltpu.SMEM(index.shape, jnp.int32), pltpu.SemaphoreType.DMA((2 * levels,))],
        [in_hbm(blocks), in_hbm(basis), in_hbm(index)],
        [coeff2[2]],
    )
    weights += more
    (value,) = step("level2_1", [(2, 1, coeff2[1], near2[1])], [basis_v])
    third(1, value)

    def result(j, count, dtype):
        return in_vmem(count * rows, widths[j], dtype=dtype)

    direct = [[d] for d in range(n_blk)]

    def tail(j, after, order, arrived=(), folding=None):
        (coeff4,) = step(f"level3_{j}", [(3, j, coeff3[j], near3[j])], after)
        near4 = cross(4, coeff4)
        extra = [v for _, group in arrived for v in group]
        outs = [in_vmem(rank, widths[j], dtype=F32)] + [result(at, 1, BF16) for at, _ in arrived]
        if folding is not None:
            at, keep, got, count = folding
            extra += [keep, got]
            outs += [result(at, count // 2, BF16), result(at, count // 2, F32)]
        partial, *more = call(
            functools.partial(
                between_kernel, bits[4], parts[j], [len(group) for _, group in arrived], folding is not None
            ),
            f"between_{j}",
            [VMEM] * (2 + len(extra)),
            outs,
            [],
            [here(v) for v in (coeff4, weights[4], *extra)],
        )
        out = call(
            functools.partial(last_kernel, bits[4], parts[j], order),
            f"last_{j}",
            [VMEM] * 4,
            [result(j, len(o), BF16 if at else F32) for at, o in enumerate(order)],
            [],
            [here(v) for v in (partial, near4, weights[4], basis_v)],
            flops=COST if j < len(widths) - 1 else 0,
        )
        return out, more

    def direct_sum(out):
        return [out[0]] + [partner(out[d], "blk", d) for d in range(n_blk - 1, 0, -1)]

    masks = [1 << b for b in range(n_blk.bit_length() - 1)]
    halves = [0]
    for mask in masks[::-1]:
        halves = halves + [d | mask for d in halves]

    def begin_sum(j, out):
        keep, send = out
        got, count = partner(send, "blk", masks[0]), n_blk // 2
        for mask in masks[1:-1]:
            send, keep = call(
                fold_kernel,
                f"fold_{j}_{mask}",
                [VMEM] * 2,
                [result(j, count // 2, BF16), result(j, count // 2, F32)],
                [],
                [here(keep), here(got)],
            )
            got, count = partner(send, "blk", mask), count // 2
        return j, keep, got, count

    out0, _ = tail(0, [coeff3[1]], direct)
    group0 = direct_sum(out0)
    (value,) = step("level2_2", [(2, 2, coeff2[2], near2[2])], [out0[0]])
    third(2, value)
    (total0,) = call(
        sum_kernel, "sum_0", [VMEM] * n_blk, [result(0, 1, BF16)], [], [here(v) for v in group0], [coeff3[2]]
    )
    (value,) = step("level1_3", [job1(3)], [total0])
    second(3, value)
    out1, _ = tail(1, [coeff2[3]], direct)
    group1 = direct_sum(out1)
    (value,) = step("level2_3", [(2, 3, coeff2[3], near2[3])], [out1[0]])
    third(3, value)
    out2, (total1,) = tail(
        2, [coeff3[3]], [halves[: n_blk // 2], halves[n_blk // 2 :]], [(1, group1)]
    )
    fold2 = begin_sum(2, out2)
    out3, (send2, keep2) = tail(3, [out2[0]], direct, (), fold2)
    got2 = partner(send2, "blk", masks[-1])
    group3 = direct_sum(out3)
    (total2,) = call(sum_kernel, "sum_2", [VMEM] * 2, [result(2, 1, BF16)], [], [here(keep2), here(got2)], [out3[0]], 0)
    groups = [[total0], [total1], [total2], group3]
    flat = [here(v) for group in groups for v in group]
    return pl.pallas_call(
        functools.partial(end_kernel, places, [len(group) for group in groups]),
        name="end",
        in_specs=[VMEM] * len(flat),
        out_specs=VMEM,
        out_shape=jax.ShapeDtypeStruct((slots, rows, columns), BF16),
        compiler_params=pltpu.CompilerParams(vmem_limit_bytes=8 * 2**20),
    )(*flat)


def solution(mesh):
    in_specs = (
        P("blk", "box", None, None),
        P("blk", "box", None, None),
        P("blk", None, "box", None, None),
        P("blk", None, "box"),
        P("blk", "box", None, None),
    )
    out_specs = P("box", "blk", None)
    return jax.shard_map(
        on_device, mesh=mesh, in_specs=in_specs, out_specs=out_specs, check_vma=False
    )
```

```python
import functools

import jax
import jax.numpy as jnp
from jax import lax
from jax.experimental import pallas as pl
from jax.experimental.pallas import tpu as pltpu
from jax.sharding import PartitionSpec as P

SHARES = (1, 2, 3, 2)
PRELOADED = 2
DEPTHS = 2
COST = 6 * 10**9
BF16 = jnp.bfloat16
F32 = jnp.float32
ANY = pl.BlockSpec(memory_space=pl.ANY)
VMEM = pl.BlockSpec(memory_space=pltpu.VMEM)


def dot(a, b):
    return jnp.dot(a, b, preferred_element_type=F32)


def in_vmem(*shape, dtype=BF16):
    return pltpu.VMEM(shape, dtype)


def here(value):
    return pltpu.with_memory_space_constraint(value, pltpu.VMEM)


def in_hbm(value):
    return pltpu.with_memory_space_constraint(value, pltpu.HBM)


def call(kernel, name, in_specs, out_shape, scratch, args, after=(), flops=COST, limit=8 * 2**20, through=()):
    count, outs = len(in_specs), len(out_shape)

    def body(*refs):
        held = refs[count + len(after) + len(through) :]
        kernel(*refs[:count], *held[:outs], *held[outs + len(through) :])

    return pl.pallas_call(
        body,
        name=name,
        in_specs=[*in_specs, *[ANY] * (len(after) + len(through))],
        out_specs=[VMEM] * outs + [ANY] * len(through),
        out_shape=[*out_shape, *[in_vmem(*v.shape, dtype=v.dtype) for v in through]],
        scratch_shapes=scratch,
        input_output_aliases={count + len(after) + at: outs + at for at in range(len(through))},
        compiler_params=pltpu.CompilerParams(vmem_limit_bytes=limit),
        cost_estimate=pl.CostEstimate(flops=flops, bytes_accessed=0, transcendentals=0),
    )(*args, *after, *[here(v) for v in through])


def partner(value, axis, mask):
    pairs = [(source, source ^ mask) for source in range(lax.axis_size(axis))]
    return lax.ppermute(value, axis, pairs)


def leaf_kernel(excite, leaves, blocks, index, first, rest, *refs):
    count = PRELOADED
    nexts = refs[:count]
    excite_v, leaves_v, blocks_v, index_s, coeff, sems = refs[count:]
    slots, rank = leaves.shape[0], leaves.shape[1]
    columns, width = excite.shape[2], first.shape[1]
    base = 1 + 2 * (1 + count)
    listing = pltpu.make_async_copy(index, index_s, sems.at[0])
    listing.start()
    loads = []
    depth = leaves.shape[2] // DEPTHS
    spans = [pl.ds(k * depth, depth) for k in range(DEPTHS)]
    for s in range(slots):
        for k, span in enumerate(spans):
            at = base + 2 * (s * DEPTHS + k)
            a = pltpu.make_async_copy(leaves.at[s, :, span], leaves_v.at[s, :, span], sems.at[at])
            b = pltpu.make_async_copy(excite.at[s, span], excite_v.at[s, span], sems.at[at + 1])
            a.start()
            b.start()
            loads.append((a, b))
    listing.wait()
    weights, later = [], []
    for s in range(slots):
        c = pltpu.make_async_copy(blocks.at[0, index_s[s, 0]], blocks_v.at[s], sems.at[1 + s])
        c.start()
        weights.append(c)
    for level in range(1, 1 + count):
        for s in range(slots):
            c = pltpu.make_async_copy(
                blocks.at[level, index_s[s, level]], nexts[level - 1].at[s], sems.at[1 + 2 * level + s]
            )
            c.start()
            later.append(c)
    for s in range(slots):
        total = None
        for k, span in enumerate(spans):
            for load in loads[s * DEPTHS + k]:
                load.wait()
            part = dot(leaves_v[s, :, span], excite_v[s, span])
            total = part if total is None else total + part
        coeff[s * rank : (s + 1) * rank, :] = total.astype(BF16)
    for s in range(slots):
        weights[s].wait()
        out = dot(blocks_v[s], coeff[...]).astype(BF16)
        if s == 0:
            first[...] = out[:, :width]
            rest[:, : columns - width] = out[:, width:]
        else:
            rest[:, s * columns - width : (s + 1) * columns - width] = out
    for c in later:
        c.wait()


def prefetch_kernel(blocks, basis, index, *refs):
    count = blocks.shape[0] - 1 - PRELOADED
    outs, basis_v, index_s, sems = refs[:count], refs[count], refs[count + 1], refs[count + 2]
    listing = pltpu.make_async_copy(index, index_s, sems.at[0])
    listing.start()
    c = pltpu.make_async_copy(basis, basis_v, sems.at[1 + 2 * count])
    c.start()
    copies = [c]
    listing.wait()
    for at in range(count):
        level = at + 1 + PRELOADED
        for s in range(2):
            c = pltpu.make_async_copy(blocks.at[level, index_s[s, level]], outs[at].at[s], sems.at[1 + 2 * at + s])
            c.start()
            copies.append(c)
    for c in copies:
        c.wait()


def upper_half(bit):
    return (lax.axis_index("box") >> bit) & 1


def mix(weights, own, other, bit, buf, parts, out):
    rank = own.shape[0]
    upper = upper_half(bit)
    buf[pl.ds(pl.multiple_of(upper * rank, rank), rank), :] = own
    buf[pl.ds(pl.multiple_of((1 - upper) * rank, rank), rank), :] = other
    for s, start, stop in parts:
        out[:, start:stop] = dot(weights[s], buf[:, start:stop]).astype(BF16)


def levels_kernel(jobs, *refs):
    count = len(jobs)
    ins, outs, bufs = refs[: 3 * count], refs[3 * count : 4 * count], refs[4 * count :]
    for at, (bit, parts, lanes) in enumerate(jobs):
        own, other, weights = ins[3 * at : 3 * at + 3]
        mix(weights, own[:, lanes], other[:, lanes], bit, bufs[at], parts, outs[at])


def half_dot(weights, s, half, value):
    rank = value.shape[0]
    return dot(weights[s, :, pl.ds(pl.multiple_of(half * rank, 128), rank)], value)


def sum_kernel(mine, *refs):
    total = mine[...]
    for piece in refs[:-1]:
        total = total + piece[...].astype(F32)
    refs[-1][...] = total.astype(BF16)


def between_kernel(bit, parts, counts, own, weights, *refs):
    refs = list(refs)
    groups = [[refs.pop(0) for _ in range(count)] for count in counts]
    partial = refs.pop(0)
    for s, start, stop in parts:
        partial[:, start:stop] = half_dot(weights, s, upper_half(bit), own[:, start:stop])
    for group, out in zip(groups, refs):
        sum_kernel(*group, out)


def last_kernel(bit, parts, partial, other, weights, basis, *refs):
    rows = refs[0].shape[0]
    me = lax.axis_index("blk")
    for s, start, stop in parts:
        mixed = partial[:, start:stop] + half_dot(weights, s, 1 - upper_half(bit), other[:, start:stop])
        coeff = mixed.astype(BF16)
        for d, ref in enumerate(refs):
            row = pl.multiple_of((me ^ d) * rows, rows)
            ref[:, start:stop] = dot(basis[s, pl.ds(row, rows), :], coeff).astype(ref.dtype)


def end_kernel(places, counts, *refs):
    refs = list(refs)
    out = refs[-1]
    for place, count in zip(places, counts):
        group = [refs.pop(0) for _ in range(count)]
        for s, column, start, stop in place:
            total = group[0][:, start:stop].astype(F32)
            for piece in group[1:]:
                total = total + piece[:, start:stop].astype(F32)
            out[s, :, column : column + stop - start] = total.astype(BF16)


def on_device(excitation, leaf_basis, transfer, transfer_index, out_basis):
    excite, leaves, blocks, basis = excitation[0], leaf_basis[0], transfer[0], out_basis[0]
    index = transfer_index[0].T
    slots, rank, points = leaves.shape
    levels = blocks.shape[0]
    columns = excite.shape[2]
    n_blk = lax.axis_size("blk")
    rows = basis.shape[1] // n_blk
    nbits = lax.axis_size("box").bit_length() - 1
    bits = [None] + [(level - 1) % nbits for level in range(1, levels)]
    pair = in_vmem(slots, rank, 2 * rank)

    unit = slots * columns // sum(SHARES)
    widths = [unit * share for share in SHARES]
    begins = [sum(widths[:j]) for j in range(len(widths))]
    parts, places = [], []
    for begin, width in zip(begins, widths):
        part, place, lane = [], [], 0
        while lane < width:
            s, column = divmod(begin + lane, columns)
            size = min(width - lane, columns - column)
            part.append((s, lane, lane + size))
            place.append((s, column, lane, lane + size))
            lane += size
        parts.append(part)
        places.append(place)

    first, rest, *weights = call(
        leaf_kernel,
        "leaf",
        [ANY] * 4,
        [in_vmem(rank, widths[0]), in_vmem(rank, slots * columns - widths[0])] + [pair] * PRELOADED,
        [
            in_vmem(*excite.shape),
            in_vmem(*leaves.shape),
            pair,
            pltpu.SMEM(index.shape, jnp.int32),
            in_vmem(2 * rank, columns),
            pltpu.SemaphoreType.DMA((1 + 2 * (1 + PRELOADED) + 2 * slots * DEPTHS,)),
        ],
        [in_hbm(excite), in_hbm(leaves), in_hbm(blocks), in_hbm(index)],
        limit=24 * 2**20,
    )
    weights = [None, *weights]

    def cross(level, value):
        return partner(value, "box", 2 ** bits[level])

    near_first = cross(1, first)

    def step(name, jobs, after=(), flops=COST, through=()):
        args = [here(v) for level, j, own, other in jobs for v in (own, other, weights[level])]
        described, sizes = [], []
        for level, j, _, _ in jobs:
            begin = begins[j] - widths[0] if level == 1 and j else 0
            described.append((bits[level], parts[j], slice(begin, begin + widths[j])))
            sizes.append(widths[j])
        return call(
            functools.partial(levels_kernel, described),
            name,
            [VMEM] * len(args),
            [in_vmem(rank, size) for size in sizes],
            [in_vmem(2 * rank, size) for size in sizes],
            args,
            after,
            flops,
            through=through,
        )

    def job1(j):
        return (1, j, rest, near_rest) if j else (1, j, first, near_first)

    coeff2, near2, coeff3, near3 = {}, {}, {}, {}

    def second(j, value):
        coeff2[j] = value
        near2[j] = cross(2, value)

    def third(j, value):
        coeff3[j] = value
        near3[j] = cross(3, value)

    value, rest = step("level1_0", [job1(0)], through=[rest])
    near_rest = cross(1, rest)
    second(0, value)
    (value,) = step("level1_1", [job1(1)], [coeff2[0]])
    second(1, value)
    *more, basis_v = call(
        prefetch_kernel,
        "prefetch",
        [ANY] * 3,
        [pair] * (levels - 1 - PRELOADED) + [in_vmem(*basis.shape)],
        [pltpu.SMEM(index.shape, jnp.int32), pltpu.SemaphoreType.DMA((2 * levels,))],
        [in_hbm(blocks), in_hbm(basis), in_hbm(index)],
        [coeff2[1]],
    )
    weights += more
    (value,) = step("level2_0", [(2, 0, coeff2[0], near2[0])], [basis_v])
    third(0, value)
    (value,) = step("level1_2", [job1(2)], [coeff3[0]])
    second(2, value)
    (value,) = step("level2_1", [(2, 1, coeff2[1], near2[1])], [coeff2[2]])
    third(1, value)

    def tail(j, after, arrived=()):
        (coeff4,) = step(f"level3_{j}", [(3, j, coeff3[j], near3[j])], after)
        near4 = cross(4, coeff4)
        partial, *totals = call(
            functools.partial(between_kernel, bits[4], parts[j], [len(group) for _, group in arrived]),
            f"between_{j}",
            [VMEM] * (2 + sum(len(group) for _, group in arrived)),
            [in_vmem(rank, widths[j], dtype=F32)] + [in_vmem(rows, widths[at]) for at, _ in arrived],
            [],
            [here(v) for v in (coeff4, weights[4], *(v for _, group in arrived for v in group))],
        )
        out = call(
            functools.partial(last_kernel, bits[4], parts[j]),
            f"last_{j}",
            [VMEM] * 4,
            [in_vmem(rows, widths[j], dtype=F32)] + [in_vmem(rows, widths[j])] * (n_blk - 1),
            [],
            [here(v) for v in (partial, near4, weights[4], basis_v)],
            flops=COST if j < len(widths) - 1 else 0,
        )
        group = [out[0]] + [partner(out[d], "blk", d) for d in range(n_blk - 1, 0, -1)]
        return group, totals

    group0, _ = tail(0, [coeff3[1]])
    (value,) = step("level2_2", [(2, 2, coeff2[2], near2[2])], [group0[0]])
    third(2, value)
    (total0,) = call(
        sum_kernel,
        "sum_0",
        [VMEM] * n_blk,
        [in_vmem(rows, widths[0])],
        [],
        [here(v) for v in group0],
        [coeff3[2]],
    )
    (value,) = step("level1_3", [job1(3)], [total0])
    second(3, value)
    group1, _ = tail(1, [coeff2[3]])
    (value,) = step("level2_3", [(2, 3, coeff2[3], near2[3])], [group1[0]])
    third(3, value)
    group2, (total1,) = tail(2, [coeff3[3]], [(1, group1)])
    group3, _ = tail(3, [group2[0]])
    groups = [[total0], [total1], group2, group3]
    flat = [here(v) for group in groups for v in group]
    return pl.pallas_call(
        functools.partial(end_kernel, places, [len(group) for group in groups]),
        name="end",
        in_specs=[VMEM] * len(flat),
        out_specs=VMEM,
        out_shape=jax.ShapeDtypeStruct((slots, rows, columns), BF16),
        compiler_params=pltpu.CompilerParams(vmem_limit_bytes=8 * 2**20),
    )(*flat)


def solution(mesh):
    in_specs = (
        P("blk", "box", None, None),
        P("blk", "box", None, None),
        P("blk", None, "box", None, None),
        P("blk", None, "box"),
        P("blk", "box", None, None),
    )
    out_specs = P("box", "blk", None)
    return jax.shard_map(
        on_device, mesh=mesh, in_specs=in_specs, out_specs=out_specs, check_vma=False
    )
```

```python
import functools

import jax
import jax.numpy as jnp
from jax import lax
from jax.experimental import pallas as pl
from jax.experimental.pallas import tpu as pltpu
from jax.sharding import PartitionSpec as P

SHARES = (1, 2, 3, 2)
PRELOADED = 2
DEPTHS = 1
COST = 6 * 10**9
BF16 = jnp.bfloat16
F32 = jnp.float32
ANY = pl.BlockSpec(memory_space=pl.ANY)
VMEM = pl.BlockSpec(memory_space=pltpu.VMEM)


def dot(a, b):
    return jnp.dot(a, b, preferred_element_type=F32)


def in_vmem(*shape, dtype=BF16):
    return pltpu.VMEM(shape, dtype)


def here(value):
    return pltpu.with_memory_space_constraint(value, pltpu.VMEM)


def in_hbm(value):
    return pltpu.with_memory_space_constraint(value, pltpu.HBM)


def call(kernel, name, in_specs, out_shape, scratch, args, after=(), flops=COST, limit=8 * 2**20, through=()):
    count, outs = len(in_specs), len(out_shape)

    def body(*refs):
        held = refs[count + len(after) + len(through) :]
        kernel(*refs[:count], *held[:outs], *held[outs + len(through) :])

    return pl.pallas_call(
        body,
        name=name,
        in_specs=[*in_specs, *[ANY] * (len(after) + len(through))],
        out_specs=[VMEM] * outs + [ANY] * len(through),
        out_shape=[*out_shape, *[in_vmem(*v.shape, dtype=v.dtype) for v in through]],
        scratch_shapes=scratch,
        input_output_aliases={count + len(after) + at: outs + at for at in range(len(through))},
        compiler_params=pltpu.CompilerParams(vmem_limit_bytes=limit),
        cost_estimate=pl.CostEstimate(flops=flops, bytes_accessed=0, transcendentals=0),
    )(*args, *after, *[here(v) for v in through])


def partner(value, axis, mask):
    pairs = [(source, source ^ mask) for source in range(lax.axis_size(axis))]
    return lax.ppermute(value, axis, pairs)


def leaf_kernel(excite, leaves, blocks, index, first, rest, *refs):
    count = PRELOADED
    nexts = refs[:count]
    excite_v, leaves_v, blocks_v, index_s, coeff, sems = refs[count:]
    slots, rank = leaves.shape[0], leaves.shape[1]
    columns, width = excite.shape[2], first.shape[1]
    base = 1 + 2 * (1 + count)
    listing = pltpu.make_async_copy(index, index_s, sems.at[0])
    listing.start()
    loads = []
    depth = leaves.shape[2] // DEPTHS
    spans = [pl.ds(k * depth, depth) for k in range(DEPTHS)]
    for s in range(slots):
        for k, span in enumerate(spans):
            at = base + 2 * (s * DEPTHS + k)
            a = pltpu.make_async_copy(leaves.at[s, :, span], leaves_v.at[s, :, span], sems.at[at])
            b = pltpu.make_async_copy(excite.at[s, span], excite_v.at[s, span], sems.at[at + 1])
            a.start()
            b.start()
            loads.append((a, b))
    listing.wait()
    weights, later = [], []
    for s in range(slots):
        c = pltpu.make_async_copy(blocks.at[0, index_s[s, 0]], blocks_v.at[s], sems.at[1 + s])
        c.start()
        weights.append(c)
    for level in range(1, 1 + count):
        for s in range(slots):
            c = pltpu.make_async_copy(
                blocks.at[level, index_s[s, level]], nexts[level - 1].at[s], sems.at[1 + 2 * level + s]
            )
            c.start()
            later.append(c)
    for s in range(slots):
        total = None
        for k, span in enumerate(spans):
            for load in loads[s * DEPTHS + k]:
                load.wait()
            part = dot(leaves_v[s, :, span], excite_v[s, span])
            total = part if total is None else total + part
        coeff[s * rank : (s + 1) * rank, :] = total.astype(BF16)
    for s in range(slots):
        weights[s].wait()
        out = dot(blocks_v[s], coeff[...]).astype(BF16)
        if s == 0:
            first[...] = out[:, :width]
            rest[:, : columns - width] = out[:, width:]
        else:
            rest[:, s * columns - width : (s + 1) * columns - width] = out
    for c in later:
        c.wait()


def prefetch_kernel(blocks, basis, index, *refs):
    count = blocks.shape[0] - 1 - PRELOADED
    outs, basis_v, index_s, sems = refs[:count], refs[count], refs[count + 1], refs[count + 2]
    listing = pltpu.make_async_copy(index, index_s, sems.at[0])
    listing.start()
    c = pltpu.make_async_copy(basis, basis_v, sems.at[1 + 2 * count])
    c.start()
    copies = [c]
    listing.wait()
    for at in range(count):
        level = at + 1 + PRELOADED
        for s in range(2):
            c = pltpu.make_async_copy(blocks.at[level, index_s[s, level]], outs[at].at[s], sems.at[1 + 2 * at + s])
            c.start()
            copies.append(c)
    for c in copies:
        c.wait()


def upper_half(bit):
    return (lax.axis_index("box") >> bit) & 1


def mix(weights, own, other, bit, buf, parts, out):
    rank = own.shape[0]
    upper = upper_half(bit)
    buf[pl.ds(pl.multiple_of(upper * rank, rank), rank), :] = own
    buf[pl.ds(pl.multiple_of((1 - upper) * rank, rank), rank), :] = other
    for s, start, stop in parts:
        out[:, start:stop] = dot(weights[s], buf[:, start:stop]).astype(BF16)


def levels_kernel(jobs, *refs):
    count = len(jobs)
    ins, outs, bufs = refs[: 3 * count], refs[3 * count : 4 * count], refs[4 * count :]
    for at, (bit, parts, lanes) in enumerate(jobs):
        own, other, weights = ins[3 * at : 3 * at + 3]
        mix(weights, own[:, lanes], other[:, lanes], bit, bufs[at], parts, outs[at])


def half_dot(weights, s, half, value):
    rank = value.shape[0]
    return dot(weights[s, :, pl.ds(pl.multiple_of(half * rank, 128), rank)], value)


def sum_kernel(mine, *refs):
    total = mine[...]
    for piece in refs[:-1]:
        total = total + piece[...].astype(F32)
    refs[-1][...] = total.astype(BF16)


def between_kernel(bit, parts, counts, own, weights, *refs):
    refs = list(refs)
    groups = [[refs.pop(0) for _ in range(count)] for count in counts]
    partial = refs.pop(0)
    for s, start, stop in parts:
        partial[:, start:stop] = half_dot(weights, s, upper_half(bit), own[:, start:stop])
    for group, out in zip(groups, refs):
        sum_kernel(*group, out)


def last_kernel(bit, parts, partial, other, weights, basis, *refs):
    rows = refs[0].shape[0]
    me = lax.axis_index("blk")
    for s, start, stop in parts:
        mixed = partial[:, start:stop] + half_dot(weights, s, 1 - upper_half(bit), other[:, start:stop])
        coeff = mixed.astype(BF16)
        for d, ref in enumerate(refs):
            row = pl.multiple_of((me ^ d) * rows, rows)
            ref[:, start:stop] = dot(basis[s, pl.ds(row, rows), :], coeff).astype(ref.dtype)


def end_kernel(places, counts, *refs):
    refs = list(refs)
    out = refs[-1]
    for place, count in zip(places, counts):
        group = [refs.pop(0) for _ in range(count)]
        for s, column, start, stop in place:
            total = group[0][:, start:stop].astype(F32)
            for piece in group[1:]:
                total = total + piece[:, start:stop].astype(F32)
            out[s, :, column : column + stop - start] = total.astype(BF16)


def on_device(excitation, leaf_basis, transfer, transfer_index, out_basis):
    excite, leaves, blocks, basis = excitation[0], leaf_basis[0], transfer[0], out_basis[0]
    index = transfer_index[0].T
    slots, rank, points = leaves.shape
    levels = blocks.shape[0]
    columns = excite.shape[2]
    n_blk = lax.axis_size("blk")
    rows = basis.shape[1] // n_blk
    nbits = lax.axis_size("box").bit_length() - 1
    bits = [None] + [(level - 1) % nbits for level in range(1, levels)]
    pair = in_vmem(slots, rank, 2 * rank)

    unit = slots * columns // sum(SHARES)
    widths = [unit * share for share in SHARES]
    begins = [sum(widths[:j]) for j in range(len(widths))]
    parts, places = [], []
    for begin, width in zip(begins, widths):
        part, place, lane = [], [], 0
        while lane < width:
            s, column = divmod(begin + lane, columns)
            size = min(width - lane, columns - column)
            part.append((s, lane, lane + size))
            place.append((s, column, lane, lane + size))
            lane += size
        parts.append(part)
        places.append(place)

    first, rest, *weights = call(
        leaf_kernel,
        "leaf",
        [ANY] * 4,
        [in_vmem(rank, widths[0]), in_vmem(rank, slots * columns - widths[0])] + [pair] * PRELOADED,
        [
            in_vmem(*excite.shape),
            in_vmem(*leaves.shape),
            pair,
            pltpu.SMEM(index.shape, jnp.int32),
            in_vmem(2 * rank, columns),
            pltpu.SemaphoreType.DMA((1 + 2 * (1 + PRELOADED) + 2 * slots * DEPTHS,)),
        ],
        [in_hbm(excite), in_hbm(leaves), in_hbm(blocks), in_hbm(index)],
        limit=24 * 2**20,
    )
    weights = [None, *weights]

    def cross(level, value):
        return partner(value, "box", 2 ** bits[level])

    near_first = cross(1, first)

    def step(name, jobs, after=(), flops=COST, through=()):
        args = [here(v) for level, j, own, other in jobs for v in (own, other, weights[level])]
        described, sizes = [], []
        for level, j, _, _ in jobs:
            begin = begins[j] - widths[0] if level == 1 and j else 0
            described.append((bits[level], parts[j], slice(begin, begin + widths[j])))
            sizes.append(widths[j])
        return call(
            functools.partial(levels_kernel, described),
            name,
            [VMEM] * len(args),
            [in_vmem(rank, size) for size in sizes],
            [in_vmem(2 * rank, size) for size in sizes],
            args,
            after,
            flops,
            through=through,
        )

    def job1(j):
        return (1, j, rest, near_rest) if j else (1, j, first, near_first)

    coeff2, near2, coeff3, near3 = {}, {}, {}, {}

    def second(j, value):
        coeff2[j] = value
        near2[j] = cross(2, value)

    def third(j, value):
        coeff3[j] = value
        near3[j] = cross(3, value)

    value, rest = step("level1_0", [job1(0)], through=[rest])
    near_rest = cross(1, rest)
    second(0, value)
    (value,) = step("level1_1", [job1(1)], [coeff2[0]])
    second(1, value)
    (value,) = step("level1_2", [job1(2)], [coeff2[1]])
    second(2, value)
    *more, basis_v = call(
        prefetch_kernel,
        "prefetch",
        [ANY] * 3,
        [pair] * (levels - 1 - PRELOADED) + [in_vmem(*basis.shape)],
        [pltpu.SMEM(index.shape, jnp.int32), pltpu.SemaphoreType.DMA((2 * levels,))],
        [in_hbm(blocks), in_hbm(basis), in_hbm(index)],
        [coeff2[2]],
    )
    weights += more
    (value,) = step("level2_0", [(2, 0, coeff2[0], near2[0])], [basis_v])
    third(0, value)
    (value,) = step("level2_1", [(2, 1, coeff2[1], near2[1])], [coeff3[0]])
    third(1, value)

    def tail(j, after, arrived=()):
        (coeff4,) = step(f"level3_{j}", [(3, j, coeff3[j], near3[j])], after)
        near4 = cross(4, coeff4)
        partial, *totals = call(
            functools.partial(between_kernel, bits[4], parts[j], [len(group) for _, group in arrived]),
            f"between_{j}",
            [VMEM] * (2 + sum(len(group) for _, group in arrived)),
            [in_vmem(rank, widths[j], dtype=F32)] + [in_vmem(rows, widths[at]) for at, _ in arrived],
            [],
            [here(v) for v in (coeff4, weights[4], *(v for _, group in arrived for v in group))],
        )
        out = call(
            functools.partial(last_kernel, bits[4], parts[j]),
            f"last_{j}",
            [VMEM] * 4,
            [in_vmem(rows, widths[j], dtype=F32)] + [in_vmem(rows, widths[j])] * (n_blk - 1),
            [],
            [here(v) for v in (partial, near4, weights[4], basis_v)],
            flops=COST if j < len(widths) - 1 else 0,
        )
        group = [out[0]] + [partner(out[d], "blk", d) for d in range(n_blk - 1, 0, -1)]
        return group, totals

    group0, _ = tail(0, [coeff3[1]])
    (value,) = step("level2_2", [(2, 2, coeff2[2], near2[2])], [group0[0]])
    third(2, value)
    (total0,) = call(
        sum_kernel,
        "sum_0",
        [VMEM] * n_blk,
        [in_vmem(rows, widths[0])],
        [],
        [here(v) for v in group0],
        [coeff3[2]],
    )
    (value,) = step("level1_3", [job1(3)], [total0])
    second(3, value)
    group1, _ = tail(1, [coeff2[3]])
    (value,) = step("level2_3", [(2, 3, coeff2[3], near2[3])], [group1[0]])
    third(3, value)
    group2, (total1,) = tail(2, [coeff3[3]], [(1, group1)])
    group3, _ = tail(3, [group2[0]])
    groups = [[total0], [total1], group2, group3]
    flat = [here(v) for group in groups for v in group]
    return pl.pallas_call(
        functools.partial(end_kernel, places, [len(group) for group in groups]),
        name="end",
        in_specs=[VMEM] * len(flat),
        out_specs=VMEM,
        out_shape=jax.ShapeDtypeStruct((slots, rows, columns), BF16),
        compiler_params=pltpu.CompilerParams(vmem_limit_bytes=8 * 2**20),
    )(*flat)


def solution(mesh):
    in_specs = (
        P("blk", "box", None, None),
        P("blk", "box", None, None),
        P("blk", None, "box", None, None),
        P("blk", None, "box"),
        P("blk", "box", None, None),
    )
    out_specs = P("box", "blk", None)
    return jax.shard_map(
        on_device, mesh=mesh, in_specs=in_specs, out_specs=out_specs, check_vma=False
    )
```

```python
import functools

import jax
import jax.numpy as jnp
from jax import lax
from jax.experimental import pallas as pl
from jax.experimental.pallas import tpu as pltpu
from jax.sharding import PartitionSpec as P

SHARES = (1, 2, 3, 2)
PRELOADED = 2
DEPTHS = 1
COST = 6 * 10**9
BF16 = jnp.bfloat16
F32 = jnp.float32
ANY = pl.BlockSpec(memory_space=pl.ANY)
VMEM = pl.BlockSpec(memory_space=pltpu.VMEM)


def dot(a, b):
    return jnp.dot(a, b, preferred_element_type=F32)


def in_vmem(*shape, dtype=BF16):
    return pltpu.VMEM(shape, dtype)


def here(value):
    return pltpu.with_memory_space_constraint(value, pltpu.VMEM)


def in_hbm(value):
    return pltpu.with_memory_space_constraint(value, pltpu.HBM)


def call(kernel, name, in_specs, out_shape, scratch, args, after=(), flops=COST, limit=8 * 2**20, through=()):
    count, outs = len(in_specs), len(out_shape)

    def body(*refs):
        held = refs[count + len(after) + len(through) :]
        kernel(*refs[:count], *held[:outs], *held[outs + len(through) :])

    return pl.pallas_call(
        body,
        name=name,
        in_specs=[*in_specs, *[ANY] * (len(after) + len(through))],
        out_specs=[VMEM] * outs + [ANY] * len(through),
        out_shape=[*out_shape, *[in_vmem(*v.shape, dtype=v.dtype) for v in through]],
        scratch_shapes=scratch,
        input_output_aliases={count + len(after) + at: outs + at for at in range(len(through))},
        compiler_params=pltpu.CompilerParams(vmem_limit_bytes=limit),
        cost_estimate=pl.CostEstimate(flops=flops, bytes_accessed=0, transcendentals=0),
    )(*args, *after, *[here(v) for v in through])


def partner(value, axis, mask):
    pairs = [(source, source ^ mask) for source in range(lax.axis_size(axis))]
    return lax.ppermute(value, axis, pairs)


def leaf_kernel(excite, leaves, blocks, index, first, rest, *refs):
    count = PRELOADED
    nexts = refs[:count]
    excite_v, leaves_v, blocks_v, index_s, coeff, sems = refs[count:]
    slots, rank = leaves.shape[0], leaves.shape[1]
    columns, width = excite.shape[2], first.shape[1]
    base = 1 + 2 * (1 + count)
    listing = pltpu.make_async_copy(index, index_s, sems.at[0])
    listing.start()
    loads = []
    depth = leaves.shape[2] // DEPTHS
    spans = [pl.ds(k * depth, depth) for k in range(DEPTHS)]
    for s in range(slots):
        for k, span in enumerate(spans):
            at = base + 2 * (s * DEPTHS + k)
            a = pltpu.make_async_copy(leaves.at[s, :, span], leaves_v.at[s, :, span], sems.at[at])
            b = pltpu.make_async_copy(excite.at[s, span], excite_v.at[s, span], sems.at[at + 1])
            a.start()
            b.start()
            loads.append((a, b))
    listing.wait()
    weights, later = [], []
    for s in range(slots):
        c = pltpu.make_async_copy(blocks.at[0, index_s[s, 0]], blocks_v.at[s], sems.at[1 + s])
        c.start()
        weights.append(c)
    for level in range(1, 1 + count):
        for s in range(slots):
            c = pltpu.make_async_copy(
                blocks.at[level, index_s[s, level]], nexts[level - 1].at[s], sems.at[1 + 2 * level + s]
            )
            c.start()
            later.append(c)
    for s in range(slots):
        total = None
        for k, span in enumerate(spans):
            for load in loads[s * DEPTHS + k]:
                load.wait()
            part = dot(leaves_v[s, :, span], excite_v[s, span])
            total = part if total is None else total + part
        coeff[s * rank : (s + 1) * rank, :] = total.astype(BF16)
    for s in range(slots):
        weights[s].wait()
        out = dot(blocks_v[s], coeff[...]).astype(BF16)
        if s == 0:
            first[...] = out[:, :width]
            rest[:, : columns - width] = out[:, width:]
        else:
            rest[:, s * columns - width : (s + 1) * columns - width] = out
    for c in later:
        c.wait()


def prefetch_kernel(blocks, basis, index, *refs):
    count = blocks.shape[0] - 1 - PRELOADED
    outs, basis_v, index_s, sems = refs[:count], refs[count], refs[count + 1], refs[count + 2]
    listing = pltpu.make_async_copy(index, index_s, sems.at[0])
    listing.start()
    c = pltpu.make_async_copy(basis, basis_v, sems.at[1 + 2 * count])
    c.start()
    copies = [c]
    listing.wait()
    for at in range(count):
        level = at + 1 + PRELOADED
        for s in range(2):
            c = pltpu.make_async_copy(blocks.at[level, index_s[s, level]], outs[at].at[s], sems.at[1 + 2 * at + s])
            c.start()
            copies.append(c)
    for c in copies:
        c.wait()


def upper_half(bit):
    return (lax.axis_index("box") >> bit) & 1


def mix(weights, own, other, bit, buf, parts, out):
    rank = own.shape[0]
    upper = upper_half(bit)
    buf[pl.ds(pl.multiple_of(upper * rank, rank), rank), :] = own
    buf[pl.ds(pl.multiple_of((1 - upper) * rank, rank), rank), :] = other
    for s, start, stop in parts:
        out[:, start:stop] = dot(weights[s], buf[:, start:stop]).astype(BF16)


def levels_kernel(jobs, *refs):
    count = len(jobs)
    ins, outs, bufs = refs[: 3 * count], refs[3 * count : 4 * count], refs[4 * count :]
    for at, (bit, parts, lanes) in enumerate(jobs):
        own, other, weights = ins[3 * at : 3 * at + 3]
        mix(weights, own[:, lanes], other[:, lanes], bit, bufs[at], parts, outs[at])


def half_dot(weights, s, half, value):
    rank = value.shape[0]
    return dot(weights[s, :, pl.ds(pl.multiple_of(half * rank, 128), rank)], value)


def sum_kernel(mine, *refs):
    total = mine[...]
    for piece in refs[:-1]:
        total = total + piece[...].astype(F32)
    refs[-1][...] = total.astype(BF16)


def between_kernel(bit, cuts, counts, weights, *refs):
    refs = list(refs)
    owns = [refs.pop(0) for _ in cuts]
    groups = [[refs.pop(0) for _ in range(count)] for count in counts]
    partial = refs.pop(0)
    for own, (begin, parts) in zip(owns, cuts):
        for s, start, stop in parts:
            partial[:, begin + start : begin + stop] = half_dot(
                weights, s, upper_half(bit), own[:, start:stop]
            )
    for group, out in zip(groups, refs):
        sum_kernel(*group, out)


def last_kernel(bit, cuts, partial, weights, basis, *refs):
    others, refs = refs[: len(cuts)], refs[len(cuts) :]
    rows = refs[0].shape[0]
    me = lax.axis_index("blk")
    for other, (begin, parts) in zip(others, cuts):
        for s, start, stop in parts:
            lanes = slice(begin + start, begin + stop)
            mixed = partial[:, lanes] + half_dot(weights, s, 1 - upper_half(bit), other[:, start:stop])
            coeff = mixed.astype(BF16)
            for d, ref in enumerate(refs):
                row = pl.multiple_of((me ^ d) * rows, rows)
                ref[:, lanes] = dot(basis[s, pl.ds(row, rows), :], coeff).astype(ref.dtype)


def end_kernel(places, counts, *refs):
    refs = list(refs)
    out = refs[-1]
    for place, count in zip(places, counts):
        group = [refs.pop(0) for _ in range(count)]
        for s, column, start, stop in place:
            total = group[0][:, start:stop].astype(F32)
            for piece in group[1:]:
                total = total + piece[:, start:stop].astype(F32)
            out[s, :, column : column + stop - start] = total.astype(BF16)


def on_device(excitation, leaf_basis, transfer, transfer_index, out_basis):
    excite, leaves, blocks, basis = excitation[0], leaf_basis[0], transfer[0], out_basis[0]
    index = transfer_index[0].T
    slots, rank, points = leaves.shape
    levels = blocks.shape[0]
    columns = excite.shape[2]
    n_blk = lax.axis_size("blk")
    rows = basis.shape[1] // n_blk
    nbits = lax.axis_size("box").bit_length() - 1
    bits = [None] + [(level - 1) % nbits for level in range(1, levels)]
    pair = in_vmem(slots, rank, 2 * rank)

    unit = slots * columns // sum(SHARES)
    widths = [unit * share for share in SHARES]
    begins = [sum(widths[:j]) for j in range(len(widths))]
    parts, places = [], []
    for begin, width in zip(begins, widths):
        part, place, lane = [], [], 0
        while lane < width:
            s, column = divmod(begin + lane, columns)
            size = min(width - lane, columns - column)
            part.append((s, lane, lane + size))
            place.append((s, column, lane, lane + size))
            lane += size
        parts.append(part)
        places.append(place)

    first, rest, *weights = call(
        leaf_kernel,
        "leaf",
        [ANY] * 4,
        [in_vmem(rank, widths[0]), in_vmem(rank, slots * columns - widths[0])] + [pair] * PRELOADED,
        [
            in_vmem(*excite.shape),
            in_vmem(*leaves.shape),
            pair,
            pltpu.SMEM(index.shape, jnp.int32),
            in_vmem(2 * rank, columns),
            pltpu.SemaphoreType.DMA((1 + 2 * (1 + PRELOADED) + 2 * slots * DEPTHS,)),
        ],
        [in_hbm(excite), in_hbm(leaves), in_hbm(blocks), in_hbm(index)],
        limit=24 * 2**20,
    )
    weights = [None, *weights]

    def cross(level, value):
        return partner(value, "box", 2 ** bits[level])

    near_first = cross(1, first)

    def within(j, begin, size):
        found = []
        for s, start, stop in parts[j]:
            start, stop = max(start - begin, 0), min(stop - begin, size)
            if start < stop:
                found.append((s, start, stop))
        return found

    def step(name, jobs, after=(), flops=COST, through=()):
        args = [here(v) for level, _, own, other, *_ in jobs for v in (own, other, weights[level])]
        described, sizes = [], []
        for level, j, _, _, *lanes in jobs:
            begin, size = lanes or (0, widths[j])
            part = within(j, begin, size)
            if level == 1 and j:
                begin += begins[j] - widths[0]
            described.append((bits[level], part, slice(begin, begin + size)))
            sizes.append(size)
        return call(
            functools.partial(levels_kernel, described),
            name,
            [VMEM] * len(args),
            [in_vmem(rank, size) for size in sizes],
            [in_vmem(2 * rank, size) for size in sizes],
            args,
            after,
            flops,
            through=through,
        )

    def job1(j):
        return (1, j, rest, near_rest) if j else (1, j, first, near_first)

    coeff2, near2, coeff3, near3 = {}, {}, {}, {}

    def second(j, value):
        coeff2[j] = value
        near2[j] = cross(2, value)

    def third(j, value):
        coeff3[j] = value
        near3[j] = cross(3, value)

    value, rest = step("level1_0", [job1(0)], through=[rest])
    near_rest = cross(1, rest)
    second(0, value)
    (value,) = step("level1_1", [job1(1)], [coeff2[0]])
    second(1, value)
    (value,) = step("level1_2", [job1(2)], [coeff2[1]])
    second(2, value)
    *more, basis_v = call(
        prefetch_kernel,
        "prefetch",
        [ANY] * 3,
        [pair] * (levels - 1 - PRELOADED) + [in_vmem(*basis.shape)],
        [pltpu.SMEM(index.shape, jnp.int32), pltpu.SemaphoreType.DMA((2 * levels,))],
        [in_hbm(blocks), in_hbm(basis), in_hbm(index)],
        [coeff2[2]],
    )
    weights += more
    (value,) = step("level2_0", [(2, 0, coeff2[0], near2[0])], [basis_v])
    third(0, value)
    (value,) = step("level2_1", [(2, 1, coeff2[1], near2[1])], [coeff3[0]])
    third(1, value)

    def tail(name, members, after, arrived=(), flops=COST, beside=COST, pieces=1):
        size = sum(widths[j] for j in members)
        cuts, jobs = [], []
        for j in members:
            lanes = widths[j] // pieces
            for at in range(0, widths[j], lanes):
                cuts.append((begins[j] - begins[members[0]] + at, within(j, at, lanes)))
                jobs.append((3, j, coeff3[j], near3[j], at, lanes))
        coeff4 = step(f"level3_{name}", jobs, after)
        near4 = [cross(4, value) for value in coeff4]
        partial, *totals = call(
            functools.partial(between_kernel, bits[4], cuts, [len(group) for _, group in arrived]),
            f"between_{name}",
            [VMEM] * (1 + len(cuts) + sum(len(group) for _, group in arrived)),
            [in_vmem(rank, size, dtype=F32)] + [in_vmem(rows, lanes) for lanes, _ in arrived],
            [],
            [here(v) for v in (weights[4], *coeff4, *(v for _, group in arrived for v in group))],
            flops=beside,
        )
        out = call(
            functools.partial(last_kernel, bits[4], cuts),
            f"last_{name}",
            [VMEM] * (3 + len(cuts)),
            [in_vmem(rows, size, dtype=F32)] + [in_vmem(rows, size)] * (n_blk - 1),
            [],
            [here(v) for v in (partial, weights[4], basis_v, *near4)],
            flops=flops,
        )
        group = [out[0]] + [partner(out[d], "blk", d) for d in range(n_blk - 1, 0, -1)]
        return (size, group), totals

    (value,) = step("level2_2", [(2, 2, coeff2[2], near2[2])], [coeff3[1]])
    third(2, value)
    (value,) = step("level1_3", [job1(3)], [coeff3[2]])
    second(3, value)
    group1, _ = tail("1", (0, 1), [coeff2[3]])
    (value,) = step("level2_3", [(2, 3, coeff2[3], near2[3])], [group1[1][0]])
    third(3, value)
    group2, (total1,) = tail("2", (2,), [coeff3[3]], [group1])
    group3, _ = tail("3", (3,), [group2[1][0]], flops=0, beside=10**9, pieces=2)
    places = [
        [
            (s, column, begins[j] - begins[members[0]] + start, begins[j] - begins[members[0]] + stop)
            for j in members
            for s, column, start, stop in places[j]
        ]
        for members in ((0, 1), (2,), (3,))
    ]
    groups = [[total1], group2[1], group3[1]]
    flat = [here(v) for group in groups for v in group]
    return pl.pallas_call(
        functools.partial(end_kernel, places, [len(group) for group in groups]),
        name="end",
        in_specs=[VMEM] * len(flat),
        out_specs=VMEM,
        out_shape=jax.ShapeDtypeStruct((slots, rows, columns), BF16),
        compiler_params=pltpu.CompilerParams(vmem_limit_bytes=8 * 2**20),
    )(*flat)


def solution(mesh):
    in_specs = (
        P("blk", "box", None, None),
        P("blk", "box", None, None),
        P("blk", None, "box", None, None),
        P("blk", None, "box"),
        P("blk", "box", None, None),
    )
    out_specs = P("box", "blk", None)
    return jax.shard_map(
        on_device, mesh=mesh, in_specs=in_specs, out_specs=out_specs, check_vma=False
    )
```

```python
import functools

import jax
import jax.numpy as jnp
from jax import lax
from jax.experimental import pallas as pl
from jax.experimental.pallas import tpu as pltpu
from jax.sharding import PartitionSpec as P

SHARES = (1, 2, 3, 2)
PRELOADED = 2
DEPTHS = 1
COST = 6 * 10**9
BF16 = jnp.bfloat16
F32 = jnp.float32
ANY = pl.BlockSpec(memory_space=pl.ANY)
VMEM = pl.BlockSpec(memory_space=pltpu.VMEM)


def dot(a, b):
    return jnp.dot(a, b, preferred_element_type=F32)


def in_vmem(*shape, dtype=BF16):
    return pltpu.VMEM(shape, dtype)


def here(value):
    return pltpu.with_memory_space_constraint(value, pltpu.VMEM)


def in_hbm(value):
    return pltpu.with_memory_space_constraint(value, pltpu.HBM)


def call(kernel, name, in_specs, out_shape, scratch, args, after=(), flops=COST, limit=8 * 2**20, through=()):
    count, outs = len(in_specs), len(out_shape)

    def body(*refs):
        held = refs[count + len(after) + len(through) :]
        kernel(*refs[:count], *held[:outs], *held[outs + len(through) :])

    return pl.pallas_call(
        body,
        name=name,
        in_specs=[*in_specs, *[ANY] * (len(after) + len(through))],
        out_specs=[VMEM] * outs + [ANY] * len(through),
        out_shape=[*out_shape, *[in_vmem(*v.shape, dtype=v.dtype) for v in through]],
        scratch_shapes=scratch,
        input_output_aliases={count + len(after) + at: outs + at for at in range(len(through))},
        compiler_params=pltpu.CompilerParams(vmem_limit_bytes=limit),
        cost_estimate=pl.CostEstimate(flops=flops, bytes_accessed=0, transcendentals=0),
    )(*args, *after, *[here(v) for v in through])


def partner(value, axis, mask):
    pairs = [(source, source ^ mask) for source in range(lax.axis_size(axis))]
    return lax.ppermute(value, axis, pairs)


def leaf_kernel(excite, leaves, blocks, index, first, rest, *refs):
    count = PRELOADED
    nexts = refs[:count]
    excite_v, leaves_v, blocks_v, index_s, coeff, sems = refs[count:]
    slots, rank = leaves.shape[0], leaves.shape[1]
    columns, width = excite.shape[2], first.shape[1]
    base = 1 + 2 * (1 + count)
    listing = pltpu.make_async_copy(index, index_s, sems.at[0])
    listing.start()
    loads = []
    depth = leaves.shape[2] // DEPTHS
    spans = [pl.ds(k * depth, depth) for k in range(DEPTHS)]
    for s in range(slots):
        for k, span in enumerate(spans):
            at = base + 2 * (s * DEPTHS + k)
            a = pltpu.make_async_copy(leaves.at[s, :, span], leaves_v.at[s, :, span], sems.at[at])
            b = pltpu.make_async_copy(excite.at[s, span], excite_v.at[s, span], sems.at[at + 1])
            a.start()
            b.start()
            loads.append((a, b))
    listing.wait()
    weights, later = [], []
    for s in range(slots):
        c = pltpu.make_async_copy(blocks.at[0, index_s[s, 0]], blocks_v.at[s], sems.at[1 + s])
        c.start()
        weights.append(c)
    for level in range(1, 1 + count):
        for s in range(slots):
            c = pltpu.make_async_copy(
                blocks.at[level, index_s[s, level]], nexts[level - 1].at[s], sems.at[1 + 2 * level + s]
            )
            c.start()
            later.append(c)
    for s in range(slots):
        total = None
        for k, span in enumerate(spans):
            for load in loads[s * DEPTHS + k]:
                load.wait()
            part = dot(leaves_v[s, :, span], excite_v[s, span])
            total = part if total is None else total + part
        coeff[s * rank : (s + 1) * rank, :] = total.astype(BF16)
    for s in range(slots):
        weights[s].wait()
        out = dot(blocks_v[s], coeff[...]).astype(BF16)
        if s == 0:
            first[...] = out[:, :width]
            rest[:, : columns - width] = out[:, width:]
        else:
            rest[:, s * columns - width : (s + 1) * columns - width] = out
    for c in later:
        c.wait()


def prefetch_kernel(blocks, basis, index, *refs):
    count = blocks.shape[0] - 1 - PRELOADED
    outs, basis_v, index_s, sems = refs[:count], refs[count], refs[count + 1], refs[count + 2]
    listing = pltpu.make_async_copy(index, index_s, sems.at[0])
    listing.start()
    c = pltpu.make_async_copy(basis, basis_v, sems.at[1 + 2 * count])
    c.start()
    copies = [c]
    listing.wait()
    for at in range(count):
        level = at + 1 + PRELOADED
        for s in range(2):
            c = pltpu.make_async_copy(blocks.at[level, index_s[s, level]], outs[at].at[s], sems.at[1 + 2 * at + s])
            c.start()
            copies.append(c)
    for c in copies:
        c.wait()


def upper_half(bit):
    return (lax.axis_index("box") >> bit) & 1


def mix(weights, own, other, bit, buf, parts, out):
    rank = own.shape[0]
    upper = upper_half(bit)
    buf[pl.ds(pl.multiple_of(upper * rank, rank), rank), :] = own
    buf[pl.ds(pl.multiple_of((1 - upper) * rank, rank), rank), :] = other
    for s, start, stop in parts:
        out[:, start:stop] = dot(weights[s], buf[:, start:stop]).astype(BF16)


def levels_kernel(jobs, *refs):
    count = len(jobs)
    ins, outs, bufs = refs[: 3 * count], refs[3 * count : 4 * count], refs[4 * count :]
    for at, (bit, parts, lanes) in enumerate(jobs):
        own, other, weights = ins[3 * at : 3 * at + 3]
        mix(weights, own[:, lanes], other[:, lanes], bit, bufs[at], parts, outs[at])


def half_dot(weights, s, half, value):
    rank = value.shape[0]
    return dot(weights[s, :, pl.ds(pl.multiple_of(half * rank, 128), rank)], value)


def sum_kernel(mine, *refs):
    total = mine[...]
    for piece in refs[:-1]:
        total = total + piece[...].astype(F32)
    refs[-1][...] = total.astype(BF16)


def between_kernel(bit, cuts, counts, weights, *refs):
    refs = list(refs)
    owns = [refs.pop(0) for _ in cuts]
    groups = [[refs.pop(0) for _ in range(count)] for count in counts]
    partial = refs.pop(0)
    for own, (begin, parts) in zip(owns, cuts):
        for s, start, stop in parts:
            partial[:, begin + start : begin + stop] = half_dot(
                weights, s, upper_half(bit), own[:, start:stop]
            )
    for group, out in zip(groups, refs):
        sum_kernel(*group, out)


def last_kernel(bit, cuts, partial, weights, basis, *refs):
    others, refs = refs[: len(cuts)], refs[len(cuts) :]
    rows = refs[0].shape[0]
    me = lax.axis_index("blk")
    for other, (begin, parts) in zip(others, cuts):
        for s, start, stop in parts:
            lanes = slice(begin + start, begin + stop)
            mixed = partial[:, lanes] + half_dot(weights, s, 1 - upper_half(bit), other[:, start:stop])
            coeff = mixed.astype(BF16)
            for d, ref in enumerate(refs):
                row = pl.multiple_of((me ^ d) * rows, rows)
                ref[:, lanes] = dot(basis[s, pl.ds(row, rows), :], coeff).astype(ref.dtype)


def end_kernel(places, counts, *refs):
    refs = list(refs)
    out = refs[-1]
    for place, count in zip(places, counts):
        group = [refs.pop(0) for _ in range(count)]
        for s, column, start, stop in place:
            total = group[0][:, start:stop].astype(F32)
            for piece in group[1:]:
                total = total + piece[:, start:stop].astype(F32)
            out[s, :, column : column + stop - start] = total.astype(BF16)


def on_device(excitation, leaf_basis, transfer, transfer_index, out_basis):
    excite, leaves, blocks, basis = excitation[0], leaf_basis[0], transfer[0], out_basis[0]
    index = transfer_index[0].T
    slots, rank, points = leaves.shape
    levels = blocks.shape[0]
    columns = excite.shape[2]
    n_blk = lax.axis_size("blk")
    rows = basis.shape[1] // n_blk
    nbits = lax.axis_size("box").bit_length() - 1
    bits = [None] + [(level - 1) % nbits for level in range(1, levels)]
    pair = in_vmem(slots, rank, 2 * rank)

    unit = slots * columns // sum(SHARES)
    widths = [unit * share for share in SHARES]
    begins = [sum(widths[:j]) for j in range(len(widths))]
    parts, places = [], []
    for begin, width in zip(begins, widths):
        part, place, lane = [], [], 0
        while lane < width:
            s, column = divmod(begin + lane, columns)
            size = min(width - lane, columns - column)
            part.append((s, lane, lane + size))
            place.append((s, column, lane, lane + size))
            lane += size
        parts.append(part)
        places.append(place)

    first, rest, *weights = call(
        leaf_kernel,
        "leaf",
        [ANY] * 4,
        [in_vmem(rank, widths[0]), in_vmem(rank, slots * columns - widths[0])] + [pair] * PRELOADED,
        [
            in_vmem(*excite.shape),
            in_vmem(*leaves.shape),
            pair,
            pltpu.SMEM(index.shape, jnp.int32),
            in_vmem(2 * rank, columns),
            pltpu.SemaphoreType.DMA((1 + 2 * (1 + PRELOADED) + 2 * slots * DEPTHS,)),
        ],
        [in_hbm(excite), in_hbm(leaves), in_hbm(blocks), in_hbm(index)],
        limit=24 * 2**20,
    )
    weights = [None, *weights]

    def cross(level, value):
        return partner(value, "box", 2 ** bits[level])

    near_first = cross(1, first)

    def within(j, begin, size):
        found = []
        for s, start, stop in parts[j]:
            start, stop = max(start - begin, 0), min(stop - begin, size)
            if start < stop:
                found.append((s, start, stop))
        return found

    def step(name, jobs, after=(), flops=COST, through=()):
        args = [here(v) for level, _, own, other, *_ in jobs for v in (own, other, weights[level])]
        described, sizes = [], []
        for level, j, _, _, *lanes in jobs:
            begin, size = lanes or (0, widths[j])
            part = within(j, begin, size)
            if level == 1 and j:
                begin += begins[j] - widths[0]
            described.append((bits[level], part, slice(begin, begin + size)))
            sizes.append(size)
        return call(
            functools.partial(levels_kernel, described),
            name,
            [VMEM] * len(args),
            [in_vmem(rank, size) for size in sizes],
            [in_vmem(2 * rank, size) for size in sizes],
            args,
            after,
            flops,
            through=through,
        )

    def job1(j):
        return (1, j, rest, near_rest) if j else (1, j, first, near_first)

    coeff2, near2, coeff3, near3 = {}, {}, {}, {}

    def second(j, value):
        coeff2[j] = value
        near2[j] = cross(2, value)

    def third(j, value):
        coeff3[j] = value
        near3[j] = cross(3, value)

    value, rest = step("level1_0", [job1(0)], through=[rest])
    near_rest = cross(1, rest)
    second(0, value)
    (value,) = step("level1_1", [job1(1)], [coeff2[0]])
    second(1, value)
    (value,) = step("level1_2", [job1(2)], [coeff2[1]])
    second(2, value)
    *more, basis_v = call(
        prefetch_kernel,
        "prefetch",
        [ANY] * 3,
        [pair] * (levels - 1 - PRELOADED) + [in_vmem(*basis.shape)],
        [pltpu.SMEM(index.shape, jnp.int32), pltpu.SemaphoreType.DMA((2 * levels,))],
        [in_hbm(blocks), in_hbm(basis), in_hbm(index)],
        [coeff2[2]],
    )
    weights += more
    (value,) = step("level2_0", [(2, 0, coeff2[0], near2[0])], [basis_v])
    third(0, value)
    (value,) = step("level2_1", [(2, 1, coeff2[1], near2[1])], [coeff3[0]])
    third(1, value)

    def tail(name, members, after, arrived=(), flops=COST, beside=COST, pieces=1):
        size = sum(widths[j] for j in members)
        cuts, jobs = [], []
        for j in members:
            lanes = widths[j] // pieces
            for at in range(0, widths[j], lanes):
                cuts.append((begins[j] - begins[members[0]] + at, within(j, at, lanes)))
                jobs.append((3, j, coeff3[j], near3[j], at, lanes))
        coeff4 = step(f"level3_{name}", jobs, after)
        near4 = [cross(4, value) for value in coeff4]
        partial, *totals = call(
            functools.partial(between_kernel, bits[4], cuts, [len(group) for _, group in arrived]),
            f"between_{name}",
            [VMEM] * (1 + len(cuts) + sum(len(group) for _, group in arrived)),
            [in_vmem(rank, size, dtype=F32)] + [in_vmem(rows, lanes) for lanes, _ in arrived],
            [],
            [here(v) for v in (weights[4], *coeff4, *(v for _, group in arrived for v in group))],
            flops=beside,
        )
        out = call(
            functools.partial(last_kernel, bits[4], cuts),
            f"last_{name}",
            [VMEM] * (3 + len(cuts)),
            [in_vmem(rows, size, dtype=F32)] + [in_vmem(rows, size)] * (n_blk - 1),
            [],
            [here(v) for v in (partial, weights[4], basis_v, *near4)],
            flops=flops,
        )
        group = [out[0]] + [partner(out[d], "blk", d) for d in range(n_blk - 1, 0, -1)]
        return (size, group), totals

    (value,) = step("level1_3", [job1(3)], [coeff3[1], near2[2]])
    second(3, value)
    (value,) = step("level2_2", [(2, 2, coeff2[2], near2[2])], [coeff2[3]])
    third(2, value)
    group1, _ = tail("1", (0, 1), [coeff3[2]])
    (value,) = step("level2_3", [(2, 3, coeff2[3], near2[3])], [group1[1][0]])
    third(3, value)
    group2, (total1,) = tail("2", (2,), [coeff3[3]], [group1])
    group3, _ = tail("3", (3,), [group2[1][0]], flops=0, beside=10**9, pieces=2)
    places = [
        [
            (s, column, begins[j] - begins[members[0]] + start, begins[j] - begins[members[0]] + stop)
            for j in members
            for s, column, start, stop in places[j]
        ]
        for members in ((0, 1), (2,), (3,))
    ]
    groups = [[total1], group2[1], group3[1]]
    flat = [here(v) for group in groups for v in group]
    return pl.pallas_call(
        functools.partial(end_kernel, places, [len(group) for group in groups]),
        name="end",
        in_specs=[VMEM] * len(flat),
        out_specs=VMEM,
        out_shape=jax.ShapeDtypeStruct((slots, rows, columns), BF16),
        compiler_params=pltpu.CompilerParams(vmem_limit_bytes=8 * 2**20),
    )(*flat)


def solution(mesh):
    in_specs = (
        P("blk", "box", None, None),
        P("blk", "box", None, None),
        P("blk", None, "box", None, None),
        P("blk", None, "box"),
        P("blk", "box", None, None),
    )
    out_specs = P("box", "blk", None)
    return jax.shard_map(
        on_device, mesh=mesh, in_specs=in_specs, out_specs=out_specs, check_vma=False
    )
```

```python
import functools

import jax
import jax.numpy as jnp
from jax import lax
from jax.experimental import pallas as pl
from jax.experimental.pallas import tpu as pltpu
from jax.sharding import PartitionSpec as P

SHARES = (1, 3, 3, 1)
PRELOADED = 2
COST = 6 * 10**9
BF16 = jnp.bfloat16
F32 = jnp.float32
ANY = pl.BlockSpec(memory_space=pl.ANY)
VMEM = pl.BlockSpec(memory_space=pltpu.VMEM)


def dot(a, b):
    return jnp.dot(a, b, preferred_element_type=F32)


def in_vmem(*shape, dtype=BF16):
    return pltpu.VMEM(shape, dtype)


def here(value):
    return pltpu.with_memory_space_constraint(value, pltpu.VMEM)


def in_hbm(value):
    return pltpu.with_memory_space_constraint(value, pltpu.HBM)


def call(kernel, name, in_specs, out_shape, scratch, args, after=(), flops=COST, limit=8 * 2**20):
    count = len(in_specs)

    def body(*refs):
        kernel(*refs[:count], *refs[count + len(after) :])

    return pl.pallas_call(
        body,
        name=name,
        in_specs=[*in_specs, *[ANY] * len(after)],
        out_specs=[VMEM] * len(out_shape),
        out_shape=out_shape,
        scratch_shapes=scratch,
        compiler_params=pltpu.CompilerParams(vmem_limit_bytes=limit),
        cost_estimate=pl.CostEstimate(flops=flops, bytes_accessed=0, transcendentals=0),
    )(*args, *after)


def partner(value, axis, mask):
    pairs = [(source, source ^ mask) for source in range(lax.axis_size(axis))]
    return lax.ppermute(value, axis, pairs)


def leaf_kernel(excite, leaves, blocks, index, first, rest, *refs):
    count = PRELOADED
    nexts = refs[:count]
    excite_v, leaves_v, blocks_v, index_s, coeff, sems = refs[count:]
    slots, rank = leaves.shape[0], leaves.shape[1]
    columns, width = excite.shape[2], first.shape[1]
    listing = pltpu.make_async_copy(index, index_s, sems.at[0])
    listing.start()
    loads = []
    for s in range(slots):
        a = pltpu.make_async_copy(leaves.at[s], leaves_v.at[s], sems.at[1 + s])
        b = pltpu.make_async_copy(excite.at[s], excite_v.at[s], sems.at[3 + s])
        a.start()
        b.start()
        loads.append((a, b))
    listing.wait()
    weights, later = [], []
    for s in range(slots):
        c = pltpu.make_async_copy(blocks.at[0, index_s[s, 0]], blocks_v.at[s], sems.at[5 + s])
        c.start()
        weights.append(c)
    for level in range(1, 1 + count):
        for s in range(slots):
            c = pltpu.make_async_copy(
                blocks.at[level, index_s[s, level]], nexts[level - 1].at[s], sems.at[5 + 2 * level + s]
            )
            c.start()
            later.append(c)
    for s in range(slots):
        for load in loads[s]:
            load.wait()
        coeff[s * rank : (s + 1) * rank, :] = dot(leaves_v[s], excite_v[s]).astype(BF16)
    for s in range(slots):
        weights[s].wait()
        out = dot(blocks_v[s], coeff[...]).astype(BF16)
        if s == 0:
            first[...] = out[:, :width]
            rest[:, : columns - width] = out[:, width:]
        else:
            rest[:, s * columns - width : (s + 1) * columns - width] = out
    for c in later:
        c.wait()


def prefetch_kernel(blocks, basis, index, *refs):
    count = blocks.shape[0] - 1 - PRELOADED
    outs, basis_v, index_s, sems = refs[:count], refs[count], refs[count + 1], refs[count + 2]
    listing = pltpu.make_async_copy(index, index_s, sems.at[0])
    listing.start()
    c = pltpu.make_async_copy(basis, basis_v, sems.at[1 + 2 * count])
    c.start()
    copies = [c]
    listing.wait()
    for at in range(count):
        level = at + 1 + PRELOADED
        for s in range(2):
            c = pltpu.make_async_copy(blocks.at[level, index_s[s, level]], outs[at].at[s], sems.at[1 + 2 * at + s])
            c.start()
            copies.append(c)
    for c in copies:
        c.wait()


def upper_half(bit):
    return (lax.axis_index("box") >> bit) & 1


def mix(weights, own, other, bit, buf, parts, out):
    rank = own.shape[0]
    upper = upper_half(bit)
    buf[pl.ds(pl.multiple_of(upper * rank, rank), rank), :] = own
    buf[pl.ds(pl.multiple_of((1 - upper) * rank, rank), rank), :] = other
    for s, start, stop in parts:
        out[:, start:stop] = dot(weights[s], buf[:, start:stop]).astype(BF16)


def levels_kernel(jobs, *refs):
    count = len(jobs)
    ins, outs, bufs = refs[: 3 * count], refs[3 * count : 4 * count], refs[4 * count :]
    for at, (bit, parts, lanes) in enumerate(jobs):
        own, other, weights = ins[3 * at : 3 * at + 3]
        mix(weights, own[:, lanes], other[:, lanes], bit, bufs[at], parts, outs[at])


def half_dot(weights, s, half, value):
    rank = value.shape[0]
    return dot(weights[s, :, pl.ds(pl.multiple_of(half * rank, 128), rank)], value)


def sum_kernel(mine, *refs):
    total = mine[...]
    for piece in refs[:-1]:
        total = total + piece[...].astype(F32)
    refs[-1][...] = total.astype(BF16)


def between_kernel(bit, parts, counts, own, weights, *refs):
    refs = list(refs)
    groups = [[refs.pop(0) for _ in range(count)] for count in counts]
    partial = refs.pop(0)
    for s, start, stop in parts:
        partial[:, start:stop] = half_dot(weights, s, upper_half(bit), own[:, start:stop])
    for group, out in zip(groups, refs):
        sum_kernel(*group, out)


def last_kernel(bit, parts, partial, other, weights, basis, *refs):
    rows = refs[0].shape[0]
    me = lax.axis_index("blk")
    for s, start, stop in parts:
        mixed = partial[:, start:stop] + half_dot(weights, s, 1 - upper_half(bit), other[:, start:stop])
        coeff = mixed.astype(BF16)
        for d, ref in enumerate(refs):
            row = pl.multiple_of((me ^ d) * rows, rows)
            ref[:, start:stop] = dot(basis[s, pl.ds(row, rows), :], coeff).astype(ref.dtype)


def end_kernel(places, counts, *refs):
    refs = list(refs)
    out = refs[-1]
    for place, count in zip(places, counts):
        group = [refs.pop(0) for _ in range(count)]
        for s, column, start, stop in place:
            total = group[0][:, start:stop].astype(F32)
            for piece in group[1:]:
                total = total + piece[:, start:stop].astype(F32)
            out[s, :, column : column + stop - start] = total.astype(BF16)


def on_device(excitation, leaf_basis, transfer, transfer_index, out_basis):
    excite, leaves, blocks, basis = excitation[0], leaf_basis[0], transfer[0], out_basis[0]
    index = transfer_index[0].T
    slots, rank, points = leaves.shape
    levels = blocks.shape[0]
    columns = excite.shape[2]
    n_blk = lax.axis_size("blk")
    rows = basis.shape[1] // n_blk
    nbits = lax.axis_size("box").bit_length() - 1
    bits = [None] + [(level - 1) % nbits for level in range(1, levels)]
    pair = in_vmem(slots, rank, 2 * rank)

    unit = slots * columns // sum(SHARES)
    widths = [unit * share for share in SHARES]
    begins = [sum(widths[:j]) for j in range(len(widths))]
    parts, places = [], []
    for begin, width in zip(begins, widths):
        part, place, lane = [], [], 0
        while lane < width:
            s, column = divmod(begin + lane, columns)
            size = min(width - lane, columns - column)
            part.append((s, lane, lane + size))
            place.append((s, column, lane, lane + size))
            lane += size
        parts.append(part)
        places.append(place)

    first, rest, *weights = call(
        leaf_kernel,
        "leaf",
        [ANY] * 4,
        [in_vmem(rank, widths[0]), in_vmem(rank, slots * columns - widths[0])] + [pair] * PRELOADED,
        [
            in_vmem(*excite.shape),
            in_vmem(*leaves.shape),
            pair,
            pltpu.SMEM(index.shape, jnp.int32),
            in_vmem(2 * rank, columns),
            pltpu.SemaphoreType.DMA((7 + 2 * PRELOADED,)),
        ],
        [in_hbm(excite), in_hbm(leaves), in_hbm(blocks), in_hbm(index)],
        limit=24 * 2**20,
    )
    weights = [None, *weights]

    def cross(level, value):
        return partner(value, "box", 2 ** bits[level])

    near_first, near_rest = cross(1, first), cross(1, rest)

    def step(name, jobs, after=(), flops=COST):
        args = [here(v) for level, j, own, other in jobs for v in (own, other, weights[level])]
        described, sizes = [], []
        for level, j, _, _ in jobs:
            begin = begins[j] - widths[0] if level == 1 and j else 0
            described.append((bits[level], parts[j], slice(begin, begin + widths[j])))
            sizes.append(widths[j])
        return call(
            functools.partial(levels_kernel, described),
            name,
            [VMEM] * len(args),
            [in_vmem(rank, size) for size in sizes],
            [in_vmem(2 * rank, size) for size in sizes],
            args,
            after,
            flops,
        )

    def job1(j):
        return (1, j, rest, near_rest) if j else (1, j, first, near_first)

    coeff2, near2, coeff3, near3 = {}, {}, {}, {}

    def second(j, value):
        coeff2[j] = value
        near2[j] = cross(2, value)

    def third(j, value):
        coeff3[j] = value
        near3[j] = cross(3, value)

    (value,) = step("level1_0", [job1(0)])
    second(0, value)
    (value,) = step("level1_1", [job1(1)], [coeff2[0]])
    second(1, value)
    (value,) = step("level2_0", [(2, 0, coeff2[0], near2[0])], [coeff2[1]])
    third(0, value)
    (value,) = step("level1_2", [job1(2)], [coeff3[0]])
    second(2, value)
    *more, basis_v = call(
        prefetch_kernel,
        "prefetch",
        [ANY] * 3,
        [pair] * (levels - 1 - PRELOADED) + [in_vmem(*basis.shape)],
        [pltpu.SMEM(index.shape, jnp.int32), pltpu.SemaphoreType.DMA((2 * levels,))],
        [in_hbm(blocks), in_hbm(basis), in_hbm(index)],
        [coeff2[2]],
    )
    weights += more
    (value,) = step("level2_1", [(2, 1, coeff2[1], near2[1])], [basis_v])
    third(1, value)

    def tail(j, after, arrived=()):
        (coeff4,) = step(f"level3_{j}", [(3, j, coeff3[j], near3[j])], after)
        near4 = cross(4, coeff4)
        partial, *totals = call(
            functools.partial(between_kernel, bits[4], parts[j], [len(group) for _, group in arrived]),
            f"between_{j}",
            [VMEM] * (2 + sum(len(group) for _, group in arrived)),
            [in_vmem(rank, widths[j], dtype=F32)] + [in_vmem(rows, widths[at]) for at, _ in arrived],
            [],
            [here(v) for v in (coeff4, weights[4], *(v for _, group in arrived for v in group))],
        )
        out = call(
            functools.partial(last_kernel, bits[4], parts[j]),
            f"last_{j}",
            [VMEM] * 4,
            [in_vmem(rows, widths[j], dtype=F32)] + [in_vmem(rows, widths[j])] * (n_blk - 1),
            [],
            [here(v) for v in (partial, near4, weights[4], basis_v)],
            flops=COST if j < len(widths) - 1 else 0,
        )
        group = [out[0]] + [partner(out[d], "blk", d) for d in range(n_blk - 1, 0, -1)]
        return group, totals

    group0, _ = tail(0, [coeff3[1]])
    (value,) = step("level2_2", [(2, 2, coeff2[2], near2[2])], [group0[0]])
    third(2, value)
    (total0,) = call(
        sum_kernel,
        "sum_0",
        [VMEM] * n_blk,
        [in_vmem(rows, widths[0])],
        [],
        [here(v) for v in group0],
        [coeff3[2]],
    )
    (value,) = step("level1_3", [job1(3)], [total0])
    second(3, value)
    group1, _ = tail(1, [coeff2[3]])
    (value,) = step("level2_3", [(2, 3, coeff2[3], near2[3])], [group1[0]])
    third(3, value)
    group2, (total1,) = tail(2, [coeff3[3]], [(1, group1)])
    group3, _ = tail(3, [group2[0]])
    (total2,) = call(
        sum_kernel,
        "sum_2",
        [VMEM] * n_blk,
        [in_vmem(rows, widths[2])],
        [],
        [here(v) for v in group2],
        [group3[0]],
        0,
    )
    groups = [[total0], [total1], [total2], group3]
    flat = [here(v) for group in groups for v in group]
    return pl.pallas_call(
        functools.partial(end_kernel, places, [len(group) for group in groups]),
        name="end",
        in_specs=[VMEM] * len(flat),
        out_specs=VMEM,
        out_shape=jax.ShapeDtypeStruct((slots, rows, columns), BF16),
        compiler_params=pltpu.CompilerParams(vmem_limit_bytes=8 * 2**20),
    )(*flat)


def solution(mesh):
    in_specs = (
        P("blk", "box", None, None),
        P("blk", "box", None, None),
        P("blk", None, "box", None, None),
        P("blk", None, "box"),
        P("blk", "box", None, None),
    )
    out_specs = P("box", "blk", None)
    return jax.shard_map(
        on_device, mesh=mesh, in_specs=in_specs, out_specs=out_specs, check_vma=False
    )
```

```python
import functools

import jax
import jax.numpy as jnp
from jax import lax
from jax.experimental import pallas as pl
from jax.experimental.pallas import tpu as pltpu
from jax.sharding import PartitionSpec as P

SHARES = (1, 2, 3, 2)
PRELOADED = 2
COST = 6 * 10**9
BF16 = jnp.bfloat16
F32 = jnp.float32
ANY = pl.BlockSpec(memory_space=pl.ANY)
VMEM = pl.BlockSpec(memory_space=pltpu.VMEM)


def dot(a, b):
    return jnp.dot(a, b, preferred_element_type=F32)


def in_vmem(*shape, dtype=BF16):
    return pltpu.VMEM(shape, dtype)


def here(value):
    return pltpu.with_memory_space_constraint(value, pltpu.VMEM)


def in_hbm(value):
    return pltpu.with_memory_space_constraint(value, pltpu.HBM)


def call(kernel, name, in_specs, out_shape, scratch, args, after=(), flops=COST, limit=8 * 2**20):
    count = len(in_specs)

    def body(*refs):
        kernel(*refs[:count], *refs[count + len(after) :])

    return pl.pallas_call(
        body,
        name=name,
        in_specs=[*in_specs, *[ANY] * len(after)],
        out_specs=[VMEM] * len(out_shape),
        out_shape=out_shape,
        scratch_shapes=scratch,
        compiler_params=pltpu.CompilerParams(vmem_limit_bytes=limit),
        cost_estimate=pl.CostEstimate(flops=flops, bytes_accessed=0, transcendentals=0),
    )(*args, *after)


def partner(value, axis, mask):
    pairs = [(source, source ^ mask) for source in range(lax.axis_size(axis))]
    return lax.ppermute(value, axis, pairs)


def leaf_kernel(excite, leaves, blocks, index, first, rest, *refs):
    count = PRELOADED
    nexts = refs[:count]
    excite_v, leaves_v, blocks_v, index_s, coeff, sems = refs[count:]
    slots, rank = leaves.shape[0], leaves.shape[1]
    columns, width = excite.shape[2], first.shape[1]
    listing = pltpu.make_async_copy(index, index_s, sems.at[0])
    listing.start()
    loads = []
    for s in range(slots):
        a = pltpu.make_async_copy(leaves.at[s], leaves_v.at[s], sems.at[1 + s])
        b = pltpu.make_async_copy(excite.at[s], excite_v.at[s], sems.at[3 + s])
        a.start()
        b.start()
        loads.append((a, b))
    listing.wait()
    weights, later = [], []
    for s in range(slots):
        c = pltpu.make_async_copy(blocks.at[0, index_s[s, 0]], blocks_v.at[s], sems.at[5 + s])
        c.start()
        weights.append(c)
    for level in range(1, 1 + count):
        for s in range(slots):
            c = pltpu.make_async_copy(
                blocks.at[level, index_s[s, level]], nexts[level - 1].at[s], sems.at[5 + 2 * level + s]
            )
            c.start()
            later.append(c)
    for s in range(slots):
        for load in loads[s]:
            load.wait()
        coeff[s * rank : (s + 1) * rank, :] = dot(leaves_v[s], excite_v[s]).astype(BF16)
    for s in range(slots):
        weights[s].wait()
        out = dot(blocks_v[s], coeff[...]).astype(BF16)
        if s == 0:
            first[...] = out[:, :width]
            rest[:, : columns - width] = out[:, width:]
        else:
            rest[:, s * columns - width : (s + 1) * columns - width] = out
    for c in later:
        c.wait()


def prefetch_kernel(blocks, basis, index, *refs):
    count = blocks.shape[0] - 1 - PRELOADED
    outs, basis_v, index_s, sems = refs[:count], refs[count], refs[count + 1], refs[count + 2]
    listing = pltpu.make_async_copy(index, index_s, sems.at[0])
    listing.start()
    c = pltpu.make_async_copy(basis, basis_v, sems.at[1 + 2 * count])
    c.start()
    copies = [c]
    listing.wait()
    for at in range(count):
        level = at + 1 + PRELOADED
        for s in range(2):
            c = pltpu.make_async_copy(blocks.at[level, index_s[s, level]], outs[at].at[s], sems.at[1 + 2 * at + s])
            c.start()
            copies.append(c)
    for c in copies:
        c.wait()


def upper_half(bit):
    return (lax.axis_index("box") >> bit) & 1


def mix(weights, own, other, bit, buf, parts, out):
    rank = own.shape[0]
    upper = upper_half(bit)
    buf[pl.ds(pl.multiple_of(upper * rank, rank), rank), :] = own
    buf[pl.ds(pl.multiple_of((1 - upper) * rank, rank), rank), :] = other
    for s, start, stop in parts:
        out[:, start:stop] = dot(weights[s], buf[:, start:stop]).astype(BF16)


def levels_kernel(jobs, *refs):
    count = len(jobs)
    ins, outs, bufs = refs[: 3 * count], refs[3 * count : 4 * count], refs[4 * count :]
    for at, (bit, parts, lanes) in enumerate(jobs):
        own, other, weights = ins[3 * at : 3 * at + 3]
        mix(weights, own[:, lanes], other[:, lanes], bit, bufs[at], parts, outs[at])


def half_dot(weights, s, half, value):
    rank = value.shape[0]
    return dot(weights[s, :, pl.ds(pl.multiple_of(half * rank, 128), rank)], value)


def sum_kernel(mine, *refs):
    total = mine[...]
    for piece in refs[:-1]:
        total = total + piece[...].astype(F32)
    refs[-1][...] = total.astype(BF16)


def between_kernel(bit, parts, counts, folds, own, weights, *refs):
    refs = list(refs)
    groups = [[refs.pop(0) for _ in range(count)] for count in counts]
    held = [refs.pop(0) for _ in range(2 * folds)]
    partial = refs.pop(0)
    for s, start, stop in parts:
        partial[:, start:stop] = half_dot(weights, s, upper_half(bit), own[:, start:stop])
    for group in groups:
        sum_kernel(*group, refs.pop(0))
    fold_kernel(*held, *refs)


def fold_kernel(*refs):
    half = len(refs) // 2
    for at in range(0, half, 2):
        keep, got, rest, send = refs[at], refs[at + 1], refs[half + at], refs[half + at + 1]
        rows = rest.shape[0]
        rest[...] = keep[:rows] + got[:rows].astype(F32)
        send[...] = (keep[rows:] + got[rows:].astype(F32)).astype(BF16)


def join_kernel(*refs):
    out, row = refs[-1], 0
    for keep, got in zip(refs[:-1:2], refs[1:-1:2]):
        out[row : row + keep.shape[0], :] = (keep[...] + got[...].astype(F32)).astype(BF16)
        row += keep.shape[0]


def last_kernel(bit, parts, homes, partial, other, weights, basis, *refs):
    rows = basis.shape[1] // lax.axis_size("blk")
    me = lax.axis_index("blk")
    for s, start, stop in parts:
        mixed = partial[:, start:stop] + half_dot(weights, s, 1 - upper_half(bit), other[:, start:stop])
        coeff = mixed.astype(BF16)
        for d, home in enumerate(homes):
            row = pl.multiple_of((me ^ d) * rows, rows)
            piece = dot(basis[s, pl.ds(row, rows), :], coeff)
            for begin, size, at, to in home:
                ref = refs[at]
                ref[to : to + size, start:stop] = piece[begin : begin + size].astype(ref.dtype)


def end_kernel(places, counts, *refs):
    refs = list(refs)
    out = refs[-1]
    for place, count in zip(places, counts):
        group = [refs.pop(0) for _ in range(count)]
        for s, column, start, stop in place:
            total = group[0][:, start:stop].astype(F32)
            for piece in group[1:]:
                total = total + piece[:, start:stop].astype(F32)
            out[s, :, column : column + stop - start] = total.astype(BF16)


def on_device(excitation, leaf_basis, transfer, transfer_index, out_basis):
    excite, leaves, blocks, basis = excitation[0], leaf_basis[0], transfer[0], out_basis[0]
    index = transfer_index[0].T
    slots, rank, points = leaves.shape
    levels = blocks.shape[0]
    columns = excite.shape[2]
    n_blk = lax.axis_size("blk")
    rows = basis.shape[1] // n_blk
    nbits = lax.axis_size("box").bit_length() - 1
    bits = [None] + [(level - 1) % nbits for level in range(1, levels)]
    pair = in_vmem(slots, rank, 2 * rank)

    unit = slots * columns // sum(SHARES)
    widths = [unit * share for share in SHARES]
    begins = [sum(widths[:j]) for j in range(len(widths))]
    parts, places = [], []
    for begin, width in zip(begins, widths):
        part, place, lane = [], [], 0
        while lane < width:
            s, column = divmod(begin + lane, columns)
            size = min(width - lane, columns - column)
            part.append((s, lane, lane + size))
            place.append((s, column, lane, lane + size))
            lane += size
        parts.append(part)
        places.append(place)

    first, rest, *weights = call(
        leaf_kernel,
        "leaf",
        [ANY] * 4,
        [in_vmem(rank, widths[0]), in_vmem(rank, slots * columns - widths[0])] + [pair] * PRELOADED,
        [
            in_vmem(*excite.shape),
            in_vmem(*leaves.shape),
            pair,
            pltpu.SMEM(index.shape, jnp.int32),
            in_vmem(2 * rank, columns),
            pltpu.SemaphoreType.DMA((7 + 2 * PRELOADED,)),
        ],
        [in_hbm(excite), in_hbm(leaves), in_hbm(blocks), in_hbm(index)],
        limit=24 * 2**20,
    )
    weights = [None, *weights]

    def cross(level, value):
        return partner(value, "box", 2 ** bits[level])

    near_first, near_rest = cross(1, first), cross(1, rest)

    def step(name, jobs, after=(), flops=COST):
        args = [here(v) for level, j, own, other in jobs for v in (own, other, weights[level])]
        described, sizes = [], []
        for level, j, _, _ in jobs:
            begin = begins[j] - widths[0] if level == 1 and j else 0
            described.append((bits[level], parts[j], slice(begin, begin + widths[j])))
            sizes.append(widths[j])
        return call(
            functools.partial(levels_kernel, described),
            name,
            [VMEM] * len(args),
            [in_vmem(rank, size) for size in sizes],
            [in_vmem(2 * rank, size) for size in sizes],
            args,
            after,
            flops,
        )

    def job1(j):
        return (1, j, rest, near_rest) if j else (1, j, first, near_first)

    coeff2, near2, coeff3, near3 = {}, {}, {}, {}

    def second(j, value):
        coeff2[j] = value
        near2[j] = cross(2, value)

    def third(j, value):
        coeff3[j] = value
        near3[j] = cross(3, value)

    (value,) = step("level1_0", [job1(0)])
    second(0, value)
    (value,) = step("level1_1", [job1(1)], [coeff2[0]])
    second(1, value)
    (value,) = step("level2_0", [(2, 0, coeff2[0], near2[0])], [coeff2[1]])
    third(0, value)
    (value,) = step("level1_2", [job1(2)], [coeff3[0]])
    second(2, value)
    *more, basis_v = call(
        prefetch_kernel,
        "prefetch",
        [ANY] * 3,
        [pair] * (levels - 1 - PRELOADED) + [in_vmem(*basis.shape)],
        [pltpu.SMEM(index.shape, jnp.int32), pltpu.SemaphoreType.DMA((2 * levels,))],
        [in_hbm(blocks), in_hbm(basis), in_hbm(index)],
        [coeff2[2]],
    )
    weights += more
    (value,) = step("level2_1", [(2, 1, coeff2[1], near2[1])], [basis_v])
    third(1, value)

    masks = [1 << b for b in range(n_blk.bit_length() - 1)]
    orders = [masks, masks[::-1]]
    half = rows // 2
    whole = [[(0, rows, d, 0)] for d in range(n_blk)]
    halved = [[] for _ in range(n_blk)]
    for side, order in enumerate(orders):
        pieces = [0]
        for mask in order[::-1]:
            pieces = pieces + [d | mask for d in pieces]
        for at, d in enumerate(pieces):
            sent, to = divmod(at, n_blk // 2)
            halved[d].append((side * half, half, 2 * side + sent, to * half))

    def halves(j, count):
        shape = (count * half, widths[j])
        return [in_vmem(*shape, dtype=kind) for _ in orders for kind in (F32, BF16)]

    def exchange(values, at):
        return [
            v
            for side, order in enumerate(orders)
            for v in (values[2 * side], partner(values[2 * side + 1], "blk", order[at]))
        ]

    def begin_sum(j, out):
        held, count = exchange(out, 0), n_blk // 2
        for at in range(1, len(masks) - 1):
            count //= 2
            out = call(
                fold_kernel, f"fold_{j}_{at}", [VMEM] * 4, halves(j, count), [], [here(v) for v in held]
            )
            held = exchange(out, at)
        return held

    def tail(j, after, arrived=(), folding=(), halving=False):
        (coeff4,) = step(f"level3_{j}", [(3, j, coeff3[j], near3[j])], after)
        near4 = cross(4, coeff4)
        held = folding[1] if folding else []
        extra = [v for _, group in arrived for v in group] + held
        partial, *more = call(
            functools.partial(
                between_kernel, bits[4], parts[j], [len(group) for _, group in arrived], len(held) // 2
            ),
            f"between_{j}",
            [VMEM] * (2 + len(extra)),
            [in_vmem(rank, widths[j], dtype=F32)]
            + [in_vmem(rows, widths[at]) for at, _ in arrived]
            + (halves(folding[0], 1) if folding else []),
            [],
            [here(v) for v in (coeff4, weights[4], *extra)],
        )
        if halving:
            outs = halves(j, n_blk // 2)
        else:
            outs = [in_vmem(rows, widths[j], dtype=BF16 if d else F32) for d in range(n_blk)]
        out = call(
            functools.partial(last_kernel, bits[4], parts[j], halved if halving else whole),
            f"last_{j}",
            [VMEM] * 4,
            outs,
            [],
            [here(v) for v in (partial, near4, weights[4], basis_v)],
            flops=COST if j < len(widths) - 1 else 0,
        )
        if halving:
            return out, begin_sum(j, out), more
        return out, [out[0]] + [partner(out[d], "blk", d) for d in range(n_blk - 1, 0, -1)], more

    _, group0, _ = tail(0, [coeff3[1]])
    (value,) = step("level2_2", [(2, 2, coeff2[2], near2[2])], [group0[0]])
    third(2, value)
    (total0,) = call(
        sum_kernel,
        "sum_0",
        [VMEM] * n_blk,
        [in_vmem(rows, widths[0])],
        [],
        [here(v) for v in group0],
        [coeff3[2]],
    )
    (value,) = step("level1_3", [job1(3)], [total0])
    second(3, value)
    _, group1, _ = tail(1, [coeff2[3]])
    (value,) = step("level2_3", [(2, 3, coeff2[3], near2[3])], [group1[0]])
    third(3, value)
    out2, held2, (total1,) = tail(2, [coeff3[3]], [(1, group1)], halving=True)
    out3, group3, more = tail(3, [out2[0]], folding=(2, held2))
    held2 = exchange(more, len(masks) - 1)
    (total2,) = call(
        join_kernel,
        "sum_2",
        [VMEM] * 4,
        [in_vmem(rows, widths[2])],
        [],
        [here(v) for v in held2],
        [out3[0]],
    )
    groups = [[total0], [total1], [total2], group3]
    flat = [here(v) for group in groups for v in group]
    return pl.pallas_call(
        functools.partial(end_kernel, places, [len(group) for group in groups]),
        name="end",
        in_specs=[VMEM] * len(flat),
        out_specs=VMEM,
        out_shape=jax.ShapeDtypeStruct((slots, rows, columns), BF16),
        compiler_params=pltpu.CompilerParams(vmem_limit_bytes=8 * 2**20),
    )(*flat)


def solution(mesh):
    in_specs = (
        P("blk", "box", None, None),
        P("blk", "box", None, None),
        P("blk", None, "box", None, None),
        P("blk", None, "box"),
        P("blk", "box", None, None),
    )
    out_specs = P("box", "blk", None)
    return jax.shard_map(
        on_device, mesh=mesh, in_specs=in_specs, out_specs=out_specs, check_vma=False
    )
```

```python
import functools

import jax
import jax.numpy as jnp
from jax import lax
from jax.experimental import pallas as pl
from jax.experimental.pallas import tpu as pltpu
from jax.sharding import PartitionSpec as P

SHARES = (1, 2, 3, 2)
PRELOADED = 2
COST = 6 * 10**9
BF16 = jnp.bfloat16
F32 = jnp.float32
ANY = pl.BlockSpec(memory_space=pl.ANY)
VMEM = pl.BlockSpec(memory_space=pltpu.VMEM)


def dot(a, b):
    return jnp.dot(a, b, preferred_element_type=F32)


def in_vmem(*shape, dtype=BF16):
    return pltpu.VMEM(shape, dtype)


def here(value):
    return pltpu.with_memory_space_constraint(value, pltpu.VMEM)


def in_hbm(value):
    return pltpu.with_memory_space_constraint(value, pltpu.HBM)


def call(kernel, name, in_specs, out_shape, scratch, args, after=(), flops=COST, limit=8 * 2**20):
    count = len(in_specs)

    def body(*refs):
        kernel(*refs[:count], *refs[count + len(after) :])

    return pl.pallas_call(
        body,
        name=name,
        in_specs=[*in_specs, *[ANY] * len(after)],
        out_specs=[VMEM] * len(out_shape),
        out_shape=out_shape,
        scratch_shapes=scratch,
        compiler_params=pltpu.CompilerParams(vmem_limit_bytes=limit),
        cost_estimate=pl.CostEstimate(flops=flops, bytes_accessed=0, transcendentals=0),
    )(*args, *after)


def partner(value, axis, mask):
    pairs = [(source, source ^ mask) for source in range(lax.axis_size(axis))]
    return lax.ppermute(value, axis, pairs)


def leaf_kernel(excite, leaves, blocks, index, first, rest, *refs):
    count = PRELOADED
    nexts = refs[:count]
    excite_v, leaves_v, blocks_v, index_s, coeff, sems = refs[count:]
    slots, rank = leaves.shape[0], leaves.shape[1]
    columns, width = excite.shape[2], first.shape[1]
    listing = pltpu.make_async_copy(index, index_s, sems.at[0])
    listing.start()
    loads = []
    for s in range(slots):
        a = pltpu.make_async_copy(leaves.at[s], leaves_v.at[s], sems.at[1 + s])
        b = pltpu.make_async_copy(excite.at[s], excite_v.at[s], sems.at[3 + s])
        a.start()
        b.start()
        loads.append((a, b))
    listing.wait()
    weights, later = [], []
    for s in range(slots):
        c = pltpu.make_async_copy(blocks.at[0, index_s[s, 0]], blocks_v.at[s], sems.at[5 + s])
        c.start()
        weights.append(c)
    for level in range(1, 1 + count):
        for s in range(slots):
            c = pltpu.make_async_copy(
                blocks.at[level, index_s[s, level]], nexts[level - 1].at[s], sems.at[5 + 2 * level + s]
            )
            c.start()
            later.append(c)
    for s in range(slots):
        for load in loads[s]:
            load.wait()
        coeff[s * rank : (s + 1) * rank, :] = dot(leaves_v[s], excite_v[s]).astype(BF16)
    for s in range(slots):
        weights[s].wait()
        out = dot(blocks_v[s], coeff[...]).astype(BF16)
        if s == 0:
            first[...] = out[:, :width]
            rest[:, : columns - width] = out[:, width:]
        else:
            rest[:, s * columns - width : (s + 1) * columns - width] = out
    for c in later:
        c.wait()


def prefetch_kernel(blocks, basis, index, *refs):
    count = blocks.shape[0] - 1 - PRELOADED
    outs, basis_v, index_s, sems = refs[:count], refs[count], refs[count + 1], refs[count + 2]
    listing = pltpu.make_async_copy(index, index_s, sems.at[0])
    listing.start()
    c = pltpu.make_async_copy(basis, basis_v, sems.at[1 + 2 * count])
    c.start()
    copies = [c]
    listing.wait()
    for at in range(count):
        level = at + 1 + PRELOADED
        for s in range(2):
            c = pltpu.make_async_copy(blocks.at[level, index_s[s, level]], outs[at].at[s], sems.at[1 + 2 * at + s])
            c.start()
            copies.append(c)
    for c in copies:
        c.wait()


def upper_half(bit):
    return (lax.axis_index("box") >> bit) & 1


def mix(weights, own, other, bit, buf, parts, out):
    rank = own.shape[0]
    upper = upper_half(bit)
    buf[pl.ds(pl.multiple_of(upper * rank, rank), rank), :] = own
    buf[pl.ds(pl.multiple_of((1 - upper) * rank, rank), rank), :] = other
    for s, start, stop in parts:
        out[:, start:stop] = dot(weights[s], buf[:, start:stop]).astype(BF16)


def levels_kernel(jobs, *refs):
    count = len(jobs)
    ins, outs, bufs = refs[: 3 * count], refs[3 * count : 4 * count], refs[4 * count :]
    for at, (bit, parts, lanes) in enumerate(jobs):
        own, other, weights = ins[3 * at : 3 * at + 3]
        mix(weights, own[:, lanes], other[:, lanes], bit, bufs[at], parts, outs[at])


def half_dot(weights, s, half, value):
    rank = value.shape[0]
    return dot(weights[s, :, pl.ds(pl.multiple_of(half * rank, 128), rank)], value)


def sum_kernel(mine, *refs):
    total = mine[...]
    for piece in refs[:-1]:
        total = total + piece[...].astype(F32)
    refs[-1][...] = total.astype(BF16)


def between_kernel(bit, parts, counts, folds, own, weights, *refs):
    refs = list(refs)
    groups = [[refs.pop(0) for _ in range(count)] for count in counts]
    held = [refs.pop(0) for _ in range(2 * folds)]
    partial = refs.pop(0)
    for s, start, stop in parts:
        partial[:, start:stop] = half_dot(weights, s, upper_half(bit), own[:, start:stop])
    for group in groups:
        sum_kernel(*group, refs.pop(0))
    fold_kernel(*held, *refs)


def fold_kernel(*refs):
    half = len(refs) // 2
    for at in range(0, half, 2):
        keep, got, rest, send = refs[at], refs[at + 1], refs[half + at], refs[half + at + 1]
        rows = rest.shape[0]
        rest[...] = keep[:rows] + got[:rows].astype(F32)
        send[...] = (keep[rows:] + got[rows:].astype(F32)).astype(BF16)


def join_kernel(*refs):
    out, row = refs[-1], 0
    for keep, got in zip(refs[:-1:2], refs[1:-1:2]):
        out[row : row + keep.shape[0], :] = (keep[...] + got[...].astype(F32)).astype(BF16)
        row += keep.shape[0]


def last_kernel(bit, parts, homes, partial, other, weights, basis, *refs):
    rows = basis.shape[1] // lax.axis_size("blk")
    me = lax.axis_index("blk")
    for s, start, stop in parts:
        mixed = partial[:, start:stop] + half_dot(weights, s, 1 - upper_half(bit), other[:, start:stop])
        coeff = mixed.astype(BF16)
        for d, home in enumerate(homes):
            row = pl.multiple_of((me ^ d) * rows, rows)
            piece = dot(basis[s, pl.ds(row, rows), :], coeff)
            for begin, size, at, to in home:
                ref = refs[at]
                ref[to : to + size, start:stop] = piece[begin : begin + size].astype(ref.dtype)


def end_kernel(places, counts, *refs):
    refs = list(refs)
    out = refs[-1]
    for place, count in zip(places, counts):
        group = [refs.pop(0) for _ in range(count)]
        for s, column, start, stop in place:
            total = group[0][:, start:stop].astype(F32)
            for piece in group[1:]:
                total = total + piece[:, start:stop].astype(F32)
            out[s, :, column : column + stop - start] = total.astype(BF16)


def on_device(excitation, leaf_basis, transfer, transfer_index, out_basis):
    excite, leaves, blocks, basis = excitation[0], leaf_basis[0], transfer[0], out_basis[0]
    index = transfer_index[0].T
    slots, rank, points = leaves.shape
    levels = blocks.shape[0]
    columns = excite.shape[2]
    n_blk = lax.axis_size("blk")
    rows = basis.shape[1] // n_blk
    nbits = lax.axis_size("box").bit_length() - 1
    bits = [None] + [(level - 1) % nbits for level in range(1, levels)]
    pair = in_vmem(slots, rank, 2 * rank)

    unit = slots * columns // sum(SHARES)
    widths = [unit * share for share in SHARES]
    begins = [sum(widths[:j]) for j in range(len(widths))]
    parts, places = [], []
    for begin, width in zip(begins, widths):
        part, place, lane = [], [], 0
        while lane < width:
            s, column = divmod(begin + lane, columns)
            size = min(width - lane, columns - column)
            part.append((s, lane, lane + size))
            place.append((s, column, lane, lane + size))
            lane += size
        parts.append(part)
        places.append(place)

    first, rest, *weights = call(
        leaf_kernel,
        "leaf",
        [ANY] * 4,
        [in_vmem(rank, widths[0]), in_vmem(rank, slots * columns - widths[0])] + [pair] * PRELOADED,
        [
            in_vmem(*excite.shape),
            in_vmem(*leaves.shape),
            pair,
            pltpu.SMEM(index.shape, jnp.int32),
            in_vmem(2 * rank, columns),
            pltpu.SemaphoreType.DMA((7 + 2 * PRELOADED,)),
        ],
        [in_hbm(excite), in_hbm(leaves), in_hbm(blocks), in_hbm(index)],
        limit=24 * 2**20,
    )
    weights = [None, *weights]

    def cross(level, value):
        return partner(value, "box", 2 ** bits[level])

    near_first, near_rest = cross(1, first), cross(1, rest)

    def step(name, jobs, after=(), flops=COST):
        args = [here(v) for level, j, own, other in jobs for v in (own, other, weights[level])]
        described, sizes = [], []
        for level, j, _, _ in jobs:
            begin = begins[j] - widths[0] if level == 1 and j else 0
            described.append((bits[level], parts[j], slice(begin, begin + widths[j])))
            sizes.append(widths[j])
        return call(
            functools.partial(levels_kernel, described),
            name,
            [VMEM] * len(args),
            [in_vmem(rank, size) for size in sizes],
            [in_vmem(2 * rank, size) for size in sizes],
            args,
            after,
            flops,
        )

    def job1(j):
        return (1, j, rest, near_rest) if j else (1, j, first, near_first)

    coeff2, near2, coeff3, near3 = {}, {}, {}, {}

    def second(j, value):
        coeff2[j] = value
        near2[j] = cross(2, value)

    def third(j, value):
        coeff3[j] = value
        near3[j] = cross(3, value)

    (value,) = step("level1_0", [job1(0)])
    second(0, value)
    (value,) = step("level1_1", [job1(1)], [coeff2[0]])
    second(1, value)
    (value,) = step("level2_0", [(2, 0, coeff2[0], near2[0])], [coeff2[1]])
    third(0, value)
    (value,) = step("level1_2", [job1(2)], [coeff3[0]])
    second(2, value)
    *more, basis_v = call(
        prefetch_kernel,
        "prefetch",
        [ANY] * 3,
        [pair] * (levels - 1 - PRELOADED) + [in_vmem(*basis.shape)],
        [pltpu.SMEM(index.shape, jnp.int32), pltpu.SemaphoreType.DMA((2 * levels,))],
        [in_hbm(blocks), in_hbm(basis), in_hbm(index)],
        [coeff2[2]],
    )
    weights += more
    (value,) = step("level2_1", [(2, 1, coeff2[1], near2[1])], [basis_v])
    third(1, value)

    masks = [1 << b for b in range(n_blk.bit_length() - 1)]
    orders = [masks, masks[::-1]]
    half = rows // 2
    whole = [[(0, rows, d, 0)] for d in range(n_blk)]
    halved = [[] for _ in range(n_blk)]
    for side, order in enumerate(orders):
        pieces = [0]
        for mask in order[::-1]:
            pieces = pieces + [d | mask for d in pieces]
        for at, d in enumerate(pieces):
            sent, to = divmod(at, n_blk // 2)
            halved[d].append((side * half, half, 2 * side + sent, to * half))

    def halves(j, count):
        shape = (count * half, widths[j])
        return [in_vmem(*shape, dtype=kind) for _ in orders for kind in (F32, BF16)]

    def exchange(values, at):
        return [
            v
            for side, order in enumerate(orders)
            for v in (values[2 * side], partner(values[2 * side + 1], "blk", order[at]))
        ]

    def begin_sum(j, out):
        held, count = exchange(out, 0), n_blk // 2
        for at in range(1, len(masks) - 1):
            count //= 2
            out = call(
                fold_kernel, f"fold_{j}_{at}", [VMEM] * 4, halves(j, count), [], [here(v) for v in held]
            )
            held = exchange(out, at)
        return held

    def tail(j, after, arrived=(), folding=(), halving=False):
        (coeff4,) = step(f"level3_{j}", [(3, j, coeff3[j], near3[j])], after)
        near4 = cross(4, coeff4)
        held = folding[1] if folding else []
        extra = [v for _, group in arrived for v in group] + held
        partial, *more = call(
            functools.partial(
                between_kernel, bits[4], parts[j], [len(group) for _, group in arrived], len(held) // 2
            ),
            f"between_{j}",
            [VMEM] * (2 + len(extra)),
            [in_vmem(rank, widths[j], dtype=F32)]
            + [in_vmem(rows, widths[at]) for at, _ in arrived]
            + (halves(folding[0], 1) if folding else []),
            [],
            [here(v) for v in (coeff4, weights[4], *extra)],
        )
        if halving:
            outs = halves(j, n_blk // 2)
        else:
            outs = [in_vmem(rows, widths[j], dtype=BF16 if d else F32) for d in range(n_blk)]
        out = call(
            functools.partial(last_kernel, bits[4], parts[j], halved if halving else whole),
            f"last_{j}",
            [VMEM] * 4,
            outs,
            [],
            [here(v) for v in (partial, near4, weights[4], basis_v)],
            flops=COST if j < len(widths) - 1 else 0,
        )
        if halving:
            return out, begin_sum(j, out), more
        return out, [out[0]] + [partner(out[d], "blk", d) for d in range(n_blk - 1, 0, -1)], more

    _, group0, _ = tail(0, [coeff3[1]])
    (value,) = step("level2_2", [(2, 2, coeff2[2], near2[2])], [group0[0]])
    third(2, value)
    (total0,) = call(
        sum_kernel,
        "sum_0",
        [VMEM] * n_blk,
        [in_vmem(rows, widths[0])],
        [],
        [here(v) for v in group0],
        [coeff3[2]],
    )
    (value,) = step("level1_3", [job1(3)], [total0])
    second(3, value)
    _, group1, _ = tail(1, [coeff2[3]])
    (value,) = step("level2_3", [(2, 3, coeff2[3], near2[3])], [group1[0]])
    third(3, value)
    out2, held2, (total1,) = tail(2, [coeff3[3]], [(1, group1)], halving=True)
    out3, group3, _ = tail(3, [out2[0]])
    more = call(
        fold_kernel, "fold_2", [VMEM] * 4, halves(2, 1), [], [here(v) for v in held2], [out3[0]], 0
    )
    held2 = exchange(more, len(masks) - 1)
    (total2,) = call(
        join_kernel,
        "sum_2",
        [VMEM] * 4,
        [in_vmem(rows, widths[2])],
        [],
        [here(v) for v in held2],
        [out3[0]],
        0,
    )
    groups = [[total0], [total1], [total2], group3]
    flat = [here(v) for group in groups for v in group]
    return pl.pallas_call(
        functools.partial(end_kernel, places, [len(group) for group in groups]),
        name="end",
        in_specs=[VMEM] * len(flat),
        out_specs=VMEM,
        out_shape=jax.ShapeDtypeStruct((slots, rows, columns), BF16),
        compiler_params=pltpu.CompilerParams(vmem_limit_bytes=8 * 2**20),
    )(*flat)


def solution(mesh):
    in_specs = (
        P("blk", "box", None, None),
        P("blk", "box", None, None),
        P("blk", None, "box", None, None),
        P("blk", None, "box"),
        P("blk", "box", None, None),
    )
    out_specs = P("box", "blk", None)
    return jax.shard_map(
        on_device, mesh=mesh, in_specs=in_specs, out_specs=out_specs, check_vma=False
    )
```

```python
import functools

import jax
import jax.numpy as jnp
from jax import lax
from jax.experimental import pallas as pl
from jax.experimental.pallas import tpu as pltpu
from jax.sharding import PartitionSpec as P

SHARES = (1, 2, 3, 2)
PRELOADED = 2
COST = 6 * 10**9
BF16 = jnp.bfloat16
F32 = jnp.float32
ANY = pl.BlockSpec(memory_space=pl.ANY)
VMEM = pl.BlockSpec(memory_space=pltpu.VMEM)


def dot(a, b):
    return jnp.dot(a, b, preferred_element_type=F32)


def in_vmem(*shape, dtype=BF16):
    return pltpu.VMEM(shape, dtype)


def here(value):
    return pltpu.with_memory_space_constraint(value, pltpu.VMEM)


def in_hbm(value):
    return pltpu.with_memory_space_constraint(value, pltpu.HBM)


def call(kernel, name, in_specs, out_shape, scratch, args, after=(), flops=COST, limit=8 * 2**20, through=()):
    count, outs = len(in_specs), len(out_shape)

    def body(*refs):
        held = refs[count + len(after) + len(through) :]
        kernel(*refs[:count], *held[:outs], *held[outs + len(through) :])

    return pl.pallas_call(
        body,
        name=name,
        in_specs=[*in_specs, *[ANY] * (len(after) + len(through))],
        out_specs=[VMEM] * outs + [ANY] * len(through),
        out_shape=[*out_shape, *[in_vmem(*v.shape, dtype=v.dtype) for v in through]],
        scratch_shapes=scratch,
        input_output_aliases={count + len(after) + at: outs + at for at in range(len(through))},
        compiler_params=pltpu.CompilerParams(vmem_limit_bytes=limit),
        cost_estimate=pl.CostEstimate(flops=flops, bytes_accessed=0, transcendentals=0),
    )(*args, *after, *[here(v) for v in through])


def partner(value, axis, mask):
    pairs = [(source, source ^ mask) for source in range(lax.axis_size(axis))]
    return lax.ppermute(value, axis, pairs)


def leaf_kernel(excite, leaves, blocks, index, first, rest, *refs):
    count = PRELOADED
    nexts = refs[:count]
    excite_v, leaves_v, blocks_v, index_s, coeff, sems = refs[count:]
    slots, rank = leaves.shape[0], leaves.shape[1]
    columns, width = excite.shape[2], first.shape[1]
    listing = pltpu.make_async_copy(index, index_s, sems.at[0])
    listing.start()
    loads = []
    for s in range(slots):
        a = pltpu.make_async_copy(leaves.at[s], leaves_v.at[s], sems.at[1 + s])
        b = pltpu.make_async_copy(excite.at[s], excite_v.at[s], sems.at[3 + s])
        a.start()
        b.start()
        loads.append((a, b))
    listing.wait()
    weights, later = [], []
    for s in range(slots):
        c = pltpu.make_async_copy(blocks.at[0, index_s[s, 0]], blocks_v.at[s], sems.at[5 + s])
        c.start()
        weights.append(c)
    for level in range(1, 1 + count):
        for s in range(slots):
            c = pltpu.make_async_copy(
                blocks.at[level, index_s[s, level]], nexts[level - 1].at[s], sems.at[5 + 2 * level + s]
            )
            c.start()
            later.append(c)
    for s in range(slots):
        for load in loads[s]:
            load.wait()
        coeff[s * rank : (s + 1) * rank, :] = dot(leaves_v[s], excite_v[s]).astype(BF16)
    for s in range(slots):
        weights[s].wait()
        out = dot(blocks_v[s], coeff[...]).astype(BF16)
        if s == 0:
            first[...] = out[:, :width]
            rest[:, : columns - width] = out[:, width:]
        else:
            rest[:, s * columns - width : (s + 1) * columns - width] = out
    for c in later:
        c.wait()


def prefetch_kernel(blocks, basis, index, *refs):
    count = blocks.shape[0] - 1 - PRELOADED
    outs, basis_v, index_s, sems = refs[:count], refs[count], refs[count + 1], refs[count + 2]
    listing = pltpu.make_async_copy(index, index_s, sems.at[0])
    listing.start()
    c = pltpu.make_async_copy(basis, basis_v, sems.at[1 + 2 * count])
    c.start()
    copies = [c]
    listing.wait()
    for at in range(count):
        level = at + 1 + PRELOADED
        for s in range(2):
            c = pltpu.make_async_copy(blocks.at[level, index_s[s, level]], outs[at].at[s], sems.at[1 + 2 * at + s])
            c.start()
            copies.append(c)
    for c in copies:
        c.wait()


def upper_half(bit):
    return (lax.axis_index("box") >> bit) & 1


def mix(weights, own, other, bit, buf, parts, out):
    rank = own.shape[0]
    upper = upper_half(bit)
    buf[pl.ds(pl.multiple_of(upper * rank, rank), rank), :] = own
    buf[pl.ds(pl.multiple_of((1 - upper) * rank, rank), rank), :] = other
    for s, start, stop in parts:
        out[:, start:stop] = dot(weights[s], buf[:, start:stop]).astype(BF16)


def levels_kernel(jobs, *refs):
    count = len(jobs)
    ins, outs, bufs = refs[: 3 * count], refs[3 * count : 4 * count], refs[4 * count :]
    for at, (bit, parts, lanes) in enumerate(jobs):
        own, other, weights = ins[3 * at : 3 * at + 3]
        mix(weights, own[:, lanes], other[:, lanes], bit, bufs[at], parts, outs[at])


def half_dot(weights, s, half, value):
    rank = value.shape[0]
    return dot(weights[s, :, pl.ds(pl.multiple_of(half * rank, 128), rank)], value)


def sum_kernel(mine, *refs):
    total = mine[...]
    for piece in refs[:-1]:
        total = total + piece[...].astype(F32)
    refs[-1][...] = total.astype(BF16)


def between_kernel(bit, parts, counts, folds, own, weights, *refs):
    refs = list(refs)
    groups = [[refs.pop(0) for _ in range(count)] for count in counts]
    held = [refs.pop(0) for _ in range(2 * folds)]
    partial = refs.pop(0)
    for s, start, stop in parts:
        partial[:, start:stop] = half_dot(weights, s, upper_half(bit), own[:, start:stop])
    for group in groups:
        sum_kernel(*group, refs.pop(0))
    fold_kernel(*held, *refs)


def fold_kernel(*refs):
    half = len(refs) // 2
    for at in range(0, half, 2):
        keep, got, rest, send = refs[at], refs[at + 1], refs[half + at], refs[half + at + 1]
        rows = rest.shape[0]
        rest[...] = keep[:rows] + got[:rows].astype(F32)
        send[...] = (keep[rows:] + got[rows:].astype(F32)).astype(BF16)


def join_kernel(*refs):
    out, row = refs[-1], 0
    for keep, got in zip(refs[:-1:2], refs[1:-1:2]):
        out[row : row + keep.shape[0], :] = (keep[...] + got[...].astype(F32)).astype(BF16)
        row += keep.shape[0]


def last_kernel(bit, parts, homes, partial, other, weights, basis, *refs):
    rows = basis.shape[1] // lax.axis_size("blk")
    me = lax.axis_index("blk")
    for s, start, stop in parts:
        mixed = partial[:, start:stop] + half_dot(weights, s, 1 - upper_half(bit), other[:, start:stop])
        coeff = mixed.astype(BF16)
        for d, home in enumerate(homes):
            row = pl.multiple_of((me ^ d) * rows, rows)
            piece = dot(basis[s, pl.ds(row, rows), :], coeff)
            for begin, size, at, to in home:
                ref = refs[at]
                ref[to : to + size, start:stop] = piece[begin : begin + size].astype(ref.dtype)


def end_kernel(places, counts, *refs):
    refs = list(refs)
    out = refs[-1]
    for place, count in zip(places, counts):
        group = [refs.pop(0) for _ in range(count)]
        for s, column, start, stop in place:
            total = group[0][:, start:stop].astype(F32)
            for piece in group[1:]:
                total = total + piece[:, start:stop].astype(F32)
            out[s, :, column : column + stop - start] = total.astype(BF16)


def on_device(excitation, leaf_basis, transfer, transfer_index, out_basis):
    excite, leaves, blocks, basis = excitation[0], leaf_basis[0], transfer[0], out_basis[0]
    index = transfer_index[0].T
    slots, rank, points = leaves.shape
    levels = blocks.shape[0]
    columns = excite.shape[2]
    n_blk = lax.axis_size("blk")
    rows = basis.shape[1] // n_blk
    nbits = lax.axis_size("box").bit_length() - 1
    bits = [None] + [(level - 1) % nbits for level in range(1, levels)]
    pair = in_vmem(slots, rank, 2 * rank)

    unit = slots * columns // sum(SHARES)
    widths = [unit * share for share in SHARES]
    begins = [sum(widths[:j]) for j in range(len(widths))]
    parts, places = [], []
    for begin, width in zip(begins, widths):
        part, place, lane = [], [], 0
        while lane < width:
            s, column = divmod(begin + lane, columns)
            size = min(width - lane, columns - column)
            part.append((s, lane, lane + size))
            place.append((s, column, lane, lane + size))
            lane += size
        parts.append(part)
        places.append(place)

    first, rest, *weights = call(
        leaf_kernel,
        "leaf",
        [ANY] * 4,
        [in_vmem(rank, widths[0]), in_vmem(rank, slots * columns - widths[0])] + [pair] * PRELOADED,
        [
            in_vmem(*excite.shape),
            in_vmem(*leaves.shape),
            pair,
            pltpu.SMEM(index.shape, jnp.int32),
            in_vmem(2 * rank, columns),
            pltpu.SemaphoreType.DMA((7 + 2 * PRELOADED,)),
        ],
        [in_hbm(excite), in_hbm(leaves), in_hbm(blocks), in_hbm(index)],
        limit=24 * 2**20,
    )
    weights = [None, *weights]

    def cross(level, value):
        return partner(value, "box", 2 ** bits[level])

    near_first = cross(1, first)

    def step(name, jobs, after=(), flops=COST, through=()):
        args = [here(v) for level, j, own, other in jobs for v in (own, other, weights[level])]
        described, sizes = [], []
        for level, j, _, _ in jobs:
            begin = begins[j] - widths[0] if level == 1 and j else 0
            described.append((bits[level], parts[j], slice(begin, begin + widths[j])))
            sizes.append(widths[j])
        return call(
            functools.partial(levels_kernel, described),
            name,
            [VMEM] * len(args),
            [in_vmem(rank, size) for size in sizes],
            [in_vmem(2 * rank, size) for size in sizes],
            args,
            after,
            flops,
            through=through,
        )

    def job1(j):
        return (1, j, rest, near_rest) if j else (1, j, first, near_first)

    coeff2, near2, coeff3, near3 = {}, {}, {}, {}

    def second(j, value):
        coeff2[j] = value
        near2[j] = cross(2, value)

    def third(j, value):
        coeff3[j] = value
        near3[j] = cross(3, value)

    value, rest = step("level1_0", [job1(0)], through=[rest])
    near_rest = cross(1, rest)
    second(0, value)
    (value,) = step("level1_1", [job1(1)], [coeff2[0]])
    second(1, value)
    (value,) = step("level2_0", [(2, 0, coeff2[0], near2[0])], [coeff2[1]])
    third(0, value)
    (value,) = step("level1_2", [job1(2)], [coeff3[0]])
    second(2, value)
    *more, basis_v = call(
        prefetch_kernel,
        "prefetch",
        [ANY] * 3,
        [pair] * (levels - 1 - PRELOADED) + [in_vmem(*basis.shape)],
        [pltpu.SMEM(index.shape, jnp.int32), pltpu.SemaphoreType.DMA((2 * levels,))],
        [in_hbm(blocks), in_hbm(basis), in_hbm(index)],
        [coeff2[2]],
    )
    weights += more
    (value,) = step("level2_1", [(2, 1, coeff2[1], near2[1])], [basis_v])
    third(1, value)

    masks = [1 << b for b in range(n_blk.bit_length() - 1)]
    orders = [masks, masks[::-1]]
    half = rows // 2
    whole = [[(0, rows, d, 0)] for d in range(n_blk)]
    halved = [[] for _ in range(n_blk)]
    for side, order in enumerate(orders):
        pieces = [0]
        for mask in order[::-1]:
            pieces = pieces + [d | mask for d in pieces]
        for at, d in enumerate(pieces):
            sent, to = divmod(at, n_blk // 2)
            halved[d].append((side * half, half, 2 * side + sent, to * half))

    def halves(j, count):
        shape = (count * half, widths[j])
        return [in_vmem(*shape, dtype=kind) for _ in orders for kind in (F32, BF16)]

    def exchange(values, at):
        return [
            v
            for side, order in enumerate(orders)
            for v in (values[2 * side], partner(values[2 * side + 1], "blk", order[at]))
        ]

    def begin_sum(j, out):
        held, count = exchange(out, 0), n_blk // 2
        for at in range(1, len(masks) - 1):
            count //= 2
            out = call(
                fold_kernel, f"fold_{j}_{at}", [VMEM] * 4, halves(j, count), [], [here(v) for v in held]
            )
            held = exchange(out, at)
        return held

    def tail(j, after, arrived=(), folding=(), halving=False):
        (coeff4,) = step(f"level3_{j}", [(3, j, coeff3[j], near3[j])], after)
        near4 = cross(4, coeff4)
        held = folding[1] if folding else []
        extra = [v for _, group in arrived for v in group] + held
        partial, *more = call(
            functools.partial(
                between_kernel, bits[4], parts[j], [len(group) for _, group in arrived], len(held) // 2
            ),
            f"between_{j}",
            [VMEM] * (2 + len(extra)),
            [in_vmem(rank, widths[j], dtype=F32)]
            + [in_vmem(rows, widths[at]) for at, _ in arrived]
            + (halves(folding[0], 1) if folding else []),
            [],
            [here(v) for v in (coeff4, weights[4], *extra)],
        )
        if halving:
            outs = halves(j, n_blk // 2)
        else:
            outs = [in_vmem(rows, widths[j], dtype=BF16 if d else F32) for d in range(n_blk)]
        out = call(
            functools.partial(last_kernel, bits[4], parts[j], halved if halving else whole),
            f"last_{j}",
            [VMEM] * 4,
            outs,
            [],
            [here(v) for v in (partial, near4, weights[4], basis_v)],
            flops=COST if j < len(widths) - 1 else 0,
        )
        if halving:
            return out, begin_sum(j, out), more
        return out, [out[0]] + [partner(out[d], "blk", d) for d in range(n_blk - 1, 0, -1)], more

    _, group0, _ = tail(0, [coeff3[1]])
    (value,) = step("level2_2", [(2, 2, coeff2[2], near2[2])], [group0[0]])
    third(2, value)
    (total0,) = call(
        sum_kernel,
        "sum_0",
        [VMEM] * n_blk,
        [in_vmem(rows, widths[0])],
        [],
        [here(v) for v in group0],
        [coeff3[2]],
    )
    (value,) = step("level1_3", [job1(3)], [total0])
    second(3, value)
    _, group1, _ = tail(1, [coeff2[3]])
    (value,) = step("level2_3", [(2, 3, coeff2[3], near2[3])], [group1[0]])
    third(3, value)
    out2, held2, (total1,) = tail(2, [coeff3[3]], [(1, group1)], halving=True)
    out3, group3, _ = tail(3, [out2[0]])
    more = call(
        fold_kernel, "fold_2", [VMEM] * 4, halves(2, 1), [], [here(v) for v in held2], [out3[0]], 0
    )
    held2 = exchange(more, len(masks) - 1)
    (total2,) = call(
        join_kernel,
        "sum_2",
        [VMEM] * 4,
        [in_vmem(rows, widths[2])],
        [],
        [here(v) for v in held2],
        [out3[0]],
        0,
    )
    groups = [[total0], [total1], [total2], group3]
    flat = [here(v) for group in groups for v in group]
    return pl.pallas_call(
        functools.partial(end_kernel, places, [len(group) for group in groups]),
        name="end",
        in_specs=[VMEM] * len(flat),
        out_specs=VMEM,
        out_shape=jax.ShapeDtypeStruct((slots, rows, columns), BF16),
        compiler_params=pltpu.CompilerParams(vmem_limit_bytes=8 * 2**20),
    )(*flat)


def solution(mesh):
    in_specs = (
        P("blk", "box", None, None),
        P("blk", "box", None, None),
        P("blk", None, "box", None, None),
        P("blk", None, "box"),
        P("blk", "box", None, None),
    )
    out_specs = P("box", "blk", None)
    return jax.shard_map(
        on_device, mesh=mesh, in_specs=in_specs, out_specs=out_specs, check_vma=False
    )
```

```python
import functools

import jax
import jax.numpy as jnp
from jax import lax
from jax.experimental import pallas as pl
from jax.experimental.pallas import tpu as pltpu
from jax.sharding import PartitionSpec as P

SHARES = (1, 2, 3, 2)
PRELOADED = 2
COST = 6 * 10**9
BF16 = jnp.bfloat16
F32 = jnp.float32
ANY = pl.BlockSpec(memory_space=pl.ANY)
VMEM = pl.BlockSpec(memory_space=pltpu.VMEM)


def dot(a, b):
    return jnp.dot(a, b, preferred_element_type=F32)


def in_vmem(*shape, dtype=BF16):
    return pltpu.VMEM(shape, dtype)


def here(value):
    return pltpu.with_memory_space_constraint(value, pltpu.VMEM)


def in_hbm(value):
    return pltpu.with_memory_space_constraint(value, pltpu.HBM)


def call(kernel, name, in_specs, out_shape, scratch, args, after=(), flops=COST, limit=8 * 2**20, through=()):
    count, outs = len(in_specs), len(out_shape)

    def body(*refs):
        held = refs[count + len(after) + len(through) :]
        kernel(*refs[:count], *held[:outs], *held[outs + len(through) :])

    return pl.pallas_call(
        body,
        name=name,
        in_specs=[*in_specs, *[ANY] * (len(after) + len(through))],
        out_specs=[VMEM] * outs + [ANY] * len(through),
        out_shape=[*out_shape, *[in_vmem(*v.shape, dtype=v.dtype) for v in through]],
        scratch_shapes=scratch,
        input_output_aliases={count + len(after) + at: outs + at for at in range(len(through))},
        compiler_params=pltpu.CompilerParams(vmem_limit_bytes=limit),
        cost_estimate=pl.CostEstimate(flops=flops, bytes_accessed=0, transcendentals=0),
    )(*args, *after, *[here(v) for v in through])


def partner(value, axis, mask):
    pairs = [(source, source ^ mask) for source in range(lax.axis_size(axis))]
    return lax.ppermute(value, axis, pairs)


def leaf_kernel(excite, leaves, blocks, index, first, rest, *refs):
    count = PRELOADED
    nexts = refs[:count]
    excite_v, leaves_v, blocks_v, index_s, coeff, sems = refs[count:]
    slots, rank = leaves.shape[0], leaves.shape[1]
    columns, width = excite.shape[2], first.shape[1]
    listing = pltpu.make_async_copy(index, index_s, sems.at[0])
    listing.start()
    loads = []
    for s in range(slots):
        a = pltpu.make_async_copy(leaves.at[s], leaves_v.at[s], sems.at[1 + s])
        b = pltpu.make_async_copy(excite.at[s], excite_v.at[s], sems.at[3 + s])
        a.start()
        b.start()
        loads.append((a, b))
    listing.wait()
    weights, later = [], []
    for s in range(slots):
        c = pltpu.make_async_copy(blocks.at[0, index_s[s, 0]], blocks_v.at[s], sems.at[5 + s])
        c.start()
        weights.append(c)
    for level in range(1, 1 + count):
        for s in range(slots):
            c = pltpu.make_async_copy(
                blocks.at[level, index_s[s, level]], nexts[level - 1].at[s], sems.at[5 + 2 * level + s]
            )
            c.start()
            later.append(c)
    for s in range(slots):
        for load in loads[s]:
            load.wait()
        coeff[s * rank : (s + 1) * rank, :] = dot(leaves_v[s], excite_v[s]).astype(BF16)
    for s in range(slots):
        weights[s].wait()
        out = dot(blocks_v[s], coeff[...]).astype(BF16)
        if s == 0:
            first[...] = out[:, :width]
            rest[:, : columns - width] = out[:, width:]
        else:
            rest[:, s * columns - width : (s + 1) * columns - width] = out
    for c in later:
        c.wait()


def prefetch_kernel(blocks, basis, index, *refs):
    count = blocks.shape[0] - 1 - PRELOADED
    outs, basis_v, index_s, sems = refs[:count], refs[count], refs[count + 1], refs[count + 2]
    listing = pltpu.make_async_copy(index, index_s, sems.at[0])
    listing.start()
    c = pltpu.make_async_copy(basis, basis_v, sems.at[1 + 2 * count])
    c.start()
    copies = [c]
    listing.wait()
    for at in range(count):
        level = at + 1 + PRELOADED
        for s in range(2):
            c = pltpu.make_async_copy(blocks.at[level, index_s[s, level]], outs[at].at[s], sems.at[1 + 2 * at + s])
            c.start()
            copies.append(c)
    for c in copies:
        c.wait()


def upper_half(bit):
    return (lax.axis_index("box") >> bit) & 1


def mix(weights, own, other, bit, buf, parts, out):
    rank = own.shape[0]
    upper = upper_half(bit)
    buf[pl.ds(pl.multiple_of(upper * rank, rank), rank), :] = own
    buf[pl.ds(pl.multiple_of((1 - upper) * rank, rank), rank), :] = other
    for s, start, stop in parts:
        out[:, start:stop] = dot(weights[s], buf[:, start:stop]).astype(BF16)


def levels_kernel(jobs, *refs):
    count = len(jobs)
    ins, outs, bufs = refs[: 3 * count], refs[3 * count : 4 * count], refs[4 * count :]
    for at, (bit, parts, lanes) in enumerate(jobs):
        own, other, weights = ins[3 * at : 3 * at + 3]
        mix(weights, own[:, lanes], other[:, lanes], bit, bufs[at], parts, outs[at])


def half_dot(weights, s, half, value):
    rank = value.shape[0]
    return dot(weights[s, :, pl.ds(pl.multiple_of(half * rank, 128), rank)], value)


def sum_kernel(mine, *refs):
    total = mine[...]
    for piece in refs[:-1]:
        total = total + piece[...].astype(F32)
    refs[-1][...] = total.astype(BF16)


def half_kernel(bit, parts, own, weights, partial):
    for s, start, stop in parts:
        partial[:, start:stop] = half_dot(weights, s, upper_half(bit), own[:, start:stop])


def finish_kernel(bit, parts, partial, other, weights, out):
    for s, start, stop in parts:
        mixed = partial[:, start:stop] + half_dot(weights, s, 1 - upper_half(bit), other[:, start:stop])
        out[:, start:stop] = mixed.astype(BF16)


def between_kernel(bit, parts, counts, folds, own, weights, *refs):
    refs = list(refs)
    groups = [[refs.pop(0) for _ in range(count)] for count in counts]
    held = [refs.pop(0) for _ in range(2 * folds)]
    partial = refs.pop(0)
    for s, start, stop in parts:
        partial[:, start:stop] = half_dot(weights, s, upper_half(bit), own[:, start:stop])
    for group in groups:
        sum_kernel(*group, refs.pop(0))
    fold_kernel(*held, *refs)


def fold_kernel(*refs):
    half = len(refs) // 2
    for at in range(0, half, 2):
        keep, got, rest, send = refs[at], refs[at + 1], refs[half + at], refs[half + at + 1]
        rows = rest.shape[0]
        rest[...] = keep[:rows] + got[:rows].astype(F32)
        send[...] = (keep[rows:] + got[rows:].astype(F32)).astype(BF16)


def join_kernel(*refs):
    out, row = refs[-1], 0
    for keep, got in zip(refs[:-1:2], refs[1:-1:2]):
        out[row : row + keep.shape[0], :] = (keep[...] + got[...].astype(F32)).astype(BF16)
        row += keep.shape[0]


def last_kernel(bit, parts, homes, partial, other, weights, basis, *refs):
    rows = basis.shape[1] // lax.axis_size("blk")
    me = lax.axis_index("blk")
    for s, start, stop in parts:
        mixed = partial[:, start:stop] + half_dot(weights, s, 1 - upper_half(bit), other[:, start:stop])
        coeff = mixed.astype(BF16)
        for d, home in enumerate(homes):
            row = pl.multiple_of((me ^ d) * rows, rows)
            piece = dot(basis[s, pl.ds(row, rows), :], coeff)
            for begin, size, at, to in home:
                ref = refs[at]
                ref[to : to + size, start:stop] = piece[begin : begin + size].astype(ref.dtype)


def end_kernel(places, counts, *refs):
    refs = list(refs)
    out = refs[-1]
    for place, count in zip(places, counts):
        group = [refs.pop(0) for _ in range(count)]
        for s, column, start, stop in place:
            total = group[0][:, start:stop].astype(F32)
            for piece in group[1:]:
                total = total + piece[:, start:stop].astype(F32)
            out[s, :, column : column + stop - start] = total.astype(BF16)


def on_device(excitation, leaf_basis, transfer, transfer_index, out_basis):
    excite, leaves, blocks, basis = excitation[0], leaf_basis[0], transfer[0], out_basis[0]
    index = transfer_index[0].T
    slots, rank, points = leaves.shape
    levels = blocks.shape[0]
    columns = excite.shape[2]
    n_blk = lax.axis_size("blk")
    rows = basis.shape[1] // n_blk
    nbits = lax.axis_size("box").bit_length() - 1
    bits = [None] + [(level - 1) % nbits for level in range(1, levels)]
    pair = in_vmem(slots, rank, 2 * rank)

    unit = slots * columns // sum(SHARES)
    widths = [unit * share for share in SHARES]
    begins = [sum(widths[:j]) for j in range(len(widths))]
    parts, places = [], []
    for begin, width in zip(begins, widths):
        part, place, lane = [], [], 0
        while lane < width:
            s, column = divmod(begin + lane, columns)
            size = min(width - lane, columns - column)
            part.append((s, lane, lane + size))
            place.append((s, column, lane, lane + size))
            lane += size
        parts.append(part)
        places.append(place)

    first, rest, *weights = call(
        leaf_kernel,
        "leaf",
        [ANY] * 4,
        [in_vmem(rank, widths[0]), in_vmem(rank, slots * columns - widths[0])] + [pair] * PRELOADED,
        [
            in_vmem(*excite.shape),
            in_vmem(*leaves.shape),
            pair,
            pltpu.SMEM(index.shape, jnp.int32),
            in_vmem(2 * rank, columns),
            pltpu.SemaphoreType.DMA((7 + 2 * PRELOADED,)),
        ],
        [in_hbm(excite), in_hbm(leaves), in_hbm(blocks), in_hbm(index)],
        limit=24 * 2**20,
    )
    weights = [None, *weights]

    def cross(level, value):
        return partner(value, "box", 2 ** bits[level])

    near_first = cross(1, first)

    def step(name, jobs, after=(), flops=COST, through=()):
        args = [here(v) for level, j, own, other in jobs for v in (own, other, weights[level])]
        described, sizes = [], []
        for level, j, _, _ in jobs:
            begin = begins[j] - widths[0] if level == 1 and j else 0
            described.append((bits[level], parts[j], slice(begin, begin + widths[j])))
            sizes.append(widths[j])
        return call(
            functools.partial(levels_kernel, described),
            name,
            [VMEM] * len(args),
            [in_vmem(rank, size) for size in sizes],
            [in_vmem(2 * rank, size) for size in sizes],
            args,
            after,
            flops,
            through=through,
        )

    def job1(j):
        return (1, j, rest, near_rest) if j else (1, j, first, near_first)

    coeff2, near2, coeff3, near3 = {}, {}, {}, {}

    def second(j, value):
        coeff2[j] = value
        near2[j] = cross(2, value)

    def third(j, value):
        coeff3[j] = value
        near3[j] = cross(3, value)

    value, rest = step("level1_0", [job1(0)], through=[rest])
    near_rest = cross(1, rest)
    second(0, value)
    (value,) = step("level1_1", [job1(1)], [coeff2[0]])
    second(1, value)
    (value,) = step("level2_0", [(2, 0, coeff2[0], near2[0])], [coeff2[1]])
    third(0, value)
    (value,) = step("level1_2", [job1(2)], [coeff3[0]])
    second(2, value)
    *more, basis_v = call(
        prefetch_kernel,
        "prefetch",
        [ANY] * 3,
        [pair] * (levels - 1 - PRELOADED) + [in_vmem(*basis.shape)],
        [pltpu.SMEM(index.shape, jnp.int32), pltpu.SemaphoreType.DMA((2 * levels,))],
        [in_hbm(blocks), in_hbm(basis), in_hbm(index)],
        [coeff2[2]],
    )
    weights += more
    (value,) = step("level2_1", [(2, 1, coeff2[1], near2[1])], [basis_v])
    third(1, value)

    masks = [1 << b for b in range(n_blk.bit_length() - 1)]
    orders = [masks, masks[::-1]]
    half = rows // 2
    whole = [[(0, rows, d, 0)] for d in range(n_blk)]
    halved = [[] for _ in range(n_blk)]
    for side, order in enumerate(orders):
        pieces = [0]
        for mask in order[::-1]:
            pieces = pieces + [d | mask for d in pieces]
        for at, d in enumerate(pieces):
            sent, to = divmod(at, n_blk // 2)
            halved[d].append((side * half, half, 2 * side + sent, to * half))

    def halves(j, count):
        shape = (count * half, widths[j])
        return [in_vmem(*shape, dtype=kind) for _ in orders for kind in (F32, BF16)]

    def exchange(values, at):
        return [
            v
            for side, order in enumerate(orders)
            for v in (values[2 * side], partner(values[2 * side + 1], "blk", order[at]))
        ]

    def begin_sum(j, out):
        held, count = exchange(out, 0), n_blk // 2
        for at in range(1, len(masks) - 1):
            count //= 2
            out = call(
                fold_kernel, f"fold_{j}_{at}", [VMEM] * 4, halves(j, count), [], [here(v) for v in held]
            )
            held = exchange(out, at)
        return held

    def tail(j, after, arrived=(), folding=(), halving=False):
        (coeff4,) = step(f"level3_{j}", [(3, j, coeff3[j], near3[j])], after)
        near4 = cross(4, coeff4)
        held = folding[1] if folding else []
        extra = [v for _, group in arrived for v in group] + held
        partial, *more = call(
            functools.partial(
                between_kernel, bits[4], parts[j], [len(group) for _, group in arrived], len(held) // 2
            ),
            f"between_{j}",
            [VMEM] * (2 + len(extra)),
            [in_vmem(rank, widths[j], dtype=F32)]
            + [in_vmem(rows, widths[at]) for at, _ in arrived]
            + (halves(folding[0], 1) if folding else []),
            [],
            [here(v) for v in (coeff4, weights[4], *extra)],
        )
        if halving:
            outs = halves(j, n_blk // 2)
        else:
            outs = [in_vmem(rows, widths[j], dtype=BF16 if d else F32) for d in range(n_blk)]
        out = call(
            functools.partial(last_kernel, bits[4], parts[j], halved if halving else whole),
            f"last_{j}",
            [VMEM] * 4,
            outs,
            [],
            [here(v) for v in (partial, near4, weights[4], basis_v)],
            flops=COST if j < len(widths) - 1 else 0,
        )
        if halving:
            return out, begin_sum(j, out), more
        return out, [out[0]] + [partner(out[d], "blk", d) for d in range(n_blk - 1, 0, -1)], more

    _, group0, _ = tail(0, [coeff3[1]])
    (value,) = step("level2_2", [(2, 2, coeff2[2], near2[2])], [group0[0]])
    third(2, value)
    (total0,) = call(
        sum_kernel,
        "sum_0",
        [VMEM] * n_blk,
        [in_vmem(rows, widths[0])],
        [],
        [here(v) for v in group0],
        [coeff3[2]],
    )
    (value,) = step("level1_3", [job1(3)], [total0])
    second(3, value)
    _, group1, _ = tail(1, [coeff2[3]])
    (partial,) = call(
        functools.partial(half_kernel, bits[2], parts[3]),
        "half_3",
        [VMEM] * 2,
        [in_vmem(rank, widths[3], dtype=F32)],
        [],
        [here(coeff2[3]), here(weights[2])],
        [group1[0]],
    )
    (value,) = call(
        functools.partial(finish_kernel, bits[2], parts[3]),
        "level2_3",
        [VMEM] * 3,
        [in_vmem(rank, widths[3])],
        [],
        [here(partial), here(near2[3]), here(weights[2])],
        [group1[1]],
    )
    third(3, value)
    out2, held2, (total1,) = tail(2, [coeff3[3]], [(1, group1)], halving=True)
    out3, group3, _ = tail(3, [out2[0]])
    more = call(
        fold_kernel, "fold_2", [VMEM] * 4, halves(2, 1), [], [here(v) for v in held2], [out3[0]], 0
    )
    held2 = exchange(more, len(masks) - 1)
    (total2,) = call(
        join_kernel,
        "sum_2",
        [VMEM] * 4,
        [in_vmem(rows, widths[2])],
        [],
        [here(v) for v in held2],
        [out3[0]],
        0,
    )
    groups = [[total0], [total1], [total2], group3]
    flat = [here(v) for group in groups for v in group]
    return pl.pallas_call(
        functools.partial(end_kernel, places, [len(group) for group in groups]),
        name="end",
        in_specs=[VMEM] * len(flat),
        out_specs=VMEM,
        out_shape=jax.ShapeDtypeStruct((slots, rows, columns), BF16),
        compiler_params=pltpu.CompilerParams(vmem_limit_bytes=8 * 2**20),
    )(*flat)


def solution(mesh):
    in_specs = (
        P("blk", "box", None, None),
        P("blk", "box", None, None),
        P("blk", None, "box", None, None),
        P("blk", None, "box"),
        P("blk", "box", None, None),
    )
    out_specs = P("box", "blk", None)
    return jax.shard_map(
        on_device, mesh=mesh, in_specs=in_specs, out_specs=out_specs, check_vma=False
    )
```

```python
import functools

import jax
import jax.numpy as jnp
from jax import lax
from jax.experimental import pallas as pl
from jax.experimental.pallas import tpu as pltpu
from jax.sharding import PartitionSpec as P

SHARES = (1, 2, 3, 2)
PRELOADED = 2
COST = 6 * 10**9
BF16 = jnp.bfloat16
F32 = jnp.float32
ANY = pl.BlockSpec(memory_space=pl.ANY)
VMEM = pl.BlockSpec(memory_space=pltpu.VMEM)


def dot(a, b):
    return jnp.dot(a, b, preferred_element_type=F32)


def in_vmem(*shape, dtype=BF16):
    return pltpu.VMEM(shape, dtype)


def here(value):
    return pltpu.with_memory_space_constraint(value, pltpu.VMEM)


def in_hbm(value):
    return pltpu.with_memory_space_constraint(value, pltpu.HBM)


def call(kernel, name, in_specs, out_shape, scratch, args, after=(), flops=COST, limit=8 * 2**20, through=()):
    count, outs = len(in_specs), len(out_shape)

    def body(*refs):
        held = refs[count + len(after) + len(through) :]
        kernel(*refs[:count], *held[:outs], *held[outs + len(through) :])

    return pl.pallas_call(
        body,
        name=name,
        in_specs=[*in_specs, *[ANY] * (len(after) + len(through))],
        out_specs=[VMEM] * outs + [ANY] * len(through),
        out_shape=[*out_shape, *[in_vmem(*v.shape, dtype=v.dtype) for v in through]],
        scratch_shapes=scratch,
        input_output_aliases={count + len(after) + at: outs + at for at in range(len(through))},
        compiler_params=pltpu.CompilerParams(vmem_limit_bytes=limit),
        cost_estimate=pl.CostEstimate(flops=flops, bytes_accessed=0, transcendentals=0),
    )(*args, *after, *[here(v) for v in through])


def partner(value, axis, mask):
    pairs = [(source, source ^ mask) for source in range(lax.axis_size(axis))]
    return lax.ppermute(value, axis, pairs)


def leaf_kernel(excite, leaves, blocks, index, first, rest, *refs):
    count = PRELOADED
    nexts = refs[:count]
    excite_v, leaves_v, blocks_v, index_s, coeff, sems = refs[count:]
    slots, rank = leaves.shape[0], leaves.shape[1]
    columns, width = excite.shape[2], first.shape[1]
    listing = pltpu.make_async_copy(index, index_s, sems.at[0])
    listing.start()
    loads = []
    for s in range(slots):
        a = pltpu.make_async_copy(leaves.at[s], leaves_v.at[s], sems.at[1 + s])
        b = pltpu.make_async_copy(excite.at[s], excite_v.at[s], sems.at[3 + s])
        a.start()
        b.start()
        loads.append((a, b))
    listing.wait()
    weights, later = [], []
    for s in range(slots):
        c = pltpu.make_async_copy(blocks.at[0, index_s[s, 0]], blocks_v.at[s], sems.at[5 + s])
        c.start()
        weights.append(c)
    for level in range(1, 1 + count):
        for s in range(slots):
            c = pltpu.make_async_copy(
                blocks.at[level, index_s[s, level]], nexts[level - 1].at[s], sems.at[5 + 2 * level + s]
            )
            c.start()
            later.append(c)
    for s in range(slots):
        for load in loads[s]:
            load.wait()
        coeff[s * rank : (s + 1) * rank, :] = dot(leaves_v[s], excite_v[s]).astype(BF16)
    for s in range(slots):
        weights[s].wait()
        out = dot(blocks_v[s], coeff[...]).astype(BF16)
        if s == 0:
            first[...] = out[:, :width]
            rest[:, : columns - width] = out[:, width:]
        else:
            rest[:, s * columns - width : (s + 1) * columns - width] = out
    for c in later:
        c.wait()


def prefetch_kernel(blocks, basis, index, *refs):
    count = blocks.shape[0] - 1 - PRELOADED
    outs, basis_v, index_s, sems = refs[:count], refs[count], refs[count + 1], refs[count + 2]
    listing = pltpu.make_async_copy(index, index_s, sems.at[0])
    listing.start()
    c = pltpu.make_async_copy(basis, basis_v, sems.at[1 + 2 * count])
    c.start()
    copies = [c]
    listing.wait()
    for at in range(count):
        level = at + 1 + PRELOADED
        for s in range(2):
            c = pltpu.make_async_copy(blocks.at[level, index_s[s, level]], outs[at].at[s], sems.at[1 + 2 * at + s])
            c.start()
            copies.append(c)
    for c in copies:
        c.wait()


def upper_half(bit):
    return (lax.axis_index("box") >> bit) & 1


def mix(weights, own, other, bit, buf, parts, out):
    rank = own.shape[0]
    upper = upper_half(bit)
    buf[pl.ds(pl.multiple_of(upper * rank, rank), rank), :] = own
    buf[pl.ds(pl.multiple_of((1 - upper) * rank, rank), rank), :] = other
    for s, start, stop in parts:
        out[:, start:stop] = dot(weights[s], buf[:, start:stop]).astype(BF16)


def levels_kernel(jobs, *refs):
    count = len(jobs)
    ins, outs, bufs = refs[: 3 * count], refs[3 * count : 4 * count], refs[4 * count :]
    for at, (bit, parts, lanes) in enumerate(jobs):
        own, other, weights = ins[3 * at : 3 * at + 3]
        mix(weights, own[:, lanes], other[:, lanes], bit, bufs[at], parts, outs[at])


def half_dot(weights, s, half, value):
    rank = value.shape[0]
    return dot(weights[s, :, pl.ds(pl.multiple_of(half * rank, 128), rank)], value)


def sum_kernel(mine, *refs):
    total = mine[...]
    for piece in refs[:-1]:
        total = total + piece[...].astype(F32)
    refs[-1][...] = total.astype(BF16)


def half_kernel(bit, parts, own, weights, partial):
    for s, start, stop in parts:
        partial[:, start:stop] = half_dot(weights, s, upper_half(bit), own[:, start:stop])


def finish_kernel(bit, parts, partial, other, weights, out):
    for s, start, stop in parts:
        mixed = partial[:, start:stop] + half_dot(weights, s, 1 - upper_half(bit), other[:, start:stop])
        out[:, start:stop] = mixed.astype(BF16)


def between_kernel(bit, parts, counts, folds, own, weights, *refs):
    refs = list(refs)
    groups = [[refs.pop(0) for _ in range(count)] for count in counts]
    held = [refs.pop(0) for _ in range(2 * folds)]
    partial = refs.pop(0)
    for s, start, stop in parts:
        partial[:, start:stop] = half_dot(weights, s, upper_half(bit), own[:, start:stop])
    for group in groups:
        sum_kernel(*group, refs.pop(0))
    fold_kernel(*held, *refs)


def fold_kernel(*refs):
    half = len(refs) // 2
    for at in range(0, half, 2):
        keep, got, rest, send = refs[at], refs[at + 1], refs[half + at], refs[half + at + 1]
        rows = rest.shape[0]
        rest[...] = keep[:rows] + got[:rows].astype(F32)
        send[...] = (keep[rows:] + got[rows:].astype(F32)).astype(BF16)


def join_kernel(*refs):
    out, row = refs[-1], 0
    for keep, got in zip(refs[:-1:2], refs[1:-1:2]):
        out[row : row + keep.shape[0], :] = (keep[...] + got[...].astype(F32)).astype(BF16)
        row += keep.shape[0]


def last_kernel(bit, parts, homes, partial, other, weights, basis, *refs):
    rows = basis.shape[1] // lax.axis_size("blk")
    me = lax.axis_index("blk")
    for s, start, stop in parts:
        mixed = partial[:, start:stop] + half_dot(weights, s, 1 - upper_half(bit), other[:, start:stop])
        coeff = mixed.astype(BF16)
        for d, home in enumerate(homes):
            row = pl.multiple_of((me ^ d) * rows, rows)
            piece = dot(basis[s, pl.ds(row, rows), :], coeff)
            for begin, size, at, to in home:
                ref = refs[at]
                ref[to : to + size, start:stop] = piece[begin : begin + size].astype(ref.dtype)


def end_kernel(places, counts, *refs):
    refs = list(refs)
    out = refs[-1]
    for place, count in zip(places, counts):
        group = [refs.pop(0) for _ in range(count)]
        for s, column, start, stop in place:
            total = group[0][:, start:stop].astype(F32)
            for piece in group[1:]:
                total = total + piece[:, start:stop].astype(F32)
            out[s, :, column : column + stop - start] = total.astype(BF16)


def on_device(excitation, leaf_basis, transfer, transfer_index, out_basis):
    excite, leaves, blocks, basis = excitation[0], leaf_basis[0], transfer[0], out_basis[0]
    index = transfer_index[0].T
    slots, rank, points = leaves.shape
    levels = blocks.shape[0]
    columns = excite.shape[2]
    n_blk = lax.axis_size("blk")
    rows = basis.shape[1] // n_blk
    nbits = lax.axis_size("box").bit_length() - 1
    bits = [None] + [(level - 1) % nbits for level in range(1, levels)]
    pair = in_vmem(slots, rank, 2 * rank)

    unit = slots * columns // sum(SHARES)
    widths = [unit * share for share in SHARES]
    begins = [sum(widths[:j]) for j in range(len(widths))]
    parts, places = [], []
    for begin, width in zip(begins, widths):
        part, place, lane = [], [], 0
        while lane < width:
            s, column = divmod(begin + lane, columns)
            size = min(width - lane, columns - column)
            part.append((s, lane, lane + size))
            place.append((s, column, lane, lane + size))
            lane += size
        parts.append(part)
        places.append(place)

    first, rest, *weights = call(
        leaf_kernel,
        "leaf",
        [ANY] * 4,
        [in_vmem(rank, widths[0]), in_vmem(rank, slots * columns - widths[0])] + [pair] * PRELOADED,
        [
            in_vmem(*excite.shape),
            in_vmem(*leaves.shape),
            pair,
            pltpu.SMEM(index.shape, jnp.int32),
            in_vmem(2 * rank, columns),
            pltpu.SemaphoreType.DMA((7 + 2 * PRELOADED,)),
        ],
        [in_hbm(excite), in_hbm(leaves), in_hbm(blocks), in_hbm(index)],
        limit=24 * 2**20,
    )
    weights = [None, *weights]

    def cross(level, value):
        return partner(value, "box", 2 ** bits[level])

    near_first = cross(1, first)

    def step(name, jobs, after=(), flops=COST, through=()):
        args = [here(v) for level, j, own, other in jobs for v in (own, other, weights[level])]
        described, sizes = [], []
        for level, j, _, _ in jobs:
            begin = begins[j] - widths[0] if level == 1 and j else 0
            described.append((bits[level], parts[j], slice(begin, begin + widths[j])))
            sizes.append(widths[j])
        return call(
            functools.partial(levels_kernel, described),
            name,
            [VMEM] * len(args),
            [in_vmem(rank, size) for size in sizes],
            [in_vmem(2 * rank, size) for size in sizes],
            args,
            after,
            flops,
            through=through,
        )

    def job1(j):
        return (1, j, rest, near_rest) if j else (1, j, first, near_first)

    coeff2, near2, coeff3, near3 = {}, {}, {}, {}

    def second(j, value):
        coeff2[j] = value
        near2[j] = cross(2, value)

    def third(j, value):
        coeff3[j] = value
        near3[j] = cross(3, value)

    value, rest = step("level1_0", [job1(0)], through=[rest])
    near_rest = cross(1, rest)
    second(0, value)
    (value,) = step("level1_1", [job1(1)], [coeff2[0]])
    second(1, value)
    (value,) = step("level2_0", [(2, 0, coeff2[0], near2[0])], [coeff2[1]])
    third(0, value)
    (value,) = step("level1_2", [job1(2)], [coeff3[0]])
    second(2, value)
    *more, basis_v = call(
        prefetch_kernel,
        "prefetch",
        [ANY] * 3,
        [pair] * (levels - 1 - PRELOADED) + [in_vmem(*basis.shape)],
        [pltpu.SMEM(index.shape, jnp.int32), pltpu.SemaphoreType.DMA((2 * levels,))],
        [in_hbm(blocks), in_hbm(basis), in_hbm(index)],
        [coeff2[2]],
    )
    weights += more
    (value,) = step("level2_1", [(2, 1, coeff2[1], near2[1])], [basis_v])
    third(1, value)

    masks = [1 << b for b in range(n_blk.bit_length() - 1)]
    orders = [masks, masks[::-1]]
    half = rows // 2
    whole = [[(0, rows, d, 0)] for d in range(n_blk)]
    halved = [[] for _ in range(n_blk)]
    for side, order in enumerate(orders):
        pieces = [0]
        for mask in order[::-1]:
            pieces = pieces + [d | mask for d in pieces]
        for at, d in enumerate(pieces):
            sent, to = divmod(at, n_blk // 2)
            halved[d].append((side * half, half, 2 * side + sent, to * half))

    def halves(j, count):
        shape = (count * half, widths[j])
        return [in_vmem(*shape, dtype=kind) for _ in orders for kind in (F32, BF16)]

    def exchange(values, at):
        return [
            v
            for side, order in enumerate(orders)
            for v in (values[2 * side], partner(values[2 * side + 1], "blk", order[at]))
        ]

    def begin_sum(j, out):
        held, count = exchange(out, 0), n_blk // 2
        for at in range(1, len(masks) - 1):
            count //= 2
            out = call(
                fold_kernel, f"fold_{j}_{at}", [VMEM] * 4, halves(j, count), [], [here(v) for v in held]
            )
            held = exchange(out, at)
        return held

    def tail(j, after, arrived=(), folding=(), halving=False):
        (coeff4,) = step(f"level3_{j}", [(3, j, coeff3[j], near3[j])], after)
        near4 = cross(4, coeff4)
        held = folding[1] if folding else []
        extra = [v for _, group in arrived for v in group] + held
        partial, *more = call(
            functools.partial(
                between_kernel, bits[4], parts[j], [len(group) for _, group in arrived], len(held) // 2
            ),
            f"between_{j}",
            [VMEM] * (2 + len(extra)),
            [in_vmem(rank, widths[j], dtype=F32)]
            + [in_vmem(rows, widths[at]) for at, _ in arrived]
            + (halves(folding[0], 1) if folding else []),
            [],
            [here(v) for v in (coeff4, weights[4], *extra)],
        )
        if halving:
            outs = halves(j, n_blk // 2)
        else:
            outs = [in_vmem(rows, widths[j], dtype=BF16 if d else F32) for d in range(n_blk)]
        out = call(
            functools.partial(last_kernel, bits[4], parts[j], halved if halving else whole),
            f"last_{j}",
            [VMEM] * 4,
            outs,
            [],
            [here(v) for v in (partial, near4, weights[4], basis_v)],
            flops=COST if j < len(widths) - 1 else 0,
        )
        if halving:
            return out, begin_sum(j, out), more
        return out, [out[0]] + [partner(out[d], "blk", d) for d in range(n_blk - 1, 0, -1)], more

    _, group0, _ = tail(0, [coeff3[1]])
    (value,) = step("level2_2", [(2, 2, coeff2[2], near2[2])], [group0[0]])
    third(2, value)
    (total0,) = call(
        sum_kernel,
        "sum_0",
        [VMEM] * n_blk,
        [in_vmem(rows, widths[0])],
        [],
        [here(v) for v in group0],
        [coeff3[2]],
    )
    (value,) = step("level1_3", [job1(3)], [total0])
    second(3, value)
    _, group1, _ = tail(1, [coeff2[3]])
    (partial,) = call(
        functools.partial(half_kernel, bits[2], parts[3]),
        "half_3",
        [VMEM] * 2,
        [in_vmem(rank, widths[3], dtype=F32)],
        [],
        [here(coeff2[3]), here(weights[2])],
        [group1[0]],
    )
    (value,) = call(
        functools.partial(finish_kernel, bits[2], parts[3]),
        "level2_3",
        [VMEM] * 3,
        [in_vmem(rank, widths[3])],
        [],
        [here(partial), here(near2[3]), here(weights[2])],
        [group1[1]],
    )
    third(3, value)
    _, group2, (total1,) = tail(2, [coeff3[3]], [(1, group1)])
    _, group3, _ = tail(3, [group2[0]])
    (total2,) = call(
        sum_kernel,
        "sum_2",
        [VMEM] * n_blk,
        [in_vmem(rows, widths[2])],
        [],
        [here(v) for v in group2],
        [group3[0]],
        0,
    )
    groups = [[total0], [total1], [total2], group3]
    flat = [here(v) for group in groups for v in group]
    return pl.pallas_call(
        functools.partial(end_kernel, places, [len(group) for group in groups]),
        name="end",
        in_specs=[VMEM] * len(flat),
        out_specs=VMEM,
        out_shape=jax.ShapeDtypeStruct((slots, rows, columns), BF16),
        compiler_params=pltpu.CompilerParams(vmem_limit_bytes=8 * 2**20),
    )(*flat)


def solution(mesh):
    in_specs = (
        P("blk", "box", None, None),
        P("blk", "box", None, None),
        P("blk", None, "box", None, None),
        P("blk", None, "box"),
        P("blk", "box", None, None),
    )
    out_specs = P("box", "blk", None)
    return jax.shard_map(
        on_device, mesh=mesh, in_specs=in_specs, out_specs=out_specs, check_vma=False
    )
```

```python
import functools

import jax
import jax.numpy as jnp
from jax import lax
from jax.experimental import pallas as pl
from jax.experimental.pallas import tpu as pltpu
from jax.sharding import PartitionSpec as P

SHARES = (1, 2, 3, 2)
PRELOADED = 2
COST = 6 * 10**9
BF16 = jnp.bfloat16
F32 = jnp.float32
ANY = pl.BlockSpec(memory_space=pl.ANY)
VMEM = pl.BlockSpec(memory_space=pltpu.VMEM)


def dot(a, b):
    return jnp.dot(a, b, preferred_element_type=F32)


def in_vmem(*shape, dtype=BF16):
    return pltpu.VMEM(shape, dtype)


def here(value):
    return pltpu.with_memory_space_constraint(value, pltpu.VMEM)


def in_hbm(value):
    return pltpu.with_memory_space_constraint(value, pltpu.HBM)


def call(kernel, name, in_specs, out_shape, scratch, args, after=(), flops=COST, limit=8 * 2**20, through=()):
    count, outs = len(in_specs), len(out_shape)

    def body(*refs):
        held = refs[count + len(after) + len(through) :]
        kernel(*refs[:count], *held[:outs], *held[outs + len(through) :])

    return pl.pallas_call(
        body,
        name=name,
        in_specs=[*in_specs, *[ANY] * (len(after) + len(through))],
        out_specs=[VMEM] * outs + [ANY] * len(through),
        out_shape=[*out_shape, *[in_vmem(*v.shape, dtype=v.dtype) for v in through]],
        scratch_shapes=scratch,
        input_output_aliases={count + len(after) + at: outs + at for at in range(len(through))},
        compiler_params=pltpu.CompilerParams(vmem_limit_bytes=limit),
        cost_estimate=pl.CostEstimate(flops=flops, bytes_accessed=0, transcendentals=0),
    )(*args, *after, *[here(v) for v in through])


def partner(value, axis, mask):
    pairs = [(source, source ^ mask) for source in range(lax.axis_size(axis))]
    return lax.ppermute(value, axis, pairs)


def leaf_kernel(excite, leaves, blocks, index, first, rest, *refs):
    count = PRELOADED
    nexts = refs[:count]
    excite_v, leaves_v, blocks_v, index_s, coeff, sems = refs[count:]
    slots, rank = leaves.shape[0], leaves.shape[1]
    columns, width = excite.shape[2], first.shape[1]
    listing = pltpu.make_async_copy(index, index_s, sems.at[0])
    listing.start()
    loads = []
    for s in range(slots):
        a = pltpu.make_async_copy(leaves.at[s], leaves_v.at[s], sems.at[1 + s])
        b = pltpu.make_async_copy(excite.at[s], excite_v.at[s], sems.at[3 + s])
        a.start()
        b.start()
        loads.append((a, b))
    listing.wait()
    weights, later = [], []
    for s in range(slots):
        c = pltpu.make_async_copy(blocks.at[0, index_s[s, 0]], blocks_v.at[s], sems.at[5 + s])
        c.start()
        weights.append(c)
    for level in range(1, 1 + count):
        for s in range(slots):
            c = pltpu.make_async_copy(
                blocks.at[level, index_s[s, level]], nexts[level - 1].at[s], sems.at[5 + 2 * level + s]
            )
            c.start()
            later.append(c)
    for s in range(slots):
        for load in loads[s]:
            load.wait()
        coeff[s * rank : (s + 1) * rank, :] = dot(leaves_v[s], excite_v[s]).astype(BF16)
    for s in range(slots):
        weights[s].wait()
        out = dot(blocks_v[s], coeff[...]).astype(BF16)
        if s == 0:
            first[...] = out[:, :width]
            rest[:, : columns - width] = out[:, width:]
        else:
            rest[:, s * columns - width : (s + 1) * columns - width] = out
    for c in later:
        c.wait()


def prefetch_kernel(blocks, basis, index, *refs):
    count = blocks.shape[0] - 1 - PRELOADED
    outs, basis_v, index_s, sems = refs[:count], refs[count], refs[count + 1], refs[count + 2]
    listing = pltpu.make_async_copy(index, index_s, sems.at[0])
    listing.start()
    c = pltpu.make_async_copy(basis, basis_v, sems.at[1 + 2 * count])
    c.start()
    copies = [c]
    listing.wait()
    for at in range(count):
        level = at + 1 + PRELOADED
        for s in range(2):
            c = pltpu.make_async_copy(blocks.at[level, index_s[s, level]], outs[at].at[s], sems.at[1 + 2 * at + s])
            c.start()
            copies.append(c)
    for c in copies:
        c.wait()


def upper_half(bit):
    return (lax.axis_index("box") >> bit) & 1


def mix(weights, own, other, bit, buf, parts, out):
    rank = own.shape[0]
    upper = upper_half(bit)
    buf[pl.ds(pl.multiple_of(upper * rank, rank), rank), :] = own
    buf[pl.ds(pl.multiple_of((1 - upper) * rank, rank), rank), :] = other
    for s, start, stop in parts:
        out[:, start:stop] = dot(weights[s], buf[:, start:stop]).astype(BF16)


def levels_kernel(jobs, *refs):
    count = len(jobs)
    ins, outs, bufs = refs[: 3 * count], refs[3 * count : 4 * count], refs[4 * count :]
    for at, (bit, parts, lanes) in enumerate(jobs):
        own, other, weights = ins[3 * at : 3 * at + 3]
        mix(weights, own[:, lanes], other[:, lanes], bit, bufs[at], parts, outs[at])


def half_dot(weights, s, half, value):
    rank = value.shape[0]
    return dot(weights[s, :, pl.ds(pl.multiple_of(half * rank, 128), rank)], value)


def sum_kernel(mine, *refs):
    total = mine[...]
    for piece in refs[:-1]:
        total = total + piece[...].astype(F32)
    refs[-1][...] = total.astype(BF16)


def half_kernel(bit, parts, own, weights, partial):
    for s, start, stop in parts:
        partial[:, start:stop] = half_dot(weights, s, upper_half(bit), own[:, start:stop])


def finish_kernel(bit, parts, partial, other, weights, out):
    for s, start, stop in parts:
        mixed = partial[:, start:stop] + half_dot(weights, s, 1 - upper_half(bit), other[:, start:stop])
        out[:, start:stop] = mixed.astype(BF16)


def between_kernel(bit, parts, counts, folds, own, weights, *refs):
    refs = list(refs)
    groups = [[refs.pop(0) for _ in range(count)] for count in counts]
    held = [refs.pop(0) for _ in range(2 * folds)]
    partial = refs.pop(0)
    for s, start, stop in parts:
        partial[:, start:stop] = half_dot(weights, s, upper_half(bit), own[:, start:stop])
    for group in groups:
        sum_kernel(*group, refs.pop(0))
    fold_kernel(*held, *refs)


def fold_kernel(*refs):
    half = len(refs) // 2
    for at in range(0, half, 2):
        keep, got, rest, send = refs[at], refs[at + 1], refs[half + at], refs[half + at + 1]
        rows = rest.shape[0]
        rest[...] = keep[:rows] + got[:rows].astype(F32)
        send[...] = (keep[rows:] + got[rows:].astype(F32)).astype(BF16)


def join_kernel(*refs):
    out, row = refs[-1], 0
    for keep, got in zip(refs[:-1:2], refs[1:-1:2]):
        out[row : row + keep.shape[0], :] = (keep[...] + got[...].astype(F32)).astype(BF16)
        row += keep.shape[0]


def last_kernel(bit, parts, homes, partial, other, weights, basis, *refs):
    rows = basis.shape[1] // lax.axis_size("blk")
    me = lax.axis_index("blk")
    for s, start, stop in parts:
        mixed = partial[:, start:stop] + half_dot(weights, s, 1 - upper_half(bit), other[:, start:stop])
        coeff = mixed.astype(BF16)
        for d, home in enumerate(homes):
            row = pl.multiple_of((me ^ d) * rows, rows)
            piece = dot(basis[s, pl.ds(row, rows), :], coeff)
            for begin, size, at, to in home:
                ref = refs[at]
                ref[to : to + size, start:stop] = piece[begin : begin + size].astype(ref.dtype)


def mixed_kernel(bit, parts, d, partial, other, weights, basis, coeff, ref):
    rows = ref.shape[0]
    row = pl.multiple_of((lax.axis_index("blk") ^ d) * rows, rows)
    for s, start, stop in parts:
        mixed = partial[:, start:stop] + half_dot(weights, s, 1 - upper_half(bit), other[:, start:stop])
        coeff[:, start:stop] = mixed.astype(BF16)
        ref[:, start:stop] = dot(basis[s, pl.ds(row, rows), :], coeff[:, start:stop]).astype(BF16)


def pieces_kernel(parts, coeff, basis, *refs):
    rows = refs[0].shape[0]
    me = lax.axis_index("blk")
    for s, start, stop in parts:
        for d, ref in enumerate(refs):
            row = pl.multiple_of((me ^ d) * rows, rows)
            ref[:, start:stop] = dot(basis[s, pl.ds(row, rows), :], coeff[:, start:stop]).astype(ref.dtype)


def end_kernel(places, counts, *refs):
    refs = list(refs)
    out = refs[-1]
    for place, count in zip(places, counts):
        group = [refs.pop(0) for _ in range(count)]
        for s, column, start, stop in place:
            total = group[0][:, start:stop].astype(F32)
            for piece in group[1:]:
                total = total + piece[:, start:stop].astype(F32)
            out[s, :, column : column + stop - start] = total.astype(BF16)


def on_device(excitation, leaf_basis, transfer, transfer_index, out_basis):
    excite, leaves, blocks, basis = excitation[0], leaf_basis[0], transfer[0], out_basis[0]
    index = transfer_index[0].T
    slots, rank, points = leaves.shape
    levels = blocks.shape[0]
    columns = excite.shape[2]
    n_blk = lax.axis_size("blk")
    rows = basis.shape[1] // n_blk
    nbits = lax.axis_size("box").bit_length() - 1
    bits = [None] + [(level - 1) % nbits for level in range(1, levels)]
    pair = in_vmem(slots, rank, 2 * rank)

    unit = slots * columns // sum(SHARES)
    widths = [unit * share for share in SHARES]
    begins = [sum(widths[:j]) for j in range(len(widths))]
    parts, places = [], []
    for begin, width in zip(begins, widths):
        part, place, lane = [], [], 0
        while lane < width:
            s, column = divmod(begin + lane, columns)
            size = min(width - lane, columns - column)
            part.append((s, lane, lane + size))
            place.append((s, column, lane, lane + size))
            lane += size
        parts.append(part)
        places.append(place)

    first, rest, *weights = call(
        leaf_kernel,
        "leaf",
        [ANY] * 4,
        [in_vmem(rank, widths[0]), in_vmem(rank, slots * columns - widths[0])] + [pair] * PRELOADED,
        [
            in_vmem(*excite.shape),
            in_vmem(*leaves.shape),
            pair,
            pltpu.SMEM(index.shape, jnp.int32),
            in_vmem(2 * rank, columns),
            pltpu.SemaphoreType.DMA((7 + 2 * PRELOADED,)),
        ],
        [in_hbm(excite), in_hbm(leaves), in_hbm(blocks), in_hbm(index)],
        limit=24 * 2**20,
    )
    weights = [None, *weights]

    def cross(level, value):
        return partner(value, "box", 2 ** bits[level])

    near_first = cross(1, first)

    def step(name, jobs, after=(), flops=COST, through=()):
        args = [here(v) for level, j, own, other in jobs for v in (own, other, weights[level])]
        described, sizes = [], []
        for level, j, _, _ in jobs:
            begin = begins[j] - widths[0] if level == 1 and j else 0
            described.append((bits[level], parts[j], slice(begin, begin + widths[j])))
            sizes.append(widths[j])
        return call(
            functools.partial(levels_kernel, described),
            name,
            [VMEM] * len(args),
            [in_vmem(rank, size) for size in sizes],
            [in_vmem(2 * rank, size) for size in sizes],
            args,
            after,
            flops,
            through=through,
        )

    def job1(j):
        return (1, j, rest, near_rest) if j else (1, j, first, near_first)

    coeff2, near2, coeff3, near3 = {}, {}, {}, {}

    def second(j, value):
        coeff2[j] = value
        near2[j] = cross(2, value)

    def third(j, value):
        coeff3[j] = value
        near3[j] = cross(3, value)

    value, rest = step("level1_0", [job1(0)], through=[rest])
    near_rest = cross(1, rest)
    second(0, value)
    (value,) = step("level1_1", [job1(1)], [coeff2[0]])
    second(1, value)
    (value,) = step("level2_0", [(2, 0, coeff2[0], near2[0])], [coeff2[1]])
    third(0, value)
    (value,) = step("level1_2", [job1(2)], [coeff3[0]])
    second(2, value)
    *more, basis_v = call(
        prefetch_kernel,
        "prefetch",
        [ANY] * 3,
        [pair] * (levels - 1 - PRELOADED) + [in_vmem(*basis.shape)],
        [pltpu.SMEM(index.shape, jnp.int32), pltpu.SemaphoreType.DMA((2 * levels,))],
        [in_hbm(blocks), in_hbm(basis), in_hbm(index)],
        [coeff2[2]],
    )
    weights += more
    (value,) = step("level2_1", [(2, 1, coeff2[1], near2[1])], [basis_v])
    third(1, value)

    masks = [1 << b for b in range(n_blk.bit_length() - 1)]
    orders = [masks, masks[::-1]]
    half = rows // 2
    whole = [[(0, rows, d, 0)] for d in range(n_blk)]
    halved = [[] for _ in range(n_blk)]
    for side, order in enumerate(orders):
        pieces = [0]
        for mask in order[::-1]:
            pieces = pieces + [d | mask for d in pieces]
        for at, d in enumerate(pieces):
            sent, to = divmod(at, n_blk // 2)
            halved[d].append((side * half, half, 2 * side + sent, to * half))

    def halves(j, count):
        shape = (count * half, widths[j])
        return [in_vmem(*shape, dtype=kind) for _ in orders for kind in (F32, BF16)]

    def exchange(values, at):
        return [
            v
            for side, order in enumerate(orders)
            for v in (values[2 * side], partner(values[2 * side + 1], "blk", order[at]))
        ]

    def begin_sum(j, out):
        held, count = exchange(out, 0), n_blk // 2
        for at in range(1, len(masks) - 1):
            count //= 2
            out = call(
                fold_kernel, f"fold_{j}_{at}", [VMEM] * 4, halves(j, count), [], [here(v) for v in held]
            )
            held = exchange(out, at)
        return held

    def tail(j, after, arrived=(), folding=(), halving=False):
        (coeff4,) = step(f"level3_{j}", [(3, j, coeff3[j], near3[j])], after)
        near4 = cross(4, coeff4)
        held = folding[1] if folding else []
        extra = [v for _, group in arrived for v in group] + held
        partial, *more = call(
            functools.partial(
                between_kernel, bits[4], parts[j], [len(group) for _, group in arrived], len(held) // 2
            ),
            f"between_{j}",
            [VMEM] * (2 + len(extra)),
            [in_vmem(rank, widths[j], dtype=F32)]
            + [in_vmem(rows, widths[at]) for at, _ in arrived]
            + (halves(folding[0], 1) if folding else []),
            [],
            [here(v) for v in (coeff4, weights[4], *extra)],
        )
        if j >= 2:
            coeff5, far = call(
                functools.partial(mixed_kernel, bits[4], parts[j], n_blk - 1),
                f"far_{j}",
                [VMEM] * 4,
                [in_vmem(rank, widths[j]), in_vmem(rows, widths[j])],
                [],
                [here(v) for v in (partial, near4, weights[4], basis_v)],
                flops=COST if j < len(widths) - 1 else 0,
            )
            out = call(
                functools.partial(pieces_kernel, parts[j]),
                f"last_{j}",
                [VMEM] * 2,
                [in_vmem(rows, widths[j], dtype=BF16 if d else F32) for d in range(n_blk - 1)],
                [],
                [here(coeff5), here(basis_v)],
                flops=10**9 if j == 2 else 2 * 10**8,
            )
            out = [*out, far]
            return out, [out[0]] + [partner(out[d], "blk", d) for d in range(n_blk - 1, 0, -1)], more
        if halving:
            outs = halves(j, n_blk // 2)
        else:
            outs = [in_vmem(rows, widths[j], dtype=BF16 if d else F32) for d in range(n_blk)]
        out = call(
            functools.partial(last_kernel, bits[4], parts[j], halved if halving else whole),
            f"last_{j}",
            [VMEM] * 4,
            outs,
            [],
            [here(v) for v in (partial, near4, weights[4], basis_v)],
            flops=COST if j < len(widths) - 1 else 0,
        )
        if halving:
            return out, begin_sum(j, out), more
        return out, [out[0]] + [partner(out[d], "blk", d) for d in range(n_blk - 1, 0, -1)], more

    _, group0, _ = tail(0, [coeff3[1]])
    (value,) = step("level2_2", [(2, 2, coeff2[2], near2[2])], [group0[0]])
    third(2, value)
    (total0,) = call(
        sum_kernel,
        "sum_0",
        [VMEM] * n_blk,
        [in_vmem(rows, widths[0])],
        [],
        [here(v) for v in group0],
        [coeff3[2]],
    )
    (value,) = step("level1_3", [job1(3)], [total0])
    second(3, value)
    _, group1, _ = tail(1, [coeff2[3]])
    (partial,) = call(
        functools.partial(half_kernel, bits[2], parts[3]),
        "half_3",
        [VMEM] * 2,
        [in_vmem(rank, widths[3], dtype=F32)],
        [],
        [here(coeff2[3]), here(weights[2])],
        [group1[0]],
    )
    (value,) = call(
        functools.partial(finish_kernel, bits[2], parts[3]),
        "level2_3",
        [VMEM] * 3,
        [in_vmem(rank, widths[3])],
        [],
        [here(partial), here(near2[3]), here(weights[2])],
        [group1[1]],
    )
    third(3, value)
    _, group2, (total1,) = tail(2, [coeff3[3]], [(1, group1)])
    _, group3, _ = tail(3, [group2[0]])
    (total2,) = call(
        sum_kernel,
        "sum_2",
        [VMEM] * n_blk,
        [in_vmem(rows, widths[2])],
        [],
        [here(v) for v in group2],
        [group3[0]],
        0,
    )
    groups = [[total0], [total1], [total2], group3]
    flat = [here(v) for group in groups for v in group]
    return pl.pallas_call(
        functools.partial(end_kernel, places, [len(group) for group in groups]),
        name="end",
        in_specs=[VMEM] * len(flat),
        out_specs=VMEM,
        out_shape=jax.ShapeDtypeStruct((slots, rows, columns), BF16),
        compiler_params=pltpu.CompilerParams(vmem_limit_bytes=8 * 2**20),
    )(*flat)


def solution(mesh):
    in_specs = (
        P("blk", "box", None, None),
        P("blk", "box", None, None),
        P("blk", None, "box", None, None),
        P("blk", None, "box"),
        P("blk", "box", None, None),
    )
    out_specs = P("box", "blk", None)
    return jax.shard_map(
        on_device, mesh=mesh, in_specs=in_specs, out_specs=out_specs, check_vma=False
    )
```

```python
import functools

import jax
import jax.numpy as jnp
from jax import lax
from jax.experimental import pallas as pl
from jax.experimental.pallas import tpu as pltpu
from jax.sharding import PartitionSpec as P

SHARES = (1, 2, 3, 2)
PRELOADED = 2
COST = 6 * 10**9
BF16 = jnp.bfloat16
F32 = jnp.float32
ANY = pl.BlockSpec(memory_space=pl.ANY)
VMEM = pl.BlockSpec(memory_space=pltpu.VMEM)


def dot(a, b):
    return jnp.dot(a, b, preferred_element_type=F32)


def in_vmem(*shape, dtype=BF16):
    return pltpu.VMEM(shape, dtype)


def here(value):
    return pltpu.with_memory_space_constraint(value, pltpu.VMEM)


def in_hbm(value):
    return pltpu.with_memory_space_constraint(value, pltpu.HBM)


def call(kernel, name, in_specs, out_shape, scratch, args, after=(), flops=COST, limit=8 * 2**20, through=()):
    count, outs = len(in_specs), len(out_shape)

    def body(*refs):
        held = refs[count + len(after) + len(through) :]
        kernel(*refs[:count], *held[:outs], *held[outs + len(through) :])

    return pl.pallas_call(
        body,
        name=name,
        in_specs=[*in_specs, *[ANY] * (len(after) + len(through))],
        out_specs=[VMEM] * outs + [ANY] * len(through),
        out_shape=[*out_shape, *[in_vmem(*v.shape, dtype=v.dtype) for v in through]],
        scratch_shapes=scratch,
        input_output_aliases={count + len(after) + at: outs + at for at in range(len(through))},
        compiler_params=pltpu.CompilerParams(vmem_limit_bytes=limit),
        cost_estimate=pl.CostEstimate(flops=flops, bytes_accessed=0, transcendentals=0),
    )(*args, *after, *[here(v) for v in through])


def partner(value, axis, mask):
    pairs = [(source, source ^ mask) for source in range(lax.axis_size(axis))]
    return lax.ppermute(value, axis, pairs)


def leaf_kernel(excite, leaves, blocks, index, first, rest, *refs):
    count = PRELOADED
    nexts = refs[:count]
    excite_v, leaves_v, blocks_v, index_s, coeff, sems = refs[count:]
    slots, rank = leaves.shape[0], leaves.shape[1]
    columns, width = excite.shape[2], first.shape[1]
    listing = pltpu.make_async_copy(index, index_s, sems.at[0])
    listing.start()
    loads = []
    for s in range(slots):
        a = pltpu.make_async_copy(leaves.at[s], leaves_v.at[s], sems.at[1 + s])
        b = pltpu.make_async_copy(excite.at[s], excite_v.at[s], sems.at[3 + s])
        a.start()
        b.start()
        loads.append((a, b))
    listing.wait()
    weights, later = [], []
    for s in range(slots):
        c = pltpu.make_async_copy(blocks.at[0, index_s[s, 0]], blocks_v.at[s], sems.at[5 + s])
        c.start()
        weights.append(c)
    for level in range(1, 1 + count):
        for s in range(slots):
            c = pltpu.make_async_copy(
                blocks.at[level, index_s[s, level]], nexts[level - 1].at[s], sems.at[5 + 2 * level + s]
            )
            c.start()
            later.append(c)
    for s in range(slots):
        for load in loads[s]:
            load.wait()
        coeff[s * rank : (s + 1) * rank, :] = dot(leaves_v[s], excite_v[s]).astype(BF16)
    for s in range(slots):
        weights[s].wait()
        out = dot(blocks_v[s], coeff[...]).astype(BF16)
        if s == 0:
            first[...] = out[:, :width]
            rest[:, : columns - width] = out[:, width:]
        else:
            rest[:, s * columns - width : (s + 1) * columns - width] = out
    for c in later:
        c.wait()


def prefetch_kernel(blocks, basis, index, *refs):
    count = blocks.shape[0] - 1 - PRELOADED
    outs, basis_v, index_s, sems = refs[:count], refs[count], refs[count + 1], refs[count + 2]
    listing = pltpu.make_async_copy(index, index_s, sems.at[0])
    listing.start()
    c = pltpu.make_async_copy(basis, basis_v, sems.at[1 + 2 * count])
    c.start()
    copies = [c]
    listing.wait()
    for at in range(count):
        level = at + 1 + PRELOADED
        for s in range(2):
            c = pltpu.make_async_copy(blocks.at[level, index_s[s, level]], outs[at].at[s], sems.at[1 + 2 * at + s])
            c.start()
            copies.append(c)
    for c in copies:
        c.wait()


def upper_half(bit):
    return (lax.axis_index("box") >> bit) & 1


def mix(weights, own, other, bit, buf, parts, out):
    rank = own.shape[0]
    upper = upper_half(bit)
    buf[pl.ds(pl.multiple_of(upper * rank, rank), rank), :] = own
    buf[pl.ds(pl.multiple_of((1 - upper) * rank, rank), rank), :] = other
    for s, start, stop in parts:
        out[:, start:stop] = dot(weights[s], buf[:, start:stop]).astype(BF16)


def levels_kernel(jobs, *refs):
    count = len(jobs)
    ins, outs, bufs = refs[: 3 * count], refs[3 * count : 4 * count], refs[4 * count :]
    for at, (bit, parts, lanes) in enumerate(jobs):
        own, other, weights = ins[3 * at : 3 * at + 3]
        mix(weights, own[:, lanes], other[:, lanes], bit, bufs[at], parts, outs[at])


def half_dot(weights, s, half, value):
    rank = value.shape[0]
    return dot(weights[s, :, pl.ds(pl.multiple_of(half * rank, 128), rank)], value)


def sum_kernel(mine, *refs):
    total = mine[...]
    for piece in refs[:-1]:
        total = total + piece[...].astype(F32)
    refs[-1][...] = total.astype(BF16)


def half_kernel(bit, parts, own, weights, partial):
    for s, start, stop in parts:
        partial[:, start:stop] = half_dot(weights, s, upper_half(bit), own[:, start:stop])


def finish_kernel(bit, parts, partial, other, weights, out):
    for s, start, stop in parts:
        mixed = partial[:, start:stop] + half_dot(weights, s, 1 - upper_half(bit), other[:, start:stop])
        out[:, start:stop] = mixed.astype(BF16)


def between_kernel(bit, parts, counts, folds, own, weights, *refs):
    refs = list(refs)
    groups = [[refs.pop(0) for _ in range(count)] for count in counts]
    held = [refs.pop(0) for _ in range(2 * folds)]
    partial = refs.pop(0)
    for s, start, stop in parts:
        partial[:, start:stop] = half_dot(weights, s, upper_half(bit), own[:, start:stop])
    for group in groups:
        sum_kernel(*group, refs.pop(0))
    fold_kernel(*held, *refs)


def fold_kernel(*refs):
    half = len(refs) // 2
    for at in range(0, half, 2):
        keep, got, rest, send = refs[at], refs[at + 1], refs[half + at], refs[half + at + 1]
        rows = rest.shape[0]
        rest[...] = keep[:rows] + got[:rows].astype(F32)
        send[...] = (keep[rows:] + got[rows:].astype(F32)).astype(BF16)


def join_kernel(*refs):
    out, row = refs[-1], 0
    for keep, got in zip(refs[:-1:2], refs[1:-1:2]):
        out[row : row + keep.shape[0], :] = (keep[...] + got[...].astype(F32)).astype(BF16)
        row += keep.shape[0]


def last_kernel(bit, parts, homes, partial, other, weights, basis, *refs):
    rows = basis.shape[1] // lax.axis_size("blk")
    me = lax.axis_index("blk")
    for s, start, stop in parts:
        mixed = partial[:, start:stop] + half_dot(weights, s, 1 - upper_half(bit), other[:, start:stop])
        coeff = mixed.astype(BF16)
        for d, home in enumerate(homes):
            row = pl.multiple_of((me ^ d) * rows, rows)
            piece = dot(basis[s, pl.ds(row, rows), :], coeff)
            for begin, size, at, to in home:
                ref = refs[at]
                ref[to : to + size, start:stop] = piece[begin : begin + size].astype(ref.dtype)


def mixed_kernel(bit, parts, d, partial, other, weights, basis, coeff, ref):
    rows = ref.shape[0]
    row = pl.multiple_of((lax.axis_index("blk") ^ d) * rows, rows)
    for s, start, stop in parts:
        mixed = partial[:, start:stop] + half_dot(weights, s, 1 - upper_half(bit), other[:, start:stop])
        coeff[:, start:stop] = mixed.astype(BF16)
        ref[:, start:stop] = dot(basis[s, pl.ds(row, rows), :], coeff[:, start:stop]).astype(BF16)


def pieces_kernel(parts, coeff, basis, *refs):
    rows = refs[0].shape[0]
    me = lax.axis_index("blk")
    for s, start, stop in parts:
        for d, ref in enumerate(refs):
            row = pl.multiple_of((me ^ d) * rows, rows)
            ref[:, start:stop] = dot(basis[s, pl.ds(row, rows), :], coeff[:, start:stop]).astype(ref.dtype)


def end_kernel(places, counts, *refs):
    refs = list(refs)
    out = refs[-1]
    for place, count in zip(places, counts):
        group = [refs.pop(0) for _ in range(count)]
        for s, column, start, stop in place:
            total = group[0][:, start:stop].astype(F32)
            for piece in group[1:]:
                total = total + piece[:, start:stop].astype(F32)
            out[s, :, column : column + stop - start] = total.astype(BF16)


def on_device(excitation, leaf_basis, transfer, transfer_index, out_basis):
    excite, leaves, blocks, basis = excitation[0], leaf_basis[0], transfer[0], out_basis[0]
    index = transfer_index[0].T
    slots, rank, points = leaves.shape
    levels = blocks.shape[0]
    columns = excite.shape[2]
    n_blk = lax.axis_size("blk")
    rows = basis.shape[1] // n_blk
    nbits = lax.axis_size("box").bit_length() - 1
    bits = [None] + [(level - 1) % nbits for level in range(1, levels)]
    pair = in_vmem(slots, rank, 2 * rank)

    unit = slots * columns // sum(SHARES)
    widths = [unit * share for share in SHARES]
    begins = [sum(widths[:j]) for j in range(len(widths))]
    parts, places = [], []
    for begin, width in zip(begins, widths):
        part, place, lane = [], [], 0
        while lane < width:
            s, column = divmod(begin + lane, columns)
            size = min(width - lane, columns - column)
            part.append((s, lane, lane + size))
            place.append((s, column, lane, lane + size))
            lane += size
        parts.append(part)
        places.append(place)

    first, rest, *weights = call(
        leaf_kernel,
        "leaf",
        [ANY] * 4,
        [in_vmem(rank, widths[0]), in_vmem(rank, slots * columns - widths[0])] + [pair] * PRELOADED,
        [
            in_vmem(*excite.shape),
            in_vmem(*leaves.shape),
            pair,
            pltpu.SMEM(index.shape, jnp.int32),
            in_vmem(2 * rank, columns),
            pltpu.SemaphoreType.DMA((7 + 2 * PRELOADED,)),
        ],
        [in_hbm(excite), in_hbm(leaves), in_hbm(blocks), in_hbm(index)],
        limit=24 * 2**20,
    )
    weights = [None, *weights]

    def cross(level, value):
        return partner(value, "box", 2 ** bits[level])

    near_first = cross(1, first)

    def step(name, jobs, after=(), flops=COST, through=()):
        args = [here(v) for level, j, own, other in jobs for v in (own, other, weights[level])]
        described, sizes = [], []
        for level, j, _, _ in jobs:
            begin = begins[j] - widths[0] if level == 1 and j else 0
            described.append((bits[level], parts[j], slice(begin, begin + widths[j])))
            sizes.append(widths[j])
        return call(
            functools.partial(levels_kernel, described),
            name,
            [VMEM] * len(args),
            [in_vmem(rank, size) for size in sizes],
            [in_vmem(2 * rank, size) for size in sizes],
            args,
            after,
            flops,
            through=through,
        )

    def job1(j):
        return (1, j, rest, near_rest) if j else (1, j, first, near_first)

    coeff2, near2, coeff3, near3 = {}, {}, {}, {}

    def second(j, value):
        coeff2[j] = value
        near2[j] = cross(2, value)

    def third(j, value):
        coeff3[j] = value
        near3[j] = cross(3, value)

    value, rest = step("level1_0", [job1(0)], through=[rest])
    near_rest = cross(1, rest)
    second(0, value)
    (value,) = step("level1_1", [job1(1)], [coeff2[0]])
    second(1, value)
    (value,) = step("level2_0", [(2, 0, coeff2[0], near2[0])], [coeff2[1]])
    third(0, value)
    (value,) = step("level1_2", [job1(2)], [coeff3[0]])
    second(2, value)
    *more, basis_v = call(
        prefetch_kernel,
        "prefetch",
        [ANY] * 3,
        [pair] * (levels - 1 - PRELOADED) + [in_vmem(*basis.shape)],
        [pltpu.SMEM(index.shape, jnp.int32), pltpu.SemaphoreType.DMA((2 * levels,))],
        [in_hbm(blocks), in_hbm(basis), in_hbm(index)],
        [coeff2[2]],
    )
    weights += more
    (value,) = step("level2_1", [(2, 1, coeff2[1], near2[1])], [basis_v])
    third(1, value)

    masks = [1 << b for b in range(n_blk.bit_length() - 1)]
    orders = [masks, masks[::-1]]
    half = rows // 2
    whole = [[(0, rows, d, 0)] for d in range(n_blk)]
    halved = [[] for _ in range(n_blk)]
    for side, order in enumerate(orders):
        pieces = [0]
        for mask in order[::-1]:
            pieces = pieces + [d | mask for d in pieces]
        for at, d in enumerate(pieces):
            sent, to = divmod(at, n_blk // 2)
            halved[d].append((side * half, half, 2 * side + sent, to * half))

    def halves(j, count):
        shape = (count * half, widths[j])
        return [in_vmem(*shape, dtype=kind) for _ in orders for kind in (F32, BF16)]

    def exchange(values, at):
        return [
            v
            for side, order in enumerate(orders)
            for v in (values[2 * side], partner(values[2 * side + 1], "blk", order[at]))
        ]

    def begin_sum(j, out):
        held, count = exchange(out, 0), n_blk // 2
        for at in range(1, len(masks) - 1):
            count //= 2
            out = call(
                fold_kernel, f"fold_{j}_{at}", [VMEM] * 4, halves(j, count), [], [here(v) for v in held]
            )
            held = exchange(out, at)
        return held

    def tail(j, after, arrived=(), folding=(), halving=False):
        if j >= 2:
            (ahead,) = call(
                functools.partial(half_kernel, bits[3], parts[j]),
                f"ahead_{j}",
                [VMEM] * 2,
                [in_vmem(rank, widths[j], dtype=F32)],
                [],
                [here(coeff3[j]), here(weights[3])],
                after,
                0,
            )
            (coeff4,) = call(
                functools.partial(finish_kernel, bits[3], parts[j]),
                f"level3_{j}",
                [VMEM] * 3,
                [in_vmem(rank, widths[j])],
                [],
                [here(ahead), here(near3[j]), here(weights[3])],
            )
        else:
            (coeff4,) = step(f"level3_{j}", [(3, j, coeff3[j], near3[j])], after)
        near4 = cross(4, coeff4)
        held = folding[1] if folding else []
        extra = [v for _, group in arrived for v in group] + held
        partial, *more = call(
            functools.partial(
                between_kernel, bits[4], parts[j], [len(group) for _, group in arrived], len(held) // 2
            ),
            f"between_{j}",
            [VMEM] * (2 + len(extra)),
            [in_vmem(rank, widths[j], dtype=F32)]
            + [in_vmem(rows, widths[at]) for at, _ in arrived]
            + (halves(folding[0], 1) if folding else []),
            [],
            [here(v) for v in (coeff4, weights[4], *extra)],
        )
        if j >= 2:
            coeff5, far = call(
                functools.partial(mixed_kernel, bits[4], parts[j], n_blk - 1),
                f"far_{j}",
                [VMEM] * 4,
                [in_vmem(rank, widths[j]), in_vmem(rows, widths[j])],
                [],
                [here(v) for v in (partial, near4, weights[4], basis_v)],
                flops=COST if j < len(widths) - 1 else 0,
            )
            out = call(
                functools.partial(pieces_kernel, parts[j]),
                f"last_{j}",
                [VMEM] * 2,
                [in_vmem(rows, widths[j], dtype=BF16 if d else F32) for d in range(n_blk - 1)],
                [],
                [here(coeff5), here(basis_v)],
                flops=10**9 if j == 2 else 2 * 10**8,
            )
            out = [*out, far]
            return out, [out[0]] + [partner(out[d], "blk", d) for d in range(n_blk - 1, 0, -1)], more
        if halving:
            outs = halves(j, n_blk // 2)
        else:
            outs = [in_vmem(rows, widths[j], dtype=BF16 if d else F32) for d in range(n_blk)]
        out = call(
            functools.partial(last_kernel, bits[4], parts[j], halved if halving else whole),
            f"last_{j}",
            [VMEM] * 4,
            outs,
            [],
            [here(v) for v in (partial, near4, weights[4], basis_v)],
            flops=COST if j < len(widths) - 1 else 0,
        )
        if halving:
            return out, begin_sum(j, out), more
        return out, [out[0]] + [partner(out[d], "blk", d) for d in range(n_blk - 1, 0, -1)], more

    _, group0, _ = tail(0, [coeff3[1]])
    (value,) = step("level2_2", [(2, 2, coeff2[2], near2[2])], [group0[0]])
    third(2, value)
    (total0,) = call(
        sum_kernel,
        "sum_0",
        [VMEM] * n_blk,
        [in_vmem(rows, widths[0])],
        [],
        [here(v) for v in group0],
        [coeff3[2]],
    )
    (value,) = step("level1_3", [job1(3)], [total0])
    second(3, value)
    _, group1, _ = tail(1, [coeff2[3]])
    (partial,) = call(
        functools.partial(half_kernel, bits[2], parts[3]),
        "half_3",
        [VMEM] * 2,
        [in_vmem(rank, widths[3], dtype=F32)],
        [],
        [here(coeff2[3]), here(weights[2])],
        [group1[0]],
    )
    (value,) = call(
        functools.partial(finish_kernel, bits[2], parts[3]),
        "level2_3",
        [VMEM] * 3,
        [in_vmem(rank, widths[3])],
        [],
        [here(partial), here(near2[3]), here(weights[2])],
        [group1[1]],
    )
    third(3, value)
    _, group2, (total1,) = tail(2, [coeff3[3]], [(1, group1)])
    _, group3, _ = tail(3, [group2[0]])
    (total2,) = call(
        sum_kernel,
        "sum_2",
        [VMEM] * n_blk,
        [in_vmem(rows, widths[2])],
        [],
        [here(v) for v in group2],
        [group3[0]],
        0,
    )
    groups = [[total0], [total1], [total2], group3]
    flat = [here(v) for group in groups for v in group]
    return pl.pallas_call(
        functools.partial(end_kernel, places, [len(group) for group in groups]),
        name="end",
        in_specs=[VMEM] * len(flat),
        out_specs=VMEM,
        out_shape=jax.ShapeDtypeStruct((slots, rows, columns), BF16),
        compiler_params=pltpu.CompilerParams(vmem_limit_bytes=8 * 2**20),
    )(*flat)


def solution(mesh):
    in_specs = (
        P("blk", "box", None, None),
        P("blk", "box", None, None),
        P("blk", None, "box", None, None),
        P("blk", None, "box"),
        P("blk", "box", None, None),
    )
    out_specs = P("box", "blk", None)
    return jax.shard_map(
        on_device, mesh=mesh, in_specs=in_specs, out_specs=out_specs, check_vma=False
    )
```
